32 devices in a mesh: obj: 4 (over y, x), seq: 8 (over z, core).
Axes of the slice: x: 2, y: 2, z: 4, core: 2. Of those that a mesh axis runs over, the one named last changes fastest.
Arguments:
- tokens: bfloat16 [8, 1536, 1024], P('obj', 'seq'), may hold values from -6 to 6
- camera: float32 [8, 16], P('obj'), may hold values from -4 to 4
- patches: bfloat16 [8, 1024, 768], P('obj', 'seq'), may hold values from -6 to 6
- patch_count: int32 [8], P('obj'), may hold values from 256 to 1024, as said below
- patch_index: int32 [8, 1024], P('obj', 'seq'), may hold values from 0 to 4095
- cotangent: bfloat16 [8, 1536, 1024], P('obj', 'seq'), may hold values from -6 to 6
- camera_weight: float32 [16, 2048], P(None, ('obj', 'seq')), may hold values from -0.75 to 0.75
- self_weight: float32 [1024, 3072], P(('obj', 'seq')), may hold values from -0.1875 to 0.1875
- self_output: float32 [1024, 1024], P(('obj', 'seq')), may hold values from -4 to 4
- mid_gain: float32 [1024], P(('obj', 'seq')), may hold values from 0.25 to 1.75
- mid_bias: float32 [1024], P(('obj', 'seq')), may hold values from -3 to 3
- patch_weight: float32 [768, 1024], P(('obj', 'seq')), may hold values from -0.21875 to 0.21875
- view_table: float32 [4, 1024], P(None, ('obj', 'seq')), may hold values from -5 to 5
- cross_query: float32 [1024, 1024], P(('obj', 'seq')), may hold values from -0.1875 to 0.1875
- cross_memory: float32 [1024, 2048], P(('obj', 'seq')), may hold values from -0.125 to 0.125
- cross_output: float32 [1024, 1024], P(('obj', 'seq')), may hold values from -2.5 to 2.5
- last_gain: float32 [1024], P(('obj', 'seq')), may hold values from 0.25 to 1.75
- last_bias: float32 [1024], P(('obj', 'seq')), may hold values from -3 to 3
- up_weight: float32 [1024, 4096], P(('obj', 'seq')), may hold values from -0.1875 to 0.1875
- up_bias: float32 [4096], P(('obj', 'seq')), may hold values from -3 to 3
- down_weight: float32 [4096, 1024], P(('obj', 'seq')), may hold values from -0.125 to 0.125
- down_bias: float32 [1024], P(('obj', 'seq')), may hold values from -3 to 3
Outputs:
- result: bfloat16 [8, 1536, 1024], P('obj', 'seq')
- token_grad: bfloat16 [8, 1536, 1024], P('obj', 'seq')
- patch_grad: bfloat16 [8, 1024, 768], P('obj', 'seq')
- camera_weight_grad: float32 [16, 2048], P(None, ('obj', 'seq'))
- self_weight_grad: float32 [1024, 3072], P(('obj', 'seq'))
- self_output_grad: float32 [1024, 1024], P(('obj', 'seq'))
- mid_gain_grad: float32 [1024], P(('obj', 'seq'))
- mid_bias_grad: float32 [1024], P(('obj', 'seq'))
- patch_weight_grad: float32 [768, 1024], P(('obj', 'seq'))
- view_table_grad: float32 [4, 1024], P(None, ('obj', 'seq'))
- cross_query_grad: float32 [1024, 1024], P(('obj', 'seq'))
- cross_memory_grad: float32 [1024, 2048], P(('obj', 'seq'))
- cross_output_grad: float32 [1024, 1024], P(('obj', 'seq'))
- last_gain_grad: float32 [1024], P(('obj', 'seq'))
- last_bias_grad: float32 [1024], P(('obj', 'seq'))
- up_weight_grad: float32 [1024, 4096], P(('obj', 'seq'))
- up_bias_grad: float32 [4096], P(('obj', 'seq'))
- down_weight_grad: float32 [4096, 1024], P(('obj', 'seq'))
- down_bias_grad: float32 [1024], P(('obj', 'seq'))
The draws below stay inside these ranges and needn't reach their ends.
Inputs may be any that keep to these rules, and one draw needn't show every extreme that they name: Slots j < patch_count of an object hold live patches, the rest padding. In every aligned group of 2 objects one object has all 1024 slots live. A slot's view is patch_index // 1024.
All inputs are finite; a program needn't handle non-finite values.
Results may differ from the reference program's by a relative error of at most 0.023.
Values may be sent and summed in bfloat16 or wider, within the bound.
No kernel may reach another device: no remote copies, remote signals or barrier semaphores. Data moves between devices by JAX's collectives and lax.ppermute only.
A program may use at most 384 MiB of HBM per device.

```python
import jax
import jax.numpy as jnp
from jax import lax

D = 1024
HEADS = 16
HEAD_DIM = 64
FFN = 4096
PD = 768
CAMD = 16
VIEWS = 4
VIEW_PATCHES = 1024
TRI = 1536
CAP = 1024
OBJ_DEV = 2
OBJECTS = 8


def draw_patch_count(key, part):
    key = jax.random.fold_in(key, 7)
    first, second, third = jax.random.split(key, 3)
    divisor = jax.random.randint(first, (OBJECTS,), 1, 5)
    extra = jax.random.randint(second, (OBJECTS,), 0, CAP // 8 + 1)
    counts = jnp.minimum(CAP // divisor + extra, CAP)
    chosen = jax.random.randint(third, (OBJECTS // OBJ_DEV,), 0, OBJ_DEV)
    full = jnp.arange(OBJECTS) % OBJ_DEV == jnp.repeat(chosen, OBJ_DEV)
    return jnp.where(full, CAP, counts).astype(jnp.int32)


def set_ends(values, rng, low, top_value):
    longest = values.shape.index(max(values.shape))
    spots = []
    for shift in (0, 1):
        where = [jax.random.randint(jax.random.fold_in(rng, axis), (), 0, length) for axis, length in enumerate(values.shape)]
        where[longest] = (where[longest] + shift) % values.shape[longest]
        spots.append(tuple(where))
    return values.at[spots[0]].set(low).at[spots[1]].set(top_value)


def block_levels(key, dims, pieces, low, high):
    gain = 1.0
    for axis_at, blocks in pieces:
        heights = jax.random.uniform(jax.random.fold_in(jax.random.fold_in(key, 6), axis_at), (blocks,), jnp.float32, low / len(pieces), high / len(pieces))
        gain = gain * jnp.repeat(jnp.exp(heights), dims[axis_at] // blocks).reshape((-1,) + (1,) * (len(dims) - 1 - axis_at))
    return gain


def bell_draw(rng, dims, scale, most, shards=(), kind=jnp.bfloat16):
    result = scale * jax.random.normal(rng, dims, jnp.float32)
    if shards:
        result = result * block_levels(rng, dims, shards, -0.22, 0.18)
    return jnp.clip(result, -most, most).astype(kind)


def setup_inputs(seed: int = 0) -> dict:
    seeds = jax.random.split(jax.random.key(seed), 23)
    return {
        "tokens": bell_draw(seeds[0], (OBJECTS, TRI, D), 1.0, 6.0, ((0, 4), (1, 8))),
        "camera": bell_draw(seeds[1], (OBJECTS, CAMD), 1.0, 4.0, ((0, 4),), jnp.float32),
        "patches": bell_draw(seeds[2], (OBJECTS, CAP, PD), 1.0, 6.0, ((0, 4), (1, 8))),
        "patch_count": draw_patch_count(jax.random.fold_in(seeds[22], 71), 0),
        "patch_index": set_ends(jax.random.randint(seeds[4], (OBJECTS, CAP), 0, VIEWS * VIEW_PATCHES), jax.random.fold_in(seeds[4], 1), 0, (VIEWS * VIEW_PATCHES) - 1).astype(jnp.int32),
        "cotangent": bell_draw(seeds[5], (OBJECTS, TRI, D), 1.0, 6.0, ((0, 4), (1, 8))),
        "camera_weight": bell_draw(seeds[6], (CAMD, 2 * D), (4 * CAMD) ** -0.5, 0.75, ((1, 32),), jnp.float32),
        "self_weight": bell_draw(seeds[7], (D, 3 * D), D ** -0.5, 0.1875, ((0, 32),), jnp.float32),
        "self_output": bell_draw(seeds[8], (D, D), (max(1, 3 * D // TRI)) ** -0.5, 4.0, ((0, 32),), jnp.float32),
        "mid_gain": jnp.clip(1.0 + 0.15 * jax.random.normal(seeds[9], (D,), jnp.float32), 0.25, 1.75),
        "mid_bias": bell_draw(seeds[10], (D,), 0.5, 3.0, ((0, 32),), jnp.float32),
        "patch_weight": bell_draw(seeds[11], (PD, D), PD ** -0.5, 0.21875, ((0, 32),), jnp.float32),
        "view_table": bell_draw(seeds[12], (VIEWS, D), 1.0, 5.0, ((1, 32),), jnp.float32),
        "cross_query": bell_draw(seeds[13], (D, D), D ** -0.5, 0.1875, ((0, 32),), jnp.float32),
        "cross_memory": bell_draw(seeds[14], (D, 2 * D), (2 * D) ** -0.5, 0.125, ((0, 32),), jnp.float32),
        "cross_output": bell_draw(seeds[15], (D, D), (max(1, 5 * D // CAP)) ** -0.5, 2.5, ((0, 32),), jnp.float32),
        "last_gain": jnp.clip(1.0 + 0.15 * jax.random.normal(seeds[16], (D,), jnp.float32), 0.25, 1.75),
        "last_bias": bell_draw(seeds[17], (D,), 0.5, 3.0, ((0, 32),), jnp.float32),
        "up_weight": bell_draw(seeds[18], (D, FFN), D ** -0.5, 0.1875, ((0, 32),), jnp.float32),
        "up_bias": bell_draw(seeds[19], (FFN,), 0.5, 3.0, ((0, 32),), jnp.float32),
        "down_weight": bell_draw(seeds[20], (FFN, D), (FFN // 2) ** -0.5, 0.125, ((0, 32),), jnp.float32),
        "down_bias": bell_draw(seeds[21], (D,), 0.5, 3.0, ((0, 32),), jnp.float32),
    }


@jax.custom_vjp
def low(v):
    return lax.optimization_barrier(v.astype(jnp.bfloat16)).astype(jnp.float32)

@jax.custom_vjp
def low_back(v):
    return v

def low_keep(v):
    return (low(v), None)

def low_pass(kept, grad):
    return (grad,)

def back_keep(v):
    return (v, None)

def back_low(kept, grad):
    return (low(grad),)
low.defvjp(low_keep, low_pass)
low_back.defvjp(back_keep, back_low)

def matmul(left, right):
    return jnp.dot(left, right, precision=lax.Precision.HIGHEST, preferred_element_type=jnp.float32)

def normalize(values):
    center = values - lax.optimization_barrier(jnp.mean(values, -1, keepdims=True))
    spread = lax.optimization_barrier(jnp.mean(center * center, -1, keepdims=True))
    return center * lax.rsqrt(spread + 1e-05)

def attention(query, keys, values, count):
    factor = HEAD_DIM ** (-0.5)
    live = jnp.arange(keys.shape[0]) < count

    def one_head(item):
        head_query, head_keys, head_values = item
        scores = low_back(matmul(head_query, head_keys.T) * factor)
        masked = jnp.where(live[None, :], scores, -1e+30)
        top = lax.optimization_barrier(jnp.max(masked, -1, keepdims=True))
        lifted = jnp.exp(masked - top)
        probs = low(lifted / lax.optimization_barrier(jnp.sum(lifted, -1, keepdims=True)))
        return matmul(probs, head_values)

    def by_heads(matrix):
        return matrix.reshape(matrix.shape[0], HEADS, HEAD_DIM).transpose(1, 0, 2)
    mixed = lax.map(jax.checkpoint(one_head), (by_heads(query), by_heads(keys), by_heads(values)))
    return mixed.transpose(1, 0, 2).reshape(query.shape[0], HEADS * HEAD_DIM)

def layer(inputs, camera, feats, index, count, params):
    camera_weight, self_weight, self_output, mid_gain, mid_bias, patch_weight, view_table, cross_query, cross_memory, cross_output, last_gain, last_bias, up_weight, up_bias, down_weight, down_bias = tuple((low(param) for param in params))
    modulation = matmul(camera[None, :], camera_weight)[0]
    hidden = low(normalize(inputs) * (1.0 + modulation[:D]) + modulation[D:])
    triple = low(low_back(matmul(hidden, self_weight)))
    attended = low_back(low(attention(triple[:, :D], triple[:, D:2 * D], triple[:, 2 * D:], TRI)))
    second = inputs + low_back(matmul(attended, self_output))
    normed = low(normalize(second) * mid_gain + mid_bias)
    asked = low(low_back(matmul(normed, cross_query)))
    view_hot = (index[:, None] // VIEW_PATCHES == jnp.arange(VIEWS)[None, :]).astype(jnp.float32)
    embedded = low(low_back(matmul(feats, patch_weight) + matmul(view_hot, view_table)))
    memory = low(low_back(matmul(embedded, cross_memory)))
    crossed = low_back(low(attention(asked, memory[:, :D], memory[:, D:], count)))
    third = second + low_back(matmul(crossed, cross_output))
    final = low(normalize(third) * last_gain + last_bias)
    upper = low_back(matmul(final, up_weight) + up_bias)
    active = low(jax.nn.gelu(upper, approximate=False))
    return third + low_back(matmul(active, down_weight) + down_bias)

def reference(tokens, camera, patches, patch_count, patch_index, cotangent, camera_weight, self_weight, self_output, mid_gain, mid_bias, patch_weight, view_table, cross_query, cross_memory, cross_output, last_gain, last_bias, up_weight, up_bias, down_weight, down_bias):
    params = (camera_weight, self_weight, self_output, mid_gain, mid_bias, patch_weight, view_table, cross_query, cross_memory, cross_output, last_gain, last_bias, up_weight, up_bias, down_weight, down_bias)

    def visit(totals, item):
        token_obj, camera_obj, patch_obj, count_obj, index_obj, grad_obj = item

        def apply(inputs, feats, weights):
            return layer(inputs, camera_obj, feats, index_obj, count_obj, weights)
        output, pull = jax.vjp(apply, token_obj.astype(jnp.float32), patch_obj.astype(jnp.float32), params)
        inputs_grad, feats_grad, weight_grads = pull(grad_obj.astype(jnp.float32))
        totals = jax.tree.map(lambda left, right: left + right, totals, weight_grads)
        return (totals, (output.astype(jnp.bfloat16), inputs_grad.astype(jnp.bfloat16), feats_grad.astype(jnp.bfloat16)))
    zeros = jax.tree.map(jnp.zeros_like, params)
    totals, outputs = lax.scan(visit, zeros, (tokens, camera, patches, patch_count, patch_index, cotangent))
    return (outputs[0], outputs[1], outputs[2], totals[0], totals[1], totals[2], totals[3], totals[4], totals[5], totals[6], totals[7], totals[8], totals[9], totals[10], totals[11], totals[12], totals[13], totals[14], totals[15])
```

```python
from functools import partial

import jax
import jax.numpy as jnp
from jax import lax
from jax.experimental import pallas as pl
from jax.experimental.pallas import tpu as pltpu
from jax.sharding import PartitionSpec as P

HEAD_DIM = 64
PAIR = 2 * HEAD_DIM
VIEWS = 4
VIEW_PATCHES = 1024
BOTH = ("obj", "seq")
SMALL = 16

epsilon = 1e-05
f32 = jnp.float32
bf16 = jnp.bfloat16
NN = (((1,), (0,)), ((), ()))
NT = (((1,), (1,)), ((), ()))
TN = (((0,), (0,)), ((), ()))


def dot(left, right, dims=NN):
    return lax.dot_general(left, right, dims, preferred_element_type=f32)


def params(megabytes=56):
    return pltpu.CompilerParams(vmem_limit_bytes=megabytes * 2**20)


def norm_parts(values):
    center = values - jnp.mean(values, -1, keepdims=True)
    spread = jnp.mean(center * center, -1, keepdims=True)
    scale = lax.rsqrt(spread + epsilon)
    return center * scale, scale


def norm_back(unit, scale, grad):
    return scale * (
        grad - jnp.mean(grad, -1, keepdims=True) - unit * jnp.mean(grad * unit, -1, keepdims=True)
    )


def attend_kernel(count, masked, *refs):
    q_ref, kv = refs[0], refs[1 : 1 + count]
    bias = refs[1 + count] if masked else None
    o_ref, lse_ref = refs[-2:]
    query = q_ref[...]
    keys = jnp.concatenate([r[:, :PAIR] for r in kv], 0)
    values = jnp.concatenate([r[:, PAIR:] for r in kv], 0)
    low = lax.broadcasted_iota(jnp.int32, query.shape, 1) < HEAD_DIM
    outs, lses = [], []
    for head in range(2):
        mine = low if head == 0 else ~low
        score = dot(jnp.where(mine, query, jnp.zeros_like(query)), keys, NT)
        if masked:
            score = score + bias[...]
        top = jnp.max(score, 1, keepdims=True)
        lifted = jnp.exp(score - top)
        total = jnp.sum(lifted, 1, keepdims=True)
        outs.append(dot(lifted.astype(bf16), values) * (1.0 / total))
        lses.append(top + jnp.log(total))
    o_ref[...] = jnp.where(low, outs[0], outs[1]).astype(bf16)
    lse_ref[...] = jnp.where(low, lses[0], lses[1])[None]


def attend(query, kvs, bias):
    rows, width = query.shape
    count, slots, pairs = len(kvs), kvs[0].shape[0], width // PAIR
    row = pl.BlockSpec((rows, PAIR), lambda i: (0, i))
    slot = pl.BlockSpec((slots, 2 * PAIR), lambda i: (0, i))
    masked = bias is not None
    total = count * slots
    return pl.pallas_call(
        partial(attend_kernel, count, masked),
        grid=(pairs,),
        in_specs=[row] + [slot] * count + [pl.BlockSpec((1, total), lambda i: (0, 0))] * masked,
        out_specs=[row, pl.BlockSpec((1, rows, PAIR), lambda i: (i, 0, 0))],
        out_shape=[
            jax.ShapeDtypeStruct((rows, width), bf16),
            jax.ShapeDtypeStruct((pairs, rows, PAIR), f32),
        ],
        compiler_params=params(),
        name="attend",
        cost_estimate=pl.CostEstimate(
            flops=16 * rows * total * width,
            bytes_accessed=4 * width * (rows + total),
            transcendentals=2 * pairs * rows * total,
        ),
    )(query, *kvs, *([bias] if masked else []))


def attend_back_kernel(count, masked, *refs):
    q_ref, kv = refs[0], refs[1 : 1 + count]
    o_ref, do_ref, lse_ref = refs[1 + count : 4 + count]
    bias = refs[4 + count] if masked else None
    dq_ref, dkv = refs[-1 - count], refs[-count:]
    query, grad = q_ref[...], do_ref[...]
    slots = kv[0].shape[0]
    keys = jnp.concatenate([r[:, :PAIR] for r in kv], 0)
    values = jnp.concatenate([r[:, PAIR:] for r in kv], 0)
    low = lax.broadcasted_iota(jnp.int32, query.shape, 1) < HEAD_DIM
    lse = lse_ref[0]
    product = o_ref[...].astype(f32) * grad.astype(f32)
    dk = dv = 0.0
    dqs = []
    for head in range(2):
        mine = low if head == 0 else ~low
        head_query = jnp.where(mine, query, jnp.zeros_like(query))
        head_grad = jnp.where(mine, grad, jnp.zeros_like(grad))
        score = dot(head_query, keys, NT)
        if masked:
            score = score + bias[...]
        probs = jnp.exp(score - lse[:, HEAD_DIM * head : HEAD_DIM * head + 1])
        delta = jnp.sum(jnp.where(mine, product, 0.0), 1, keepdims=True)
        score_grad = (probs * (dot(head_grad, values, NT) - delta)).astype(bf16)
        dk = dk + dot(jnp.transpose(head_query), score_grad)
        dv = dv + dot(jnp.transpose(head_grad), probs.astype(bf16))
        dqs.append(dot(score_grad, keys))
    dq_ref[...] = (jnp.where(low, dqs[0], dqs[1]) * HEAD_DIM**-0.5).astype(bf16)
    dk, dv = jnp.transpose(dk), jnp.transpose(dv)
    for j in range(count):
        dkv[j][:, :PAIR] = dk[j * slots : (j + 1) * slots].astype(bf16)
        dkv[j][:, PAIR:] = dv[j * slots : (j + 1) * slots].astype(bf16)


def attend_back(query, kvs, out, grad, lse, bias):
    rows, width = query.shape
    count, slots, pairs = len(kvs), kvs[0].shape[0], width // PAIR
    row = pl.BlockSpec((rows, PAIR), lambda i: (0, i))
    slot = pl.BlockSpec((slots, 2 * PAIR), lambda i: (0, i))
    masked = bias is not None
    total = count * slots
    result = pl.pallas_call(
        partial(attend_back_kernel, count, masked),
        grid=(pairs,),
        in_specs=[row]
        + [slot] * count
        + [row, row, pl.BlockSpec((1, rows, PAIR), lambda i: (i, 0, 0))]
        + [pl.BlockSpec((1, total), lambda i: (0, 0))] * masked,
        out_specs=[row] + [slot] * count,
        out_shape=[jax.ShapeDtypeStruct((rows, width), bf16)]
        + [jax.ShapeDtypeStruct((slots, 2 * width), bf16)] * count,
        compiler_params=params(),
        name="attend_back",
        cost_estimate=pl.CostEstimate(
            flops=40 * rows * total * width,
            bytes_accessed=8 * width * (rows + total),
            transcendentals=2 * pairs * rows * total,
        ),
    )(query, *kvs, out, grad, lse, *([bias] if masked else []))
    return result[0], result[1:]


def block_kernel(core_ref, third_ref, cot_ref, gain_ref, shift_ref, dbias_ref, ubias_ref, up_ref, down_ref,
                 result_ref, tgrad_ref, upkeep_ref, upsend_ref, dnkeep_ref, dnsend_ref, vec_ref, ubgrad_ref,
                 unit_s, final_s, final_t, out_s, fgrad_s, scale_s, wide_s, tall_s):
    step = pl.program_id(0)
    core = core_ref[0]

    @pl.when(step == 0)
    def _():
        unit, scale = norm_parts(third_ref[...])
        unit_s[...] = unit
        scale_s[...] = scale
        final = (unit * gain_ref[...] + shift_ref[...]).astype(bf16)
        final_s[...] = final
        final_t[...] = jnp.transpose(final)
        out_s[...] = jnp.zeros_like(out_s)
        fgrad_s[...] = jnp.zeros_like(fgrad_s)

    cot = cot_ref[...]
    up = up_ref[...].reshape(-1, up_ref.shape[-1])
    down = down_ref[...].reshape(-1, down_ref.shape[-1])
    upper = dot(final_s[...], up) + ubias_ref[...]
    cdf = 0.5 * (1.0 + lax.erf(upper * (0.5**0.5)))
    active = (upper * cdf).astype(bf16)
    slope = cdf + upper * (jnp.exp(-0.5 * upper * upper) * 0.3989422804014327)
    ugrad = (slope * dot(cot, down, NT)).astype(bf16)
    out_s[...] += dot(active, down)
    fgrad_s[...] += dot(ugrad, up, NT)
    ubgrad_ref[...] = jnp.sum(ugrad.astype(f32), 0, keepdims=True)
    wide_s[...] = dot(final_t[...], ugrad).astype(bf16).reshape(wide_s.shape)
    upkeep_ref[...] = wide_s[:, core]
    upsend_ref[...] = wide_s[:, 1 - core]
    tall_s[...] = dot(jnp.transpose(active), cot).astype(bf16).reshape(tall_s.shape)
    dnkeep_ref[...] = tall_s[:, core]
    dnsend_ref[...] = tall_s[:, 1 - core]

    @pl.when(step == pl.num_programs(0) - 1)
    def _():
        result_ref[...] = (third_ref[...] + (out_s[...] + dbias_ref[...])).astype(bf16)
        unit, fgrad, cotf = unit_s[...], fgrad_s[...], cot.astype(f32)
        tgrad_ref[...] = cotf + norm_back(unit, scale_s[...], fgrad * gain_ref[...])
        vec_ref[...] = jnp.zeros_like(vec_ref)
        vec_ref[0:1, :] = jnp.sum(fgrad * unit, 0, keepdims=True)
        vec_ref[1:2, :] = jnp.sum(fgrad, 0, keepdims=True)
        vec_ref[2:3, :] = jnp.sum(cotf, 0, keepdims=True)


def feed_forward(core, third, cot, gain, shift, down_bias, up_bias, packed, up_row, down_row, shard):
    rows, width = third.shape
    parts = packed.shape[0]
    hidden = up_bias.shape[1]
    tile = 512
    per = width // tile
    tall = hidden // parts
    spread = tile // tall
    steps = hidden // tile
    whole = lambda shape: pl.BlockSpec(shape, lambda j, c: (0,) * len(shape))
    wide_map = lambda base: (lambda j, c: (0, base + j // per, j % per))
    half = parts // 2
    return pl.pallas_call(
        block_kernel,
        grid_spec=pltpu.PrefetchScalarGridSpec(
            num_scalar_prefetch=1,
            grid=(steps,),
            in_specs=[
                whole((rows, width)),
                whole((rows, width)),
                whole((1, width)),
                whole((1, width)),
                whole((1, width)),
                pl.BlockSpec((1, tile), lambda j, c: (0, j)),
                pl.BlockSpec((parts, shard, tile), wide_map(up_row // shard)),
                pl.BlockSpec((spread, tall, width), lambda j, c: (j, down_row // tall, 0)),
            ],
            out_specs=[
                whole((rows, width)),
                whole((rows, width)),
                pl.BlockSpec((half, shard, tile), wide_map(0)),
                pl.BlockSpec((half, shard, tile), wide_map(0)),
                pl.BlockSpec((spread // 2, tall, width), lambda j, c: (j, 0, 0)),
                pl.BlockSpec((spread // 2, tall, width), lambda j, c: (j, 0, 0)),
                whole((8, width)),
                pl.BlockSpec((1, tile), lambda j, c: (0, j)),
            ],
            scratch_shapes=[
                pltpu.VMEM((rows, width), f32),
                pltpu.VMEM((rows, width), bf16),
                pltpu.VMEM((width, rows), bf16),
                pltpu.VMEM((rows, width), f32),
                pltpu.VMEM((rows, width), f32),
                pltpu.VMEM((rows, 1), f32),
                pltpu.VMEM((half, 2, shard, tile), bf16),
                pltpu.VMEM((spread // 2, 2, tall, width), bf16),
            ],
        ),
        out_shape=[
            jax.ShapeDtypeStruct((rows, width), bf16),
            jax.ShapeDtypeStruct((rows, width), f32),
            jax.ShapeDtypeStruct((half, tall, width), bf16),
            jax.ShapeDtypeStruct((half, tall, width), bf16),
            jax.ShapeDtypeStruct((half, tall, width), bf16),
            jax.ShapeDtypeStruct((half, tall, width), bf16),
            jax.ShapeDtypeStruct((8, width), f32),
            jax.ShapeDtypeStruct((1, hidden), f32),
        ],
        compiler_params=params(),
        name="feed_forward",
        cost_estimate=pl.CostEstimate(
            flops=12 * rows * width * hidden,
            bytes_accessed=8 * width * hidden + 12 * rows * width,
            transcendentals=2 * rows * hidden,
        ),
    )(core, third, cot, gain, shift, down_bias, up_bias, packed, packed)


class Grid:
    def __init__(self, mesh):
        self.obj, self.seq = mesh.shape["obj"], mesh.shape["seq"]
        self.all = self.obj * self.seq
        self.me = lax.axis_index("obj") * self.seq + lax.axis_index("seq")
        self.group = [m for m in (1 << k for k in range(20)) if m < self.seq // 2]
        self.far = self.seq // 2

    def swap(self, value, mask):
        return lax.ppermute(value, BOTH, [(i, i ^ mask) for i in range(self.all)])

    def bit(self, mask):
        return (self.me // mask) % 2

    def orders(self):
        low = [m for m in self.group[1:]] + [self.far]
        high = [m for m in (1 << k for k in range(20)) if self.seq <= m < self.all]
        return high[::-1] + low, high + low

    def gather_group(self, value):
        found = {0: value}
        for mask in self.group[1:][::-1] + self.group[:1]:
            found.update({d ^ mask: self.swap(v, mask) for d, v in list(found.items())})
        return [found[d] for d in range(self.seq // 2)]

    def sum_group(self, terms):
        terms = {d: [t] for d, t in enumerate(terms)}
        for mask in self.group[:1] + self.group[1:]:
            for d in [d for d in terms if d & mask]:
                moved = self.swap(add(terms.pop(d)), mask)
                terms[d ^ mask].append(moved)
        return add(terms[0])

    def scatter(self, keep, send, order):
        masks = [1 << k for k in range(20) if 1 < 1 << k < self.all][::-1]
        terms = [keep, self.swap(send, 1)]
        terms = [t.reshape((2,) * len(masks) + t.shape[1:]) for t in terms]
        for mask in order:
            axis = masks.index(mask)
            masks.remove(mask)
            bit = self.bit(mask)
            pick = lambda t, which: lax.dynamic_index_in_dim(t, which, axis, keepdims=False)
            moved = self.swap(add([pick(t, 1 - bit) for t in terms]), mask)
            terms = [pick(t, bit) for t in terms] + [moved]
        return sum(t.astype(f32) for t in terms)


def add(terms):
    if len(terms) == 1:
        return terms[0]
    return sum(t.astype(f32) for t in terms).astype(bf16)


def split_pairs(matrix):
    rows, width = matrix.shape
    return matrix.reshape(rows, 2, width // (2 * PAIR), PAIR).transpose(0, 2, 1, 3).reshape(rows, width)


def join_pairs(matrix):
    rows, width = matrix.shape
    return matrix.reshape(rows, width // (2 * PAIR), 2, PAIR).transpose(0, 2, 1, 3).reshape(rows, width)


def stack_columns(matrix, width):
    rows = matrix.shape[0]
    return matrix.reshape(rows, -1, width).transpose(1, 0, 2).reshape(-1, width)


def unstack_columns(matrix, rows):
    width = matrix.shape[1]
    return matrix.reshape(-1, rows, width).transpose(1, 0, 2).reshape(rows, -1)


def pad_rows(matrix, rows):
    return jnp.pad(matrix, ((0, rows - matrix.shape[0]), (0, 0)))


def on_device(
    mesh,
    tokens,
    camera,
    patches,
    patch_count,
    patch_index,
    cotangent,
    camera_weight,
    self_weight,
    self_output,
    mid_gain,
    mid_bias,
    patch_weight,
    view_table,
    cross_query,
    cross_memory,
    cross_output,
    last_gain,
    last_bias,
    up_weight,
    up_bias,
    down_weight,
    down_bias,
):
    grid = Grid(mesh)
    parts = grid.all
    width = self_output.shape[1]
    low = lambda v: v.astype(bf16)
    factor = HEAD_DIM**-0.5
    core = grid.bit(1)
    half = grid.bit(grid.far)

    def compact(value):
        mine = lax.dynamic_index_in_dim(value, half, 0, keepdims=False)
        other = lax.dynamic_index_in_dim(value, 1 - half, 0, keepdims=False)
        return jnp.concatenate([mine, grid.swap(other, grid.far)], 0)

    def spread(value):
        rows = value.shape[0] // 2
        mine, other = value[:rows], grid.swap(value[rows:], grid.far)
        return jnp.where(half == 0, jnp.stack([mine, other]), jnp.stack([other, mine]))

    shard = self_output.shape[0]
    queries_width = width
    self_mixed = jnp.concatenate(
        [low(self_weight[:, :width]), split_pairs(low(self_weight[:, width:]))], 1
    )
    small = jnp.concatenate(
        [
            low(camera_weight).reshape(-1),
            low(view_table).reshape(-1),
            low(mid_gain),
            low(mid_bias),
            low(last_gain),
            low(last_bias),
            low(down_bias),
            low(up_bias),
        ]
    )
    small_sizes = [
        camera_weight.size,
        view_table.size,
        shard,
        shard,
        shard,
        shard,
        shard,
        up_bias.size,
    ]
    small_rows = jnp.pad(small, (0, SMALL * width - small.size)).reshape(SMALL, width)
    first = jnp.concatenate([stack_columns(self_mixed, width), small_rows], 0)
    patch_rows = patch_weight.shape[0]
    patch_room = -(-patch_rows // 16) * 16
    tall = down_weight.shape[0]
    blocks = [
        stack_columns(low(up_weight), width),
        low(down_weight),
        low(self_output),
        low(cross_query),
        low(cross_output),
        stack_columns(split_pairs(low(cross_memory)), width),
        pad_rows(low(patch_weight), patch_room),
    ]
    starts = [0]
    for block in blocks:
        starts.append(starts[-1] + block.shape[0])
    second_pack = jnp.concatenate(blocks, 0)
    first = lax.all_gather(first, BOTH, axis=0, tiled=False)
    first_done, second_pack = lax.optimization_barrier((first, second_pack))
    first = first_done
    packed = lax.all_gather(second_pack, BOTH, axis=0, tiled=False)

    def square(source, start, rows):
        return source[:, start : start + rows].reshape(parts * rows, width)

    def columns(source, start, rows, count):
        return jnp.concatenate(
            [square(source, start + q * rows, rows) for q in range(count)], 1
        )

    full_q = square(first, 0, shard)
    full_kv = columns(first, shard, shard, 2)
    tiny = first[:, 3 * shard :].reshape(parts, -1)
    pieces = []
    at = 0
    for size in small_sizes:
        pieces.append(tiny[:, at : at + size].astype(f32))
        at += size
    full_camera = pieces[0].reshape(parts, 16, -1).transpose(1, 0, 2).reshape(16, -1)
    full_view = pieces[1].reshape(parts, VIEWS, -1).transpose(1, 0, 2).reshape(VIEWS, -1)
    g_mid, b_mid, g_last, b_last, b_down, b_up = (p.reshape(1, -1) for p in pieces[2:])
    full_out = square(packed, starts[2], shard)
    full_cq = square(packed, starts[3], shard)
    full_co = square(packed, starts[4], shard)
    full_mem = columns(packed, starts[5], shard, 2)
    full_patch = packed[:, starts[6] : starts[6] + patch_rows].reshape(-1, width)

    x = compact(tokens).astype(f32)
    cot = compact(cotangent)
    feats = compact(patches)
    views = compact(patch_index) // VIEW_PATCHES
    camera_mine = lax.dynamic_index_in_dim(camera, half, 0, keepdims=False)
    live = lax.dynamic_index_in_dim(patch_count, half, 0, keepdims=False)
    modulation = jnp.sum(camera_mine[:, None] * full_camera, 0)
    scale1, shift1 = 1.0 + modulation[None, :width], modulation[None, width:]
    unit1, rstd1 = norm_parts(x)
    hidden = low(unit1 * scale1 + shift1)
    query = low(low(dot(hidden, full_q)).astype(f32) * factor)
    kv = low(dot(hidden, full_kv))
    kvs = grid.gather_group(kv)

    view_hot = (views[:, None] == jnp.arange(VIEWS)[None, :]).astype(f32)
    view_part = sum(view_hot[:, v : v + 1] * full_view[v : v + 1] for v in range(VIEWS))
    embedded = low(dot(feats, full_patch) + view_part)
    memory = low(dot(embedded, full_mem))
    mems = grid.gather_group(memory)
    place = lax.axis_index("seq")
    chunk = patches.shape[1]
    lane = jnp.arange(chunk)
    slots = jnp.concatenate(
        [
            chunk * (place ^ d ^ far) + lane
            for d in range(grid.seq // 2)
            for far in (0, grid.far)
        ]
    )
    bias = jnp.where(slots < live, 0.0, -1e30).astype(f32).reshape(1, -1)

    attended, lse1 = attend(query, kvs, None)
    second = x + dot(attended, full_out)
    unit2, rstd2 = norm_parts(second)
    normed = low(unit2 * g_mid + b_mid)
    asked = low(low(dot(normed, full_cq)).astype(f32) * factor)
    crossed, lse2 = attend(asked, mems, bias)
    third = second + dot(crossed, full_co)
    (
        result,
        third_grad,
        up_keep,
        up_send,
        down_keep,
        down_send,
        last_vectors,
        up_bias_grad,
    ) = feed_forward(
        core.reshape(1).astype(jnp.int32),
        third,
        cot,
        g_last,
        b_last,
        b_down,
        b_up,
        packed,
        starts[0],
        starts[1],
        shard,
    )
    order_a, order_b = grid.orders()
    up_grad = grid.scatter(up_keep, up_send, order_a)
    down_grad = grid.scatter(down_keep, down_send, order_b)

    def scatter_rows(grads, order):
        joined = jnp.concatenate(grads, 1)
        joined = joined.reshape(parts // 2, 2, *joined.shape[1:])
        keep = lax.dynamic_index_in_dim(joined, core, 1, keepdims=False)
        send = lax.dynamic_index_in_dim(joined, 1 - core, 1, keepdims=False)
        return grid.scatter(keep, send, order)

    def by_owner(grad, columns=1):
        grad = low(grad).reshape(parts, -1, grad.shape[1])
        return [grad[:, :, q * width : (q + 1) * width] for q in range(columns)]

    third_low = low(third_grad)
    co_grad = dot(crossed, third_low, TN)
    crossed_grad = low(dot(third_low, full_co, NT))
    asked_grad, mem_terms = attend_back(asked, mems, crossed, crossed_grad, lse2, bias)
    memory_grad = grid.sum_group(mem_terms)
    cq_grad = dot(normed, asked_grad, TN)
    normed_grad = dot(asked_grad, full_cq, NT)
    second_grad = third_grad + norm_back(unit2, rstd2, normed_grad * g_mid)
    mid_gain_grad = jnp.sum(normed_grad * unit2, 0)
    mid_bias_grad = jnp.sum(normed_grad, 0)
    second_low = low(second_grad)
    so_grad = dot(attended, second_low, TN)
    attended_grad = low(dot(second_low, full_out, NT))
    query_grad, pair_terms = attend_back(query, kvs, attended, attended_grad, lse1, None)
    mem_w_grad = dot(embedded, memory_grad, TN)
    embedded_grad = low(dot(memory_grad, full_mem, NT))
    patch_w_grad = dot(feats, embedded_grad, TN)
    view_grad = jnp.stack(
        [jnp.sum(view_hot[:, v : v + 1] * embedded_grad.astype(f32), 0) for v in range(VIEWS)]
    )
    patch_grad = low(dot(embedded_grad, full_patch, NT))
    cross_sum = scatter_rows(by_owner(co_grad) + by_owner(cq_grad), order_a)
    mem_sum = scatter_rows(
        by_owner(mem_w_grad, 2)
        + [jnp.pad(by_owner(patch_w_grad)[0], ((0, 0), (0, patch_room - patch_rows), (0, 0)))],
        order_b,
    )
    pair_grad = grid.sum_group(pair_terms)
    q_w_grad = dot(hidden, query_grad, TN)
    kv_w_grad = dot(hidden, pair_grad, TN)
    hidden_grad = dot(query_grad, full_q, NT) + dot(pair_grad, full_kv, NT)
    modulation_grad = jnp.concatenate(
        [jnp.sum(hidden_grad * unit1, 0), jnp.sum(hidden_grad, 0)]
    )
    camera_grad = camera_mine[:, None] * modulation_grad[None]
    token_grad = low(second_grad + norm_back(unit1, rstd1, hidden_grad * scale1))
    small_grad = jnp.concatenate(
        [
            camera_grad.reshape(16, parts, -1).transpose(1, 0, 2).reshape(parts, -1),
            view_grad.reshape(VIEWS, parts, -1).transpose(1, 0, 2).reshape(parts, -1),
            mid_gain_grad.reshape(parts, -1),
            mid_bias_grad.reshape(parts, -1),
            last_vectors[0].reshape(parts, -1),
            last_vectors[1].reshape(parts, -1),
            last_vectors[2].reshape(parts, -1),
            up_bias_grad.reshape(parts, -1),
        ],
        1,
    )
    small_grad = jnp.pad(small_grad, ((0, 0), (0, SMALL * width - small_grad.shape[1])))
    small_grad = low(small_grad).reshape(parts, SMALL, width)
    self_sum_a = scatter_rows(by_owner(so_grad) + by_owner(q_w_grad), order_a)
    self_sum_b = scatter_rows(by_owner(kv_w_grad, 2) + [small_grad], order_b)

    tiny = self_sum_b[2 * shard :].reshape(-1)
    pieces = []
    at = 0
    for size in small_sizes:
        pieces.append(tiny[at : at + size])
        at += size
    kv_own = join_pairs(unstack_columns(self_sum_b[: 2 * shard], shard))
    return (
        spread(result),
        spread(token_grad),
        spread(patch_grad),
        pieces[0].reshape(camera_weight.shape),
        jnp.concatenate([self_sum_a[shard:], kv_own], 1),
        self_sum_a[:shard],
        pieces[2],
        pieces[3],
        mem_sum[2 * shard : 2 * shard + patch_rows],
        pieces[1].reshape(view_table.shape),
        cross_sum[shard:],
        join_pairs(unstack_columns(mem_sum[: 2 * shard], shard)),
        cross_sum[:shard],
        pieces[4],
        pieces[5],
        unstack_columns(up_grad, shard),
        pieces[7],
        down_grad,
        pieces[6],
    )


def solution(mesh):
    rows, flat, lanes = P(BOTH, None), P(BOTH), P(None, BOTH)
    sequence = P("obj", "seq", None)
    in_specs = (
        sequence,
        P("obj", None),
        sequence,
        P("obj"),
        P("obj", "seq"),
        sequence,
        lanes,
        rows,
        rows,
        flat,
        flat,
        rows,
        lanes,
        rows,
        rows,
        rows,
        flat,
        flat,
        rows,
        flat,
        rows,
        flat,
    )
    out_specs = (
        sequence,
        sequence,
        sequence,
        lanes,
        rows,
        rows,
        flat,
        flat,
        rows,
        lanes,
        rows,
        rows,
        rows,
        flat,
        flat,
        rows,
        flat,
        rows,
        flat,
    )
    return jax.shard_map(
        partial(on_device, mesh),
        mesh=mesh,
        in_specs=in_specs,
        out_specs=out_specs,
        check_vma=False,
    )
```

```python
from functools import partial

import jax
import jax.numpy as jnp
from jax import lax
from jax.experimental import pallas as pl
from jax.experimental.pallas import tpu as pltpu
from jax.sharding import PartitionSpec as P

HEAD_DIM = 64
PAIR = 2 * HEAD_DIM
VIEWS = 4
VIEW_PATCHES = 1024
BOTH = ("obj", "ring", "core")
SEQ = ("ring", "core")

epsilon = 1e-05
f32 = jnp.float32
bf16 = jnp.bfloat16
NN = (((1,), (0,)), ((), ()))
NT = (((1,), (1,)), ((), ()))
TN = (((0,), (0,)), ((), ()))


def dot(left, right, dims=NN):
    return lax.dot_general(left, right, dims, preferred_element_type=f32)


def params(megabytes=56):
    return pltpu.CompilerParams(vmem_limit_bytes=megabytes * 2**20)


def norm_parts(values):
    center = values - jnp.mean(values, -1, keepdims=True)
    spread = jnp.mean(center * center, -1, keepdims=True)
    scale = lax.rsqrt(spread + epsilon)
    return center * scale, scale


def norm_back(unit, scale, grad):
    return scale * (
        grad - jnp.mean(grad, -1, keepdims=True) - unit * jnp.mean(grad * unit, -1, keepdims=True)
    )


def attend_kernel(count, masked, *refs):
    q_ref, kv = refs[0], refs[1 : 1 + count]
    bias = refs[1 + count] if masked else None
    o_ref, lse_ref = refs[-2:]
    query = q_ref[...]
    keys = jnp.concatenate([r[:, :PAIR] for r in kv], 0)
    values = jnp.concatenate([r[:, PAIR:] for r in kv], 0)
    low = lax.broadcasted_iota(jnp.int32, query.shape, 1) < HEAD_DIM
    outs, lses = [], []
    for head in range(2):
        mine = low if head == 0 else ~low
        score = dot(jnp.where(mine, query, jnp.zeros_like(query)), keys, NT)
        if masked:
            score = score + bias[...]
        top = jnp.max(score, 1, keepdims=True)
        lifted = jnp.exp(score - top)
        total = jnp.sum(lifted, 1, keepdims=True)
        outs.append(dot(lifted.astype(bf16), values) * (1.0 / total))
        lses.append(top + jnp.log(total))
    o_ref[...] = jnp.where(low, outs[0], outs[1]).astype(bf16)
    lse_ref[...] = jnp.where(low, lses[0], lses[1])[None]


def attend(query, kvs, bias):
    rows, width = query.shape
    count, slots, pairs = len(kvs), kvs[0].shape[0], width // PAIR
    row = pl.BlockSpec((rows, PAIR), lambda i: (0, i))
    slot = pl.BlockSpec((slots, 2 * PAIR), lambda i: (0, i))
    masked = bias is not None
    total = count * slots
    return pl.pallas_call(
        partial(attend_kernel, count, masked),
        grid=(pairs,),
        in_specs=[row] + [slot] * count + [pl.BlockSpec((1, total), lambda i: (0, 0))] * masked,
        out_specs=[row, pl.BlockSpec((1, rows, PAIR), lambda i: (i, 0, 0))],
        out_shape=[
            jax.ShapeDtypeStruct((rows, width), bf16),
            jax.ShapeDtypeStruct((pairs, rows, PAIR), f32),
        ],
        compiler_params=params(),
        name="attend",
        cost_estimate=pl.CostEstimate(
            flops=16 * rows * total * width,
            bytes_accessed=4 * width * (rows + total),
            transcendentals=2 * pairs * rows * total,
        ),
    )(query, *kvs, *([bias] if masked else []))


def attend_back_kernel(count, masked, *refs):
    q_ref, kv = refs[0], refs[1 : 1 + count]
    o_ref, do_ref, lse_ref = refs[1 + count : 4 + count]
    bias = refs[4 + count] if masked else None
    dq_ref, dkv = refs[-1 - count], refs[-count:]
    query, grad = q_ref[...], do_ref[...]
    slots = kv[0].shape[0]
    keys = jnp.concatenate([r[:, :PAIR] for r in kv], 0)
    values = jnp.concatenate([r[:, PAIR:] for r in kv], 0)
    low = lax.broadcasted_iota(jnp.int32, query.shape, 1) < HEAD_DIM
    lse = lse_ref[0]
    product = o_ref[...].astype(f32) * grad.astype(f32)
    dk = dv = 0.0
    dqs = []
    for head in range(2):
        mine = low if head == 0 else ~low
        head_query = jnp.where(mine, query, jnp.zeros_like(query))
        head_grad = jnp.where(mine, grad, jnp.zeros_like(grad))
        score = dot(head_query, keys, NT)
        if masked:
            score = score + bias[...]
        probs = jnp.exp(score - lse[:, HEAD_DIM * head : HEAD_DIM * head + 1])
        delta = jnp.sum(jnp.where(mine, product, 0.0), 1, keepdims=True)
        score_grad = (probs * (dot(head_grad, values, NT) - delta)).astype(bf16)
        dk = dk + dot(jnp.transpose(head_query), score_grad)
        dv = dv + dot(jnp.transpose(head_grad), probs.astype(bf16))
        dqs.append(dot(score_grad, keys))
    dq_ref[...] = (jnp.where(low, dqs[0], dqs[1]) * HEAD_DIM**-0.5).astype(bf16)
    dk, dv = jnp.transpose(dk), jnp.transpose(dv)
    for j in range(count):
        dkv[j][:, :PAIR] = dk[j * slots : (j + 1) * slots].astype(bf16)
        dkv[j][:, PAIR:] = dv[j * slots : (j + 1) * slots].astype(bf16)


def attend_back(query, kvs, out, grad, lse, bias):
    rows, width = query.shape
    count, slots, pairs = len(kvs), kvs[0].shape[0], width // PAIR
    row = pl.BlockSpec((rows, PAIR), lambda i: (0, i))
    slot = pl.BlockSpec((slots, 2 * PAIR), lambda i: (0, i))
    masked = bias is not None
    total = count * slots
    result = pl.pallas_call(
        partial(attend_back_kernel, count, masked),
        grid=(pairs,),
        in_specs=[row]
        + [slot] * count
        + [row, row, pl.BlockSpec((1, rows, PAIR), lambda i: (i, 0, 0))]
        + [pl.BlockSpec((1, total), lambda i: (0, 0))] * masked,
        out_specs=[row] + [slot] * count,
        out_shape=[jax.ShapeDtypeStruct((rows, width), bf16)]
        + [jax.ShapeDtypeStruct((slots, 2 * width), bf16)] * count,
        compiler_params=params(),
        name="attend_back",
        cost_estimate=pl.CostEstimate(
            flops=40 * rows * total * width,
            bytes_accessed=8 * width * (rows + total),
            transcendentals=2 * pairs * rows * total,
        ),
    )(query, *kvs, out, grad, lse, *([bias] if masked else []))
    return result[0], result[1:]


def block_kernel(third_ref, cot_ref, gain_ref, shift_ref, dbias_ref, ubias_ref, up_ref, down_ref,
                 result_ref, tgrad_ref, grads_ref, vec_ref, ubgrad_ref,
                 unit_s, final_s, final_t, out_s, fgrad_s, scale_s, wide_s, tall_s, sems):
    step = pl.program_id(0)
    last = pl.num_programs(0) - 1
    slot = lax.rem(step, 2)
    _, parts, shard, tile = wide_s.shape
    _, spread, tall, width = tall_s.shape
    per = width // tile

    def copies(at, place):
        row = pl.multiple_of((at // per) * shard, shard)
        lane = pl.multiple_of(lax.rem(at, per) * tile, tile)
        return (
            pltpu.make_async_copy(
                wide_s.at[place],
                grads_ref.at[:, pl.ds(row, shard), pl.ds(lane, tile)],
                sems.at[0, place],
            ),
            pltpu.make_async_copy(
                tall_s.at[place],
                grads_ref.at[pl.ds(at * spread, spread), pl.ds(tall, tall), :],
                sems.at[1, place],
            ),
        )

    @pl.when(step == 0)
    def _():
        unit, scale = norm_parts(third_ref[...])
        unit_s[...] = unit
        scale_s[...] = scale
        final = (unit * gain_ref[...] + shift_ref[...]).astype(bf16)
        final_s[...] = final
        final_t[...] = jnp.transpose(final)
        out_s[...] = jnp.zeros_like(out_s)
        fgrad_s[...] = jnp.zeros_like(fgrad_s)

    @pl.when(step >= 2)
    def _():
        for copy in copies(step - 2, slot):
            copy.wait()

    cot = cot_ref[...]
    up = up_ref[...].reshape(-1, up_ref.shape[-1])
    down = down_ref[...].reshape(-1, down_ref.shape[-1])
    upper = dot(final_s[...], up) + ubias_ref[...]
    cdf = 0.5 * (1.0 + lax.erf(upper * (0.5**0.5)))
    active = (upper * cdf).astype(bf16)
    slope = cdf + upper * (jnp.exp(-0.5 * upper * upper) * 0.3989422804014327)
    ugrad = (slope * dot(cot, down, NT)).astype(bf16)
    out_s[...] += dot(active, down)
    fgrad_s[...] += dot(ugrad, up, NT)
    ubgrad_ref[...] = jnp.sum(ugrad.astype(f32), 0, keepdims=True)
    wide_s[slot] = dot(final_t[...], ugrad).astype(bf16).reshape(wide_s.shape[1:])
    tall_s[slot] = dot(jnp.transpose(active), cot).astype(bf16).reshape(tall_s.shape[1:])
    for copy in copies(step, slot):
        copy.start()

    @pl.when(step == last)
    def _():
        result_ref[...] = (third_ref[...] + (out_s[...] + dbias_ref[...])).astype(bf16)
        unit, fgrad, cotf = unit_s[...], fgrad_s[...], cot.astype(f32)
        tgrad_ref[...] = cotf + norm_back(unit, scale_s[...], fgrad * gain_ref[...])
        vec_ref[...] = jnp.zeros_like(vec_ref)
        vec_ref[0:1, :] = jnp.sum(fgrad * unit, 0, keepdims=True)
        vec_ref[1:2, :] = jnp.sum(fgrad, 0, keepdims=True)
        vec_ref[2:3, :] = jnp.sum(cotf, 0, keepdims=True)
        for copy in copies(step - 1, 1 - slot) + copies(step, slot):
            copy.wait()


def feed_forward(third, cot, gain, shift, down_bias, up_bias, packed, shard):
    rows, width = third.shape
    parts = packed.shape[0]
    hidden = up_bias.shape[1]
    tile = 512
    per = width // tile
    tall = hidden // parts
    spread = tile // tall
    steps = hidden // tile
    whole = lambda shape: pl.BlockSpec(shape, lambda j: (0,) * len(shape))
    return pl.pallas_call(
        block_kernel,
        grid=(steps,),
        in_specs=[
            whole((rows, width)),
            whole((rows, width)),
            whole((1, width)),
            whole((1, width)),
            whole((1, width)),
            pl.BlockSpec((1, tile), lambda j: (0, j)),
            pl.BlockSpec((parts, shard, tile), lambda j: (0, j // per, j % per)),
            pl.BlockSpec((spread, tall, width), lambda j: (j, 1, 0)),
        ],
        out_specs=[
            whole((rows, width)),
            whole((rows, width)),
            pl.BlockSpec(memory_space=pl.ANY),
            whole((8, width)),
            pl.BlockSpec((1, tile), lambda j: (0, j)),
        ],
        scratch_shapes=[
            pltpu.VMEM((rows, width), f32),
            pltpu.VMEM((rows, width), bf16),
            pltpu.VMEM((width, rows), bf16),
            pltpu.VMEM((rows, width), f32),
            pltpu.VMEM((rows, width), f32),
            pltpu.VMEM((rows, 1), f32),
            pltpu.VMEM((2, parts, shard, tile), bf16),
            pltpu.VMEM((2, spread, tall, width), bf16),
            pltpu.SemaphoreType.DMA((2, 2)),
        ],
        out_shape=[
            jax.ShapeDtypeStruct((rows, width), bf16),
            jax.ShapeDtypeStruct((rows, width), f32),
            jax.ShapeDtypeStruct((parts, 2 * tall, width), bf16),
            jax.ShapeDtypeStruct((8, width), f32),
            jax.ShapeDtypeStruct((1, hidden), f32),
        ],
        compiler_params=params(),
        name="feed_forward",
        cost_estimate=pl.CostEstimate(
            flops=12 * rows * width * hidden,
            bytes_accessed=8 * width * hidden + 12 * rows * width,
            transcendentals=2 * rows * hidden,
        ),
    )(third, cot, gain, shift, down_bias, up_bias, packed, packed)


def grads_kernel(jobs, core_ref, *refs):
    ins, (keep_ref, send_ref) = refs[:-2], refs[-2:]
    step = pl.program_id(0)
    half, room, width = keep_ref.shape

    def store(block, rows):
        block = block.astype(bf16).reshape(half, 2, rows, width)
        keep_ref[:, :rows] = block[:, 0]
        send_ref[:, :rows] = block[:, 1]

    def swapped(block, rows):
        block = block.astype(bf16).reshape(half, 2, rows, width)
        keep_ref[:, :rows] = block[:, 1]
        send_ref[:, :rows] = block[:, 0]

    for at, (left, right, column) in enumerate(jobs):

        @pl.when(step == at)
        def _():
            rows = ins[left].shape[1] // (2 * half)
            if rows < room:
                keep_ref[...] = jnp.zeros_like(keep_ref)
                send_ref[...] = jnp.zeros_like(send_ref)
            block = dot(ins[left][...], ins[right][:, column * width : (column + 1) * width], TN)

            @pl.when(core_ref[0] == 0)
            def _():
                store(block, rows)

            @pl.when(core_ref[0] == 1)
            def _():
                swapped(block, rows)


def weight_grads(core, arrays, jobs, parts, shard, width):
    count = len(jobs)
    whole = lambda array: pl.BlockSpec(array.shape, lambda j, c: (0, 0))
    out = pl.BlockSpec((parts // 2, shard, width), lambda j, c: (0, j, 0))
    flops = sum(2 * arrays[i].shape[0] * arrays[i].shape[1] * width for i, _, _ in jobs)
    return pl.pallas_call(
        partial(grads_kernel, jobs),
        grid_spec=pltpu.PrefetchScalarGridSpec(
            num_scalar_prefetch=1,
            grid=(count,),
            in_specs=[whole(array) for array in arrays],
            out_specs=[out, out],
        ),
        out_shape=[jax.ShapeDtypeStruct((parts // 2, count * shard, width), bf16)] * 2,
        compiler_params=params(),
        name="weight_grads",
        cost_estimate=pl.CostEstimate(
            flops=flops,
            bytes_accessed=2 * parts * count * shard * width + sum(2 * a.size for a in arrays),
            transcendentals=0,
        ),
    )(core, *arrays)


class Grid:
    def __init__(self, mesh):
        self.obj, self.seq = mesh.shape["obj"], mesh.shape["ring"] * 2
        self.all = self.obj * self.seq
        self.place = lax.axis_index("ring") * 2 + lax.axis_index("core")
        self.me = lax.axis_index("obj") * self.seq + self.place
        self.group = [m for m in (1 << k for k in range(20)) if m < self.seq // 2]
        self.far = self.seq // 2

    def swap(self, value, mask):
        return lax.ppermute(value, BOTH, [(i, i ^ mask) for i in range(self.all)])

    def bit(self, mask):
        return (self.me // mask) % 2

    def gather_group(self, value):
        found = {0: value}
        for mask in self.group[1:][::-1] + self.group[:1]:
            found.update({d ^ mask: self.swap(v, mask) for d, v in list(found.items())})
        return [found[d] for d in range(self.seq // 2)]

    def sum_group(self, terms):
        terms = {d: [t] for d, t in enumerate(terms)}
        for mask in self.group[:1] + self.group[1:]:
            for d in [d for d in terms if d & mask]:
                moved = self.swap(add(terms.pop(d)), mask)
                terms[d ^ mask].append(moved)
        return add(terms[0])

    def scatter(self, keep, send):
        moved = yield self.swap(send, 1)
        total = add([keep, moved]).reshape(self.obj, self.seq // 2, *keep.shape[1:])
        total = yield total
        moved = yield lax.all_to_all(total, "obj", 0, 0, tiled=True)
        total = jnp.sum(moved.astype(f32), 0).astype(bf16)
        moved = yield lax.all_to_all(total, "ring", 0, 0, tiled=True)
        yield jnp.sum(moved.astype(f32), 0)

    def exchange_core(self, terms):
        return [self.swap(t, 1) for t in terms[1::2]]

    def exchange_line(self, terms, moved):
        pairs = [add([t, m]) for t, m in zip(terms[::2], moved)]
        step = len(pairs) // 2
        while step > 1:
            pairs = [add([pairs[k], self.swap(pairs[k + step], 2 * step)]) for k in range(step)]
            step //= 2
        return pairs[0], self.swap(pairs[1], 2)


together = lax.optimization_barrier


def add(terms):
    if len(terms) == 1:
        return terms[0]
    return sum(t.astype(f32) for t in terms).astype(bf16)


def split_pairs(matrix):
    rows, width = matrix.shape
    return matrix.reshape(rows, 2, width // (2 * PAIR), PAIR).transpose(0, 2, 1, 3).reshape(rows, width)


def join_pairs(matrix):
    rows, width = matrix.shape
    return matrix.reshape(rows, width // (2 * PAIR), 2, PAIR).transpose(0, 2, 1, 3).reshape(rows, width)


def stack_columns(matrix, width):
    rows = matrix.shape[0]
    return matrix.reshape(rows, -1, width).transpose(1, 0, 2).reshape(-1, width)


def unstack_columns(matrix, rows):
    width = matrix.shape[1]
    return matrix.reshape(-1, rows, width).transpose(1, 0, 2).reshape(rows, -1)


def pad_rows(matrix, rows):
    return jnp.pad(matrix, ((0, rows - matrix.shape[0]), (0, 0)))


def on_device(
    mesh,
    tokens,
    camera,
    patches,
    patch_count,
    patch_index,
    cotangent,
    camera_weight,
    self_weight,
    self_output,
    mid_gain,
    mid_bias,
    patch_weight,
    view_table,
    cross_query,
    cross_memory,
    cross_output,
    last_gain,
    last_bias,
    up_weight,
    up_bias,
    down_weight,
    down_bias,
):
    grid = Grid(mesh)
    parts = grid.all
    width = self_output.shape[1]
    low = lambda v: v.astype(bf16)
    factor = HEAD_DIM**-0.5
    core = grid.bit(1)
    half = grid.bit(grid.far)

    def compact(value):
        mine = lax.dynamic_index_in_dim(value, half, 0, keepdims=False)
        other = lax.dynamic_index_in_dim(value, 1 - half, 0, keepdims=False)
        return jnp.concatenate([mine, grid.swap(other, grid.far)], 0)

    def spread(value):
        rows = value.shape[0] // 2
        mine, other = value[:rows], grid.swap(value[rows:], grid.far)
        return jnp.where(half == 0, jnp.stack([mine, other]), jnp.stack([other, mine]))

    shard = self_output.shape[0]
    self_mixed = jnp.concatenate(
        [low(self_weight[:, :width]), split_pairs(low(self_weight[:, width:]))], 1
    )
    small = jnp.concatenate(
        [
            low(camera_weight).reshape(-1),
            low(view_table).reshape(-1),
            low(mid_gain),
            low(mid_bias),
            low(last_gain),
            low(last_bias),
            low(down_bias),
            low(up_bias),
        ]
    )
    small_sizes = [
        camera_weight.size,
        view_table.size,
        shard,
        shard,
        shard,
        shard,
        shard,
        up_bias.size,
    ]
    patch_rows = patch_weight.shape[0]
    small_count = -(-small.size // width)
    patch_room = -(-(patch_rows + small_count) // shard) * shard
    small_rows = jnp.pad(small, (0, small_count * width - small.size)).reshape(-1, width)
    first = jnp.concatenate(
        [
            stack_columns(self_mixed, width),
            low(self_output),
            low(cross_query),
            low(cross_output),
            stack_columns(split_pairs(low(cross_memory)), width),
            pad_rows(jnp.concatenate([low(patch_weight), small_rows], 0), patch_room),
        ],
        0,
    )
    tokens_all = jnp.concatenate(grid.gather_group(compact(tokens)), 0)
    feats_all = jnp.concatenate(grid.gather_group(compact(patches)), 0)
    views_all = jnp.concatenate(grid.gather_group(compact(patch_index)), 0) // VIEW_PATCHES
    cot = compact(cotangent)
    first = lax.all_gather(first, BOTH, axis=0, tiled=False)
    ffn_mine = jnp.concatenate([stack_columns(low(up_weight), width), low(down_weight)], 0)
    first, ffn_mine, tokens_all, feats_all, views_all, cot = together(
        (first, ffn_mine, tokens_all, feats_all, views_all, cot)
    )
    packed = lax.all_gather(ffn_mine, BOTH, axis=0, tiled=False)

    def square(start, rows=shard):
        return first[:, start : start + rows].reshape(parts * rows, width)

    def columns(start, count):
        return jnp.concatenate([square(start + q * shard) for q in range(count)], 1)

    full_q = square(0)
    full_kv = columns(shard, 2)
    full_out = square(3 * shard)
    full_cq = square(4 * shard)
    full_co = square(5 * shard)
    full_mem = columns(6 * shard, 2)
    full_patch = square(8 * shard, patch_rows)
    at = 8 * shard + patch_rows
    tiny = first[:, at : at + small_count].reshape(parts, -1)
    pieces = []
    at = 0
    for size in small_sizes:
        pieces.append(tiny[:, at : at + size].astype(f32))
        at += size
    full_camera = pieces[0].reshape(parts, 16, -1).transpose(1, 0, 2).reshape(16, -1)
    full_view = pieces[1].reshape(parts, VIEWS, -1).transpose(1, 0, 2).reshape(VIEWS, -1)
    g_mid, b_mid, g_last, b_last, b_down, b_up = (p.reshape(1, -1) for p in pieces[2:])

    own = tokens_all.shape[0] // (grid.seq // 2)
    slots_own = feats_all.shape[0] // (grid.seq // 2)
    x_all = tokens_all.astype(f32)
    x = x_all[:own]
    camera_mine = lax.dynamic_index_in_dim(camera, half, 0, keepdims=False)
    live = lax.dynamic_index_in_dim(patch_count, half, 0, keepdims=False)
    modulation = jnp.sum(camera_mine[:, None] * full_camera, 0)
    scale1, shift1 = 1.0 + modulation[None, :width], modulation[None, width:]
    unit_all, rstd_all = norm_parts(x_all)
    unit1, rstd1 = unit_all[:own], rstd_all[:own]
    hidden_all = low(unit_all * scale1 + shift1)
    hidden = hidden_all[:own]
    query = low(low(dot(hidden, full_q)).astype(f32) * factor)
    kvs = [low(dot(hidden_all, full_kv))]

    hot_all = (views_all[:, None] == jnp.arange(VIEWS)[None, :]).astype(f32)
    view_part = sum(hot_all[:, v : v + 1] * full_view[v : v + 1] for v in range(VIEWS))
    embedded_all = low(dot(feats_all, full_patch) + view_part)
    mems = [low(dot(embedded_all, full_mem))]
    place = grid.place
    chunk = patches.shape[1]
    lane = jnp.arange(chunk)
    slots = jnp.concatenate(
        [
            chunk * (place ^ d ^ far) + lane
            for d in range(grid.seq // 2)
            for far in (0, grid.far)
        ]
    )
    bias = jnp.where(slots < live, 0.0, -1e30).astype(f32).reshape(1, -1)

    attended, lse1 = attend(query, kvs, None)
    second = x + dot(attended, full_out)
    unit2, rstd2 = norm_parts(second)
    normed = low(unit2 * g_mid + b_mid)
    asked = low(low(dot(normed, full_cq)).astype(f32) * factor)
    crossed, lse2 = attend(asked, mems, bias)
    third = second + dot(crossed, full_co)
    core_now = core.reshape(1).astype(jnp.int32)
    result, third_grad, ffn_grads, last_vectors, up_bias_grad = feed_forward(
        third, cot, g_last, b_last, b_down, b_up, packed, shard
    )
    ffn_grad = lax.psum_scatter(ffn_grads, BOTH, scatter_dimension=0, tiled=True)[0].astype(f32)
    tall = down_weight.shape[0]

    def chunks(terms):
        return jnp.split(terms, grid.seq // 2, 0)

    third_low = low(third_grad)
    crossed_grad = low(dot(third_low, full_co, NT))
    asked_grad, mem_terms = attend_back(asked, mems, crossed, crossed_grad, lse2, bias)
    mem_terms = mem_terms[0]
    normed_grad = dot(asked_grad, full_cq, NT)
    second_grad = third_grad + norm_back(unit2, rstd2, normed_grad * g_mid)
    second_low = low(second_grad)
    attended_grad = low(dot(second_low, full_out, NT))
    embedded_grad = low(dot(mem_terms, full_mem, NT))
    arrays = [
        crossed,
        third_low,
        normed,
        asked_grad,
        attended,
        second_low,
        embedded_all,
        mem_terms,
        feats_all,
        embedded_grad,
    ]
    jobs = ((0, 1, 0), (2, 3, 0), (4, 5, 0), (6, 7, 0), (6, 7, 1), (8, 9, 0))
    keep, send = weight_grads(core_now, arrays, jobs, parts, shard, width)
    rest = grid.scatter(keep, send)
    moved = next(rest)
    patch_terms = chunks(low(dot(embedded_grad, full_patch, NT)))
    patch_moved = grid.exchange_core(patch_terms)
    moved, patch_moved = together((moved, patch_moved))
    moved = rest.send(moved)
    moved, attended_grad = together((moved, attended_grad))

    moved = rest.send(moved)
    patch_mine, patch_moved = grid.exchange_line(patch_terms, patch_moved)
    query_grad, pair_terms = attend_back(query, kvs, attended, attended_grad, lse1, None)
    pair_terms = pair_terms[0]
    patch_moved, query_grad, pair_terms = together((patch_moved, query_grad, pair_terms))

    keep, send = weight_grads(
        core_now,
        [hidden, query_grad, hidden_all, pair_terms],
        ((0, 1, 0), (2, 3, 0), (2, 3, 1)),
        parts,
        shard,
        width,
    )
    own_scatter = grid.scatter(keep, send)
    own_moved = next(own_scatter)
    hidden_terms = chunks(low(dot(pair_terms, full_kv, NT)))
    hidden_moved = grid.exchange_core(hidden_terms)
    own_moved, hidden_moved = together((own_moved, hidden_moved))
    own_moved = own_scatter.send(own_moved)
    hidden_mine, hidden_moved = grid.exchange_line(hidden_terms, hidden_moved)
    hidden_query = dot(query_grad, full_q, NT)
    patch_grad = spread(low(patch_mine.astype(f32) + patch_moved.astype(f32)))
    result = spread(result)
    moved, own_moved, hidden_query, hidden_moved, result, patch_grad = together(
        (moved, own_moved, hidden_query, hidden_moved, result, patch_grad)
    )
    own_moved = own_scatter.send(own_moved)
    view_grad = jnp.stack(
        [jnp.sum(hot_all[:, v : v + 1] * embedded_grad.astype(f32), 0) for v in range(VIEWS)]
    )
    hidden_grad = hidden_query + hidden_mine.astype(f32) + hidden_moved.astype(f32)
    token_grad = low(second_grad + norm_back(unit1, rstd1, hidden_grad * scale1))
    token_grad = spread(token_grad)
    modulation_grad = jnp.concatenate(
        [jnp.sum(hidden_grad * unit1, 0), jnp.sum(hidden_grad, 0)]
    )
    camera_grad = camera_mine[:, None] * modulation_grad[None]
    vectors = jnp.concatenate(
        [
            view_grad,
            jnp.sum(normed_grad * unit2, 0)[None],
            jnp.sum(normed_grad, 0)[None],
            last_vectors[0:3],
        ],
        0,
    )
    small_grad = jnp.concatenate(
        [
            low(camera_grad).reshape(16, parts, -1).transpose(1, 0, 2).reshape(parts, -1),
            low(vectors).reshape(VIEWS + 5, parts, -1).transpose(1, 0, 2).reshape(parts, -1),
            low(up_bias_grad).reshape(parts, -1),
        ],
        1,
    )
    small_grad = jnp.pad(small_grad, ((0, 0), (0, small_count * width - small_grad.shape[1])))
    own_moved, small_grad = together((own_moved, small_grad))
    moved = rest.send(moved)
    small_grad = lax.all_to_all(small_grad.reshape(parts, small_count, width), BOTH, 0, 0, tiled=True)
    tiny = jnp.sum(small_grad.astype(f32), 0).reshape(-1)
    own_moved = own_scatter.send(own_moved)
    rest_sum = rest.send(moved)
    self_sum = own_scatter.send(own_moved)
    pieces = []
    at = 0
    for size in small_sizes:
        pieces.append(tiny[at : at + size])
        at += size
    kv_own = join_pairs(unstack_columns(self_sum[shard : 3 * shard], shard))
    return (
        result,
        token_grad,
        patch_grad,
        pieces[0].reshape(camera_weight.shape),
        jnp.concatenate([self_sum[:shard], kv_own], 1),
        rest_sum[2 * shard : 3 * shard],
        pieces[2],
        pieces[3],
        rest_sum[5 * shard : 5 * shard + patch_rows],
        pieces[1].reshape(view_table.shape),
        rest_sum[shard : 2 * shard],
        join_pairs(unstack_columns(rest_sum[3 * shard : 5 * shard], shard)),
        rest_sum[:shard],
        pieces[4],
        pieces[5],
        unstack_columns(ffn_grad[:tall], shard),
        pieces[7],
        ffn_grad[tall:],
        pieces[6],
    )


def solution(mesh):
    line = mesh.shape["seq"] // 2
    mesh = jax.sharding.Mesh(
        mesh.devices.reshape(mesh.shape["obj"], line, 2), ("obj", "ring", "core")
    )
    rows, flat, lanes = P(BOTH, None), P(BOTH), P(None, BOTH)
    sequence = P("obj", SEQ, None)
    in_specs = (
        sequence,
        P("obj", None),
        sequence,
        P("obj"),
        P("obj", SEQ),
        sequence,
        lanes,
        rows,
        rows,
        flat,
        flat,
        rows,
        lanes,
        rows,
        rows,
        rows,
        flat,
        flat,
        rows,
        flat,
        rows,
        flat,
    )
    out_specs = (
        sequence,
        sequence,
        sequence,
        lanes,
        rows,
        rows,
        flat,
        flat,
        rows,
        lanes,
        rows,
        rows,
        rows,
        flat,
        flat,
        rows,
        flat,
        rows,
        flat,
    )
    return jax.shard_map(
        partial(on_device, mesh),
        mesh=mesh,
        in_specs=in_specs,
        out_specs=out_specs,
        check_vma=False,
    )
```

```python
from functools import partial

import jax
import jax.numpy as jnp
from jax import lax
from jax.experimental import pallas as pl
from jax.experimental.pallas import tpu as pltpu
from jax.sharding import PartitionSpec as P

HEAD_DIM = 64
PAIR = 2 * HEAD_DIM
VIEWS = 4
VIEW_PATCHES = 1024
BOTH = ("obj", "ring", "core")
SEQ = ("ring", "core")

epsilon = 1e-05
f32 = jnp.float32
bf16 = jnp.bfloat16
NN = (((1,), (0,)), ((), ()))
NT = (((1,), (1,)), ((), ()))
TN = (((0,), (0,)), ((), ()))


def dot(left, right, dims=NN):
    return lax.dot_general(left, right, dims, preferred_element_type=f32)


def params(megabytes=56):
    return pltpu.CompilerParams(vmem_limit_bytes=megabytes * 2**20)


def norm_parts(values):
    center = values - jnp.mean(values, -1, keepdims=True)
    spread = jnp.mean(center * center, -1, keepdims=True)
    scale = lax.rsqrt(spread + epsilon)
    return center * scale, scale


def norm_back(unit, scale, grad):
    return scale * (
        grad - jnp.mean(grad, -1, keepdims=True) - unit * jnp.mean(grad * unit, -1, keepdims=True)
    )


def attend_kernel(count, masked, *refs):
    q_ref, kv = refs[0], refs[1 : 1 + count]
    bias = refs[1 + count] if masked else None
    o_ref, lse_ref = refs[-2:]
    query = q_ref[...]
    keys = jnp.concatenate([r[:, :PAIR] for r in kv], 0)
    values = jnp.concatenate([r[:, PAIR:] for r in kv], 0)
    low = lax.broadcasted_iota(jnp.int32, query.shape, 1) < HEAD_DIM
    outs, lses = [], []
    for head in range(2):
        mine = low if head == 0 else ~low
        score = dot(jnp.where(mine, query, jnp.zeros_like(query)), keys, NT)
        if masked:
            score = score + bias[...]
        top = jnp.max(score, 1, keepdims=True)
        lifted = jnp.exp(score - top)
        total = jnp.sum(lifted, 1, keepdims=True)
        outs.append(dot(lifted.astype(bf16), values) * (1.0 / total))
        lses.append(top + jnp.log(total))
    o_ref[...] = jnp.where(low, outs[0], outs[1]).astype(bf16)
    lse_ref[...] = jnp.where(low, lses[0], lses[1])[None]


def attend(query, kvs, bias):
    rows, width = query.shape
    count, slots, pairs = len(kvs), kvs[0].shape[0], width // PAIR
    row = pl.BlockSpec((rows, PAIR), lambda i: (0, i))
    slot = pl.BlockSpec((slots, 2 * PAIR), lambda i: (0, i))
    masked = bias is not None
    total = count * slots
    return pl.pallas_call(
        partial(attend_kernel, count, masked),
        grid=(pairs,),
        in_specs=[row] + [slot] * count + [pl.BlockSpec((1, total), lambda i: (0, 0))] * masked,
        out_specs=[row, pl.BlockSpec((1, rows, PAIR), lambda i: (i, 0, 0))],
        out_shape=[
            jax.ShapeDtypeStruct((rows, width), bf16),
            jax.ShapeDtypeStruct((pairs, rows, PAIR), f32),
        ],
        compiler_params=params(),
        name="attend",
        cost_estimate=pl.CostEstimate(flops=1, bytes_accessed=1, transcendentals=0),
    )(query, *kvs, *([bias] if masked else []))


def attend_back_kernel(count, masked, *refs):
    q_ref, kv = refs[0], refs[1 : 1 + count]
    o_ref, do_ref, lse_ref = refs[1 + count : 4 + count]
    bias = refs[4 + count] if masked else None
    dq_ref, dkv = refs[-1 - count], refs[-count:]
    query, grad = q_ref[...], do_ref[...]
    slots = kv[0].shape[0]
    keys = jnp.concatenate([r[:, :PAIR] for r in kv], 0)
    values = jnp.concatenate([r[:, PAIR:] for r in kv], 0)
    low = lax.broadcasted_iota(jnp.int32, query.shape, 1) < HEAD_DIM
    lse = lse_ref[0]
    product = o_ref[...].astype(f32) * grad.astype(f32)
    dk = dv = 0.0
    dqs = []
    for head in range(2):
        mine = low if head == 0 else ~low
        head_query = jnp.where(mine, query, jnp.zeros_like(query))
        head_grad = jnp.where(mine, grad, jnp.zeros_like(grad))
        score = dot(head_query, keys, NT)
        if masked:
            score = score + bias[...]
        probs = jnp.exp(score - lse[:, HEAD_DIM * head : HEAD_DIM * head + 1])
        delta = jnp.sum(jnp.where(mine, product, 0.0), 1, keepdims=True)
        score_grad = (probs * (dot(head_grad, values, NT) - delta)).astype(bf16)
        dk = dk + dot(jnp.transpose(head_query), score_grad)
        dv = dv + dot(jnp.transpose(head_grad), probs.astype(bf16))
        dqs.append(dot(score_grad, keys))
    dq_ref[...] = (jnp.where(low, dqs[0], dqs[1]) * HEAD_DIM**-0.5).astype(bf16)
    dk, dv = jnp.transpose(dk), jnp.transpose(dv)
    for j in range(count):
        dkv[j][:, :PAIR] = dk[j * slots : (j + 1) * slots].astype(bf16)
        dkv[j][:, PAIR:] = dv[j * slots : (j + 1) * slots].astype(bf16)


def attend_back(query, kvs, out, grad, lse, bias):
    rows, width = query.shape
    count, slots, pairs = len(kvs), kvs[0].shape[0], width // PAIR
    row = pl.BlockSpec((rows, PAIR), lambda i: (0, i))
    slot = pl.BlockSpec((slots, 2 * PAIR), lambda i: (0, i))
    masked = bias is not None
    total = count * slots
    result = pl.pallas_call(
        partial(attend_back_kernel, count, masked),
        grid=(pairs,),
        in_specs=[row]
        + [slot] * count
        + [row, row, pl.BlockSpec((1, rows, PAIR), lambda i: (i, 0, 0))]
        + [pl.BlockSpec((1, total), lambda i: (0, 0))] * masked,
        out_specs=[row] + [slot] * count,
        out_shape=[jax.ShapeDtypeStruct((rows, width), bf16)]
        + [jax.ShapeDtypeStruct((slots, 2 * width), bf16)] * count,
        compiler_params=params(),
        name="attend_back",
        cost_estimate=pl.CostEstimate(flops=1, bytes_accessed=1, transcendentals=0),
    )(query, *kvs, out, grad, lse, *([bias] if masked else []))
    return result[0], result[1:]


def block_kernel(core_ref, third_ref, cot_ref, gain_ref, shift_ref, dbias_ref, ubias_ref, up_ref, down_ref,
                 result_ref, tgrad_ref, keep_ref, send_ref, vec_ref, ubgrad_ref,
                 unit_s, final_s, final_t, out_s, fgrad_s, scale_s, wide_s, tall_s, sems):
    step = pl.program_id(0)
    last = pl.num_programs(0) - 1
    slot = lax.rem(step, 2)
    core = core_ref[0]
    _, _, half, shard, tile = wide_s.shape
    _, _, few, tall, width = tall_s.shape
    per = width // tile

    def copies(at, place):
        row = pl.multiple_of((at // per) * shard, shard)
        lane = pl.multiple_of(lax.rem(at, per) * tile, tile)
        found = []
        for which, ref in enumerate((keep_ref, send_ref)):
            found += [
                pltpu.make_async_copy(
                    wide_s.at[place, which],
                    ref.at[:, pl.ds(row, shard), pl.ds(lane, tile)],
                    sems.at[which, place],
                ),
                pltpu.make_async_copy(
                    tall_s.at[place, which],
                    ref.at[pl.ds(at * few, few), pl.ds(tall, tall), :],
                    sems.at[2 + which, place],
                ),
            ]
        return found

    @pl.when(step == 0)
    def _():
        unit, scale = norm_parts(third_ref[...])
        unit_s[...] = unit
        scale_s[...] = scale
        final = (unit * gain_ref[...] + shift_ref[...]).astype(bf16)
        final_s[...] = final
        final_t[...] = jnp.transpose(final)
        out_s[...] = jnp.zeros_like(out_s)
        fgrad_s[...] = jnp.zeros_like(fgrad_s)

    @pl.when(step >= 2)
    def _():
        for copy in copies(step - 2, slot):
            copy.wait()

    cot = cot_ref[...]
    up = up_ref[...].reshape(-1, up_ref.shape[-1])
    down = down_ref[...].reshape(-1, down_ref.shape[-1])
    upper = dot(final_s[...], up) + ubias_ref[...]
    cdf = 0.5 * (1.0 + lax.erf(upper * (0.5**0.5)))
    active = (upper * cdf).astype(bf16)
    slope = cdf + upper * (jnp.exp(-0.5 * upper * upper) * 0.3989422804014327)
    ugrad = (slope * dot(cot, down, NT)).astype(bf16)
    out_s[...] += dot(active, down)
    fgrad_s[...] += dot(ugrad, up, NT)
    ubgrad_ref[...] = jnp.sum(ugrad.astype(f32), 0, keepdims=True)
    wide = dot(final_t[...], ugrad).astype(bf16).reshape(half, 2, shard, tile)
    wide_s[slot, core] = wide[:, 0]
    wide_s[slot, 1 - core] = wide[:, 1]
    slim = dot(jnp.transpose(active), cot).astype(bf16).reshape(few, 2, tall, width)
    tall_s[slot, core] = slim[:, 0]
    tall_s[slot, 1 - core] = slim[:, 1]
    for copy in copies(step, slot):
        copy.start()

    @pl.when(step == last)
    def _():
        result_ref[...] = (third_ref[...] + (out_s[...] + dbias_ref[...])).astype(bf16)
        unit, fgrad, cotf = unit_s[...], fgrad_s[...], cot.astype(f32)
        tgrad_ref[...] = cotf + norm_back(unit, scale_s[...], fgrad * gain_ref[...])
        vec_ref[...] = jnp.zeros_like(vec_ref)
        vec_ref[0:1, :] = jnp.sum(fgrad * unit, 0, keepdims=True)
        vec_ref[1:2, :] = jnp.sum(fgrad, 0, keepdims=True)
        vec_ref[2:3, :] = jnp.sum(cotf, 0, keepdims=True)
        for copy in copies(step - 1, 1 - slot) + copies(step, slot):
            copy.wait()


def feed_forward(core, third, cot, gain, shift, down_bias, up_bias, packed, shard):
    rows, width = third.shape
    parts = packed.shape[0]
    hidden = up_bias.shape[1]
    tile = 512
    per = width // tile
    tall = hidden // parts
    spread = tile // tall
    steps = hidden // tile
    whole = lambda shape: pl.BlockSpec(shape, lambda j, c: (0,) * len(shape))
    return pl.pallas_call(
        block_kernel,
        grid_spec=pltpu.PrefetchScalarGridSpec(
            num_scalar_prefetch=1,
            grid=(steps,),
            in_specs=[
                whole((rows, width)),
                whole((rows, width)),
                whole((1, width)),
                whole((1, width)),
                whole((1, width)),
                pl.BlockSpec((1, tile), lambda j, c: (0, j)),
                pl.BlockSpec((parts, shard, tile), lambda j, c: (0, j // per, j % per)),
                pl.BlockSpec((spread, tall, width), lambda j, c: (j, 1, 0)),
            ],
            out_specs=[
                whole((rows, width)),
                whole((rows, width)),
                pl.BlockSpec(memory_space=pl.ANY),
                pl.BlockSpec(memory_space=pl.ANY),
                whole((8, width)),
                pl.BlockSpec((1, tile), lambda j, c: (0, j)),
            ],
            scratch_shapes=[
                pltpu.VMEM((rows, width), f32),
                pltpu.VMEM((rows, width), bf16),
                pltpu.VMEM((width, rows), bf16),
                pltpu.VMEM((rows, width), f32),
                pltpu.VMEM((rows, width), f32),
                pltpu.VMEM((rows, 1), f32),
                pltpu.VMEM((2, 2, parts // 2, shard, tile), bf16),
                pltpu.VMEM((2, 2, spread // 2, tall, width), bf16),
                pltpu.SemaphoreType.DMA((4, 2)),
            ],
        ),
        out_shape=[
            jax.ShapeDtypeStruct((rows, width), bf16),
            jax.ShapeDtypeStruct((rows, width), f32),
            jax.ShapeDtypeStruct((parts // 2, 2 * tall, width), bf16),
            jax.ShapeDtypeStruct((parts // 2, 2 * tall, width), bf16),
            jax.ShapeDtypeStruct((8, width), f32),
            jax.ShapeDtypeStruct((1, hidden), f32),
        ],
        compiler_params=params(),
        name="feed_forward",
        cost_estimate=pl.CostEstimate(flops=1, bytes_accessed=1, transcendentals=0),
    )(core, third, cot, gain, shift, down_bias, up_bias, packed, packed)


def grads_kernel(jobs, core_ref, *refs):
    ins, (keep_ref, send_ref) = refs[:-2], refs[-2:]
    step = pl.program_id(0)
    half, room, width = keep_ref.shape

    def store(block, rows):
        block = block.astype(bf16).reshape(half, 2, rows, width)
        keep_ref[:, :rows] = block[:, 0]
        send_ref[:, :rows] = block[:, 1]

    def swapped(block, rows):
        block = block.astype(bf16).reshape(half, 2, rows, width)
        keep_ref[:, :rows] = block[:, 1]
        send_ref[:, :rows] = block[:, 0]

    for at, (left, right, column) in enumerate(jobs):

        @pl.when(step == at)
        def _():
            rows = ins[left].shape[1] // (2 * half)
            if rows < room:
                keep_ref[...] = jnp.zeros_like(keep_ref)
                send_ref[...] = jnp.zeros_like(send_ref)
            block = dot(ins[left][...], ins[right][:, column * width : (column + 1) * width], TN)

            @pl.when(core_ref[0] == 0)
            def _():
                store(block, rows)

            @pl.when(core_ref[0] == 1)
            def _():
                swapped(block, rows)


def weight_grads(core, arrays, jobs, parts, shard, width):
    count = len(jobs)
    whole = lambda array: pl.BlockSpec(array.shape, lambda j, c: (0, 0))
    out = pl.BlockSpec((parts // 2, shard, width), lambda j, c: (0, j, 0))
    flops = sum(2 * arrays[i].shape[0] * arrays[i].shape[1] * width for i, _, _ in jobs)
    return pl.pallas_call(
        partial(grads_kernel, jobs),
        grid_spec=pltpu.PrefetchScalarGridSpec(
            num_scalar_prefetch=1,
            grid=(count,),
            in_specs=[whole(array) for array in arrays],
            out_specs=[out, out],
        ),
        out_shape=[jax.ShapeDtypeStruct((parts // 2, count * shard, width), bf16)] * 2,
        compiler_params=params(),
        name="weight_grads",
        cost_estimate=pl.CostEstimate(flops=1, bytes_accessed=1, transcendentals=0),
    )(core, *arrays)


class Grid:
    def __init__(self, mesh):
        self.obj, self.seq = mesh.shape["obj"], mesh.shape["ring"] * 2
        self.all = self.obj * self.seq
        self.place = lax.axis_index("ring") * 2 + lax.axis_index("core")
        self.me = lax.axis_index("obj") * self.seq + self.place
        self.group = [m for m in (1 << k for k in range(20)) if m < self.seq // 2]
        self.far = self.seq // 2

    def swap(self, value, mask):
        return lax.ppermute(value, BOTH, [(i, i ^ mask) for i in range(self.all)])

    def bit(self, mask):
        return (self.me // mask) % 2

    def gather_group(self, value):
        found = {0: value}
        for mask in self.group[1:][::-1] + self.group[:1]:
            found.update({d ^ mask: self.swap(v, mask) for d, v in list(found.items())})
        return [found[d] for d in range(self.seq // 2)]

    def sum_group(self, terms):
        terms = {d: [t] for d, t in enumerate(terms)}
        for mask in self.group[:1] + self.group[1:]:
            for d in [d for d in terms if d & mask]:
                moved = self.swap(add(terms.pop(d)), mask)
                terms[d ^ mask].append(moved)
        return add(terms[0])

    def scatter(self, keep, send):
        moved = yield self.swap(send, 1)
        total = add([keep, moved]).reshape(self.obj, self.seq // 2, *keep.shape[1:])
        total = yield total
        total = yield lax.psum_scatter(total, "obj", scatter_dimension=0, tiled=False)
        terms = [total]
        for mask in self.group[1:] + [self.far]:
            terms = [t.reshape(t.shape[0] // 2, 2, *t.shape[1:]) for t in terms]
            pick = lambda t, which: lax.dynamic_index_in_dim(t, which, 1, keepdims=False)
            moved = self.swap(add([pick(t, 1 - self.bit(mask)) for t in terms]), mask)
            if 4 * mask >= self.seq:
                moved = yield moved
            terms = [pick(t, self.bit(mask)) for t in terms] + [moved]
        yield sum(t[0].astype(f32) for t in terms)

    def exchange_core(self, terms):
        return [self.swap(t, 1) for t in terms[1::2]]

    def exchange_line(self, terms, moved):
        pairs = [add([t, m]) for t, m in zip(terms[::2], moved)]
        step = len(pairs) // 2
        while step > 1:
            pairs = [add([pairs[k], self.swap(pairs[k + step], 2 * step)]) for k in range(step)]
            step //= 2
        return pairs[0], self.swap(pairs[1], 2)


together = lax.optimization_barrier


def add(terms):
    if len(terms) == 1:
        return terms[0]
    return sum(t.astype(f32) for t in terms).astype(bf16)


def split_pairs(matrix):
    rows, width = matrix.shape
    return matrix.reshape(rows, 2, width // (2 * PAIR), PAIR).transpose(0, 2, 1, 3).reshape(rows, width)


def join_pairs(matrix):
    rows, width = matrix.shape
    return matrix.reshape(rows, width // (2 * PAIR), 2, PAIR).transpose(0, 2, 1, 3).reshape(rows, width)


def stack_columns(matrix, width):
    rows = matrix.shape[0]
    return matrix.reshape(rows, -1, width).transpose(1, 0, 2).reshape(-1, width)


def unstack_columns(matrix, rows):
    width = matrix.shape[1]
    return matrix.reshape(-1, rows, width).transpose(1, 0, 2).reshape(rows, -1)


def pad_rows(matrix, rows):
    return jnp.pad(matrix, ((0, rows - matrix.shape[0]), (0, 0)))


def on_device(
    mesh,
    tokens,
    camera,
    patches,
    patch_count,
    patch_index,
    cotangent,
    camera_weight,
    self_weight,
    self_output,
    mid_gain,
    mid_bias,
    patch_weight,
    view_table,
    cross_query,
    cross_memory,
    cross_output,
    last_gain,
    last_bias,
    up_weight,
    up_bias,
    down_weight,
    down_bias,
):
    grid = Grid(mesh)
    parts = grid.all
    width = self_output.shape[1]
    low = lambda v: v.astype(bf16)
    factor = HEAD_DIM**-0.5
    core = grid.bit(1)
    half = grid.bit(grid.far)

    def compact(value):
        mine = lax.dynamic_index_in_dim(value, half, 0, keepdims=False)
        other = lax.dynamic_index_in_dim(value, 1 - half, 0, keepdims=False)
        return jnp.concatenate([mine, grid.swap(other, grid.far)], 0)

    def spread(mine, other):
        mine = mine[: other.shape[0]]
        return jnp.where(half == 0, jnp.stack([mine, other]), jnp.stack([other, mine]))

    shard = self_output.shape[0]
    self_mixed = jnp.concatenate(
        [low(self_weight[:, :width]), split_pairs(low(self_weight[:, width:]))], 1
    )
    small = jnp.concatenate(
        [
            low(camera_weight).reshape(-1),
            low(view_table).reshape(-1),
            low(mid_gain),
            low(mid_bias),
            low(last_gain),
            low(last_bias),
            low(down_bias),
            low(up_bias),
        ]
    )
    small_sizes = [
        camera_weight.size,
        view_table.size,
        shard,
        shard,
        shard,
        shard,
        shard,
        up_bias.size,
    ]
    patch_rows = patch_weight.shape[0]
    small_count = -(-small.size // width)
    patch_room = -(-(patch_rows + small_count) // shard) * shard
    small_rows = jnp.pad(small, (0, small_count * width - small.size)).reshape(-1, width)
    first = jnp.concatenate(
        [
            stack_columns(self_mixed, width),
            low(self_output),
            low(cross_query),
            low(cross_output),
            stack_columns(split_pairs(low(cross_memory)), width),
            pad_rows(jnp.concatenate([low(patch_weight), small_rows], 0), patch_room),
        ],
        0,
    )
    tokens_all = jnp.concatenate(grid.gather_group(compact(tokens)), 0)
    feats_all = jnp.concatenate(grid.gather_group(compact(patches)), 0)
    views_all = jnp.concatenate(grid.gather_group(compact(patch_index)), 0) // VIEW_PATCHES
    first = lax.all_gather(first, BOTH, axis=0, tiled=False)
    ffn_mine = jnp.concatenate([stack_columns(low(up_weight), width), low(down_weight)], 0)
    first, ffn_mine, tokens_all, feats_all, views_all = together(
        (first, ffn_mine, tokens_all, feats_all, views_all)
    )
    packed = lax.all_gather(ffn_mine, BOTH, axis=0, tiled=False)

    def square(start, rows=shard):
        return first[:, start : start + rows].reshape(parts * rows, width)

    def columns(start, count):
        return jnp.concatenate([square(start + q * shard) for q in range(count)], 1)

    full_q = square(0)
    full_kv = columns(shard, 2)
    full_out = square(3 * shard)
    full_cq = square(4 * shard)
    full_co = square(5 * shard)
    full_mem = columns(6 * shard, 2)
    full_patch = square(8 * shard, patch_rows)
    at = 8 * shard + patch_rows
    tiny = first[:, at : at + small_count].reshape(parts, -1)
    pieces = []
    at = 0
    for size in small_sizes:
        pieces.append(tiny[:, at : at + size].astype(f32))
        at += size
    full_camera = pieces[0].reshape(parts, 16, -1).transpose(1, 0, 2).reshape(16, -1)
    full_view = pieces[1].reshape(parts, VIEWS, -1).transpose(1, 0, 2).reshape(VIEWS, -1)
    g_mid, b_mid, g_last, b_last, b_down, b_up = (p.reshape(1, -1) for p in pieces[2:])

    own = tokens_all.shape[0] // (grid.seq // 2)
    slots_own = feats_all.shape[0] // (grid.seq // 2)
    x_all = tokens_all.astype(f32)
    x = x_all[:own]
    camera_mine = lax.dynamic_index_in_dim(camera, half, 0, keepdims=False)
    live = lax.dynamic_index_in_dim(patch_count, half, 0, keepdims=False)
    modulation = jnp.sum(camera_mine[:, None] * full_camera, 0)
    scale1, shift1 = 1.0 + modulation[None, :width], modulation[None, width:]
    unit_all, rstd_all = norm_parts(x_all)
    unit1, rstd1 = unit_all[:own], rstd_all[:own]
    hidden_all = low(unit_all * scale1 + shift1)
    hidden = hidden_all[:own]
    query = low(low(dot(hidden, full_q)).astype(f32) * factor)
    kvs = [low(dot(hidden_all, full_kv))]

    hot_all = (views_all[:, None] == jnp.arange(VIEWS)[None, :]).astype(f32)
    view_part = sum(hot_all[:, v : v + 1] * full_view[v : v + 1] for v in range(VIEWS))
    embedded_all = low(dot(feats_all, full_patch) + view_part)
    mems = [low(dot(embedded_all, full_mem))]
    place = grid.place
    chunk = patches.shape[1]
    lane = jnp.arange(chunk)
    slots = jnp.concatenate(
        [
            chunk * (place ^ d ^ far) + lane
            for d in range(grid.seq // 2)
            for far in (0, grid.far)
        ]
    )
    bias = jnp.where(slots < live, 0.0, -1e30).astype(f32).reshape(1, -1)

    query, kvs, mems, cotangent = together((query, kvs, mems, cotangent))
    cot = compact(cotangent)
    attended, lse1 = attend(query, kvs, None)
    second = x + dot(attended, full_out)
    unit2, rstd2 = norm_parts(second)
    normed = low(unit2 * g_mid + b_mid)
    asked = low(low(dot(normed, full_cq)).astype(f32) * factor)
    crossed, lse2 = attend(asked, mems, bias)
    third = second + dot(crossed, full_co)
    third, cot = together((third, cot))
    core_now = core.reshape(1).astype(jnp.int32)
    result, third_grad, ffn_keep, ffn_send, last_vectors, up_bias_grad = feed_forward(
        core_now, third, cot, g_last, b_last, b_down, b_up, packed, shard
    )
    tall = down_weight.shape[0]

    def chunks(terms):
        return jnp.split(terms, grid.seq // 2, 0)

    ffn = grid.scatter(ffn_keep, ffn_send)
    ffn_moved = next(ffn)
    half_rows = result.shape[0] // 2
    third_low = low(third_grad)
    crossed_grad = low(dot(third_low, full_co, NT))
    ffn_moved, crossed_grad = together((ffn_moved, crossed_grad))
    ffn_moved = ffn.send(ffn_moved)
    ffn_moved, crossed_grad = together((ffn_moved, crossed_grad))

    ffn_moved = ffn.send(ffn_moved)
    result_moved = grid.swap(result[half_rows:], grid.far)
    asked_grad, mem_terms = attend_back(asked, mems, crossed, crossed_grad, lse2, bias)
    mem_terms = mem_terms[0]
    normed_grad = dot(asked_grad, full_cq, NT)
    second_grad = third_grad + norm_back(unit2, rstd2, normed_grad * g_mid)
    second_low = low(second_grad)
    attended_grad = low(dot(second_low, full_out, NT))
    embedded_grad = low(dot(mem_terms, full_mem, NT))
    arrays = [
        crossed,
        third_low,
        normed,
        asked_grad,
        attended,
        second_low,
        embedded_all,
        mem_terms,
        feats_all,
        embedded_grad,
    ]
    jobs = ((0, 1, 0), (2, 3, 0), (4, 5, 0), (6, 7, 0), (6, 7, 1), (8, 9, 0))
    keep, send = weight_grads(core_now, arrays, jobs, parts, shard, width)
    rest = grid.scatter(keep, send)
    moved = next(rest)
    patch_terms = chunks(low(dot(embedded_grad, full_patch, NT)))
    attended_grad, patch_terms, moved = together((attended_grad, patch_terms, moved))
    moved = rest.send(moved)
    patch_moved = grid.exchange_core(patch_terms)
    attended_grad, patch_moved, moved = together((attended_grad, patch_moved, moved))

    moved = rest.send(moved)
    patch_mine, patch_moved = grid.exchange_line(patch_terms, patch_moved)
    query_grad, pair_terms = attend_back(query, kvs, attended, attended_grad, lse1, None)
    pair_terms = pair_terms[0]
    ffn_moved, result_moved, patch_moved, query_grad, pair_terms = together(
        (ffn_moved, result_moved, patch_moved, query_grad, pair_terms)
    )

    ffn_moved = ffn.send(ffn_moved)
    hidden_terms = chunks(low(dot(pair_terms, full_kv, NT)))
    hidden_terms, pair_terms, query_grad = together((hidden_terms, pair_terms, query_grad))
    hidden_moved = grid.exchange_core(hidden_terms)
    keep, send = weight_grads(
        core_now,
        [hidden, query_grad, hidden_all, pair_terms],
        ((0, 1, 0), (2, 3, 0), (2, 3, 1)),
        parts,
        shard,
        width,
    )
    keep, send, hidden_moved, ffn_moved = together((keep, send, hidden_moved, ffn_moved))

    own_scatter = grid.scatter(keep, send)
    own_moved = next(own_scatter)
    hidden_mine, hidden_moved = grid.exchange_line(hidden_terms, hidden_moved)
    patch_low = low(patch_mine.astype(f32) + patch_moved.astype(f32))
    patch_half = patch_low.shape[0] // 2
    view_grad = jnp.stack(
        [jnp.sum(hot_all[:, v : v + 1] * embedded_grad.astype(f32), 0) for v in range(VIEWS)]
    )
    own_moved, patch_low, view_grad = together((own_moved, patch_low, view_grad))
    own_moved = own_scatter.send(own_moved)
    own_moved, hidden_moved, moved = together((own_moved, hidden_moved, moved))

    own_moved = own_scatter.send(own_moved)
    ffn_moved = ffn.send(ffn_moved)
    moved = rest.send(moved)
    hidden_query = dot(query_grad, full_q, NT)
    hidden_grad = hidden_query + hidden_mine.astype(f32) + hidden_moved.astype(f32)
    token_grad = low(second_grad + norm_back(unit1, rstd1, hidden_grad * scale1))
    token_grad, hidden_grad = together((token_grad, hidden_grad))
    token_moved = grid.swap(token_grad[half_rows:], grid.far)
    result = spread(result, result_moved)
    modulation_grad = jnp.concatenate(
        [jnp.sum(hidden_grad * unit1, 0), jnp.sum(hidden_grad, 0)]
    )
    camera_grad = camera_mine[:, None] * modulation_grad[None]
    vectors = jnp.concatenate(
        [
            view_grad,
            jnp.sum(normed_grad * unit2, 0)[None],
            jnp.sum(normed_grad, 0)[None],
            last_vectors[0:3],
        ],
        0,
    )
    small_grad = jnp.concatenate(
        [
            low(camera_grad).reshape(16, parts, -1).transpose(1, 0, 2).reshape(parts, -1),
            low(vectors).reshape(VIEWS + 5, parts, -1).transpose(1, 0, 2).reshape(parts, -1),
            low(up_bias_grad).reshape(parts, -1),
        ],
        1,
    )
    small_grad = jnp.pad(small_grad, ((0, 0), (0, small_count * width - small_grad.shape[1])))
    moved, small_grad, token_moved, ffn_moved, result = together(
        (moved, small_grad, token_moved, ffn_moved, result)
    )
    moved = rest.send(moved)
    small_grad = lax.all_to_all(small_grad.reshape(parts, small_count, width), BOTH, 0, 0, tiled=True)
    patch_moved = grid.swap(patch_low[patch_half:], grid.far)
    tiny = jnp.sum(small_grad.astype(f32), 0).reshape(-1)
    token_grad = spread(token_grad, token_moved)
    ffn_grad = ffn.send(ffn_moved)
    ffn_up, ffn_down = unstack_columns(ffn_grad[:tall], shard), ffn_grad[tall:]
    own_moved, moved, token_grad, patch_moved, tiny, ffn_up, ffn_down = together(
        (own_moved, moved, token_grad, patch_moved, tiny, ffn_up, ffn_down)
    )
    own_moved = own_scatter.send(own_moved)
    patch_grad = spread(patch_low, patch_moved)
    own_moved = own_scatter.send(own_moved)
    rest_sum = rest.send(moved)
    self_sum = own_scatter.send(own_moved)
    pieces = []
    at = 0
    for size in small_sizes:
        pieces.append(tiny[at : at + size])
        at += size
    kv_own = join_pairs(unstack_columns(self_sum[shard : 3 * shard], shard))
    return (
        result,
        token_grad,
        patch_grad,
        pieces[0].reshape(camera_weight.shape),
        jnp.concatenate([self_sum[:shard], kv_own], 1),
        rest_sum[2 * shard : 3 * shard],
        pieces[2],
        pieces[3],
        rest_sum[5 * shard : 5 * shard + patch_rows],
        pieces[1].reshape(view_table.shape),
        rest_sum[shard : 2 * shard],
        join_pairs(unstack_columns(rest_sum[3 * shard : 5 * shard], shard)),
        rest_sum[:shard],
        pieces[4],
        pieces[5],
        ffn_up,
        pieces[7],
        ffn_down,
        pieces[6],
    )


def solution(mesh):
    line = mesh.shape["seq"] // 2
    mesh = jax.sharding.Mesh(
        mesh.devices.reshape(mesh.shape["obj"], line, 2), ("obj", "ring", "core")
    )
    rows, flat, lanes = P(BOTH, None), P(BOTH), P(None, BOTH)
    sequence = P("obj", SEQ, None)
    in_specs = (
        sequence,
        P("obj", None),
        sequence,
        P("obj"),
        P("obj", SEQ),
        sequence,
        lanes,
        rows,
        rows,
        flat,
        flat,
        rows,
        lanes,
        rows,
        rows,
        rows,
        flat,
        flat,
        rows,
        flat,
        rows,
        flat,
    )
    out_specs = (
        sequence,
        sequence,
        sequence,
        lanes,
        rows,
        rows,
        flat,
        flat,
        rows,
        lanes,
        rows,
        rows,
        rows,
        flat,
        flat,
        rows,
        flat,
        rows,
        flat,
    )
    return jax.shard_map(
        partial(on_device, mesh),
        mesh=mesh,
        in_specs=in_specs,
        out_specs=out_specs,
        check_vma=False,
    )
```

```python
from functools import partial

import jax
import jax.numpy as jnp
from jax import lax
from jax.experimental import pallas as pl
from jax.experimental.pallas import tpu as pltpu
from jax.sharding import PartitionSpec as P

HEAD_DIM = 64
PAIR = 2 * HEAD_DIM
VIEWS = 4
VIEW_PATCHES = 1024
BOTH = ("obj", "ring", "core")
SEQ = ("ring", "core")

epsilon = 1e-05
f32 = jnp.float32
bf16 = jnp.bfloat16
NN = (((1,), (0,)), ((), ()))
NT = (((1,), (1,)), ((), ()))
TN = (((0,), (0,)), ((), ()))


def dot(left, right, dims=NN):
    return lax.dot_general(left, right, dims, preferred_element_type=f32)


def params(megabytes=56):
    return pltpu.CompilerParams(vmem_limit_bytes=megabytes * 2**20)


def norm_parts(values):
    center = values - jnp.mean(values, -1, keepdims=True)
    spread = jnp.mean(center * center, -1, keepdims=True)
    scale = lax.rsqrt(spread + epsilon)
    return center * scale, scale


def norm_back(unit, scale, grad):
    return scale * (
        grad - jnp.mean(grad, -1, keepdims=True) - unit * jnp.mean(grad * unit, -1, keepdims=True)
    )


def attend_kernel(masked, *refs):
    q_ref, kv_ref = refs[:2]
    bias = refs[2] if masked else None
    o_ref, lse_ref = refs[-2:]
    query = q_ref[...]
    keys, values = kv_ref[:, :PAIR], kv_ref[:, PAIR:]
    low = lax.broadcasted_iota(jnp.int32, query.shape, 1) < HEAD_DIM
    outs, lses = [], []
    for head in range(2):
        mine = low if head == 0 else ~low
        score = dot(jnp.where(mine, query, jnp.zeros_like(query)), keys, NT)
        if masked:
            score = score + bias[...]
        top = jnp.max(score, 1, keepdims=True)
        lifted = jnp.exp(score - top)
        total = jnp.sum(lifted, 1, keepdims=True)
        outs.append(dot(lifted.astype(bf16), values) * (1.0 / total))
        lses.append(top + jnp.log(total))
    o_ref[...] = jnp.where(low, outs[0], outs[1]).astype(bf16)
    lse_ref[...] = jnp.where(low, lses[0], lses[1])[None]


def attend(query, kv, bias):
    rows, width = query.shape
    slots, pairs = kv.shape[0], width // PAIR
    tile = min(rows, 384)
    row = pl.BlockSpec((tile, PAIR), lambda i, r: (r, i))
    masked = bias is not None
    return pl.pallas_call(
        partial(attend_kernel, masked),
        grid=(pairs, rows // tile),
        in_specs=[row, pl.BlockSpec((slots, 2 * PAIR), lambda i, r: (0, i))]
        + [pl.BlockSpec((1, slots), lambda i, r: (0, 0))] * masked,
        out_specs=[row, pl.BlockSpec((1, tile, PAIR), lambda i, r: (i, r, 0))],
        out_shape=[
            jax.ShapeDtypeStruct((rows, width), bf16),
            jax.ShapeDtypeStruct((pairs, rows, PAIR), f32),
        ],
        compiler_params=params(),
        name="attend",
        cost_estimate=pl.CostEstimate(
            flops=16 * rows * slots * width,
            bytes_accessed=4 * width * (rows + slots),
            transcendentals=2 * pairs * rows * slots,
        ),
    )(query, kv, *([bias] if masked else []))


def attend_back_kernel(masked, *refs):
    q_ref, kv_ref, o_ref, do_ref, lse_ref = refs[:5]
    bias = refs[5] if masked else None
    dq_ref, dkv_ref, dk_s, dv_s = refs[-4:]
    query, grad = q_ref[...], do_ref[...]
    keys, values = kv_ref[:, :PAIR], kv_ref[:, PAIR:]
    low = lax.broadcasted_iota(jnp.int32, query.shape, 1) < HEAD_DIM
    lse = lse_ref[0]
    product = o_ref[...].astype(f32) * grad.astype(f32)
    dk = dv = 0.0
    dqs = []
    for head in range(2):
        mine = low if head == 0 else ~low
        head_query = jnp.where(mine, query, jnp.zeros_like(query))
        head_grad = jnp.where(mine, grad, jnp.zeros_like(grad))
        score = dot(head_query, keys, NT)
        if masked:
            score = score + bias[...]
        probs = jnp.exp(score - lse[:, HEAD_DIM * head : HEAD_DIM * head + 1])
        delta = jnp.sum(jnp.where(mine, product, 0.0), 1, keepdims=True)
        score_grad = (probs * (dot(head_grad, values, NT) - delta)).astype(bf16)
        dk = dk + dot(jnp.transpose(head_query), score_grad)
        dv = dv + dot(jnp.transpose(head_grad), probs.astype(bf16))
        dqs.append(dot(score_grad, keys))
    dq_ref[...] = (jnp.where(low, dqs[0], dqs[1]) * HEAD_DIM**-0.5).astype(bf16)
    step = pl.program_id(1)

    @pl.when(step == 0)
    def _():
        dk_s[...] = dk
        dv_s[...] = dv

    @pl.when(step > 0)
    def _():
        dk_s[...] += dk
        dv_s[...] += dv

    @pl.when(step == pl.num_programs(1) - 1)
    def _():
        dkv_ref[:, :PAIR] = jnp.transpose(dk_s[...]).astype(bf16)
        dkv_ref[:, PAIR:] = jnp.transpose(dv_s[...]).astype(bf16)


def attend_back(query, kv, out, grad, lse, bias):
    rows, width = query.shape
    slots, pairs = kv.shape[0], width // PAIR
    tile = min(rows, 384)
    row = pl.BlockSpec((tile, PAIR), lambda i, r: (r, i))
    slot = pl.BlockSpec((slots, 2 * PAIR), lambda i, r: (0, i))
    masked = bias is not None
    return pl.pallas_call(
        partial(attend_back_kernel, masked),
        grid=(pairs, rows // tile),
        in_specs=[row, slot, row, row, pl.BlockSpec((1, tile, PAIR), lambda i, r: (i, r, 0))]
        + [pl.BlockSpec((1, slots), lambda i, r: (0, 0))] * masked,
        out_specs=[row, slot],
        out_shape=[
            jax.ShapeDtypeStruct((rows, width), bf16),
            jax.ShapeDtypeStruct((slots, 2 * width), bf16),
        ],
        scratch_shapes=[pltpu.VMEM((PAIR, slots), f32)] * 2,
        compiler_params=params(),
        name="attend_back",
        cost_estimate=pl.CostEstimate(
            flops=40 * rows * slots * width,
            bytes_accessed=8 * width * (rows + slots),
            transcendentals=2 * pairs * rows * slots,
        ),
    )(query, kv, out, grad, lse, *([bias] if masked else []))


def block_kernel(core_ref, third_ref, cot_ref, gain_ref, shift_ref, dbias_ref, ubias_ref, up_ref, down_ref,
                 result_ref, tgrad_ref, keep_ref, send_ref, vec_ref, ubgrad_ref,
                 unit_s, final_s, final_t, out_s, fgrad_s, scale_s, wide_s, tall_s, sems):
    step = pl.program_id(0)
    last = pl.num_programs(0) - 1
    slot = lax.rem(step, 2)
    core = core_ref[0]
    _, _, half, shard, tile = wide_s.shape
    _, _, few, tall, width = tall_s.shape
    per = width // tile

    def copies(at, place):
        row = pl.multiple_of((at // per) * shard, shard)
        lane = pl.multiple_of(lax.rem(at, per) * tile, tile)
        found = []
        for which, ref in enumerate((keep_ref, send_ref)):
            found += [
                pltpu.make_async_copy(
                    wide_s.at[place, which],
                    ref.at[:, pl.ds(row, shard), pl.ds(lane, tile)],
                    sems.at[which, place],
                ),
                pltpu.make_async_copy(
                    tall_s.at[place, which],
                    ref.at[pl.ds(at * few, few), pl.ds(tall, tall), :],
                    sems.at[2 + which, place],
                ),
            ]
        return found

    @pl.when(step == 0)
    def _():
        unit, scale = norm_parts(third_ref[...])
        unit_s[...] = unit
        scale_s[...] = scale
        final = (unit * gain_ref[...] + shift_ref[...]).astype(bf16)
        final_s[...] = final
        final_t[...] = jnp.transpose(final)
        out_s[...] = jnp.zeros_like(out_s)
        fgrad_s[...] = jnp.zeros_like(fgrad_s)

    @pl.when(step >= 2)
    def _():
        for copy in copies(step - 2, slot):
            copy.wait()

    cot = cot_ref[...]
    up = up_ref[...].reshape(-1, up_ref.shape[-1])
    down = down_ref[...].reshape(-1, down_ref.shape[-1])
    upper = dot(final_s[...], up) + ubias_ref[...]
    cdf = 0.5 * (1.0 + lax.erf(upper * (0.5**0.5)))
    active = (upper * cdf).astype(bf16)
    slope = cdf + upper * (jnp.exp(-0.5 * upper * upper) * 0.3989422804014327)
    ugrad = (slope * dot(cot, down, NT)).astype(bf16)
    out_s[...] += dot(active, down)
    fgrad_s[...] += dot(ugrad, up, NT)
    ubgrad_ref[...] = jnp.sum(ugrad.astype(f32), 0, keepdims=True)
    wide = dot(final_t[...], ugrad).astype(bf16).reshape(half, 2, shard, tile)
    wide_s[slot, core] = wide[:, 0]
    wide_s[slot, 1 - core] = wide[:, 1]
    slim = dot(jnp.transpose(active), cot).astype(bf16).reshape(few, 2, tall, width)
    tall_s[slot, core] = slim[:, 0]
    tall_s[slot, 1 - core] = slim[:, 1]
    for copy in copies(step, slot):
        copy.start()

    @pl.when(step == last)
    def _():
        result_ref[...] = (third_ref[...] + (out_s[...] + dbias_ref[...])).astype(bf16)
        unit, fgrad, cotf = unit_s[...], fgrad_s[...], cot.astype(f32)
        tgrad_ref[...] = cotf + norm_back(unit, scale_s[...], fgrad * gain_ref[...])
        vec_ref[...] = jnp.zeros_like(vec_ref)
        vec_ref[0:1, :] = jnp.sum(fgrad * unit, 0, keepdims=True)
        vec_ref[1:2, :] = jnp.sum(fgrad, 0, keepdims=True)
        vec_ref[2:3, :] = jnp.sum(cotf, 0, keepdims=True)
        for copy in copies(step - 1, 1 - slot) + copies(step, slot):
            copy.wait()


def feed_forward(core, third, cot, gain, shift, down_bias, up_bias, packed, shard):
    rows, width = third.shape
    parts = packed.shape[0]
    hidden = up_bias.shape[1]
    tile = 512
    per = width // tile
    tall = hidden // parts
    spread = tile // tall
    steps = hidden // tile
    whole = lambda shape: pl.BlockSpec(shape, lambda j, c: (0,) * len(shape))
    return pl.pallas_call(
        block_kernel,
        grid_spec=pltpu.PrefetchScalarGridSpec(
            num_scalar_prefetch=1,
            grid=(steps,),
            in_specs=[
                whole((rows, width)),
                whole((rows, width)),
                whole((1, width)),
                whole((1, width)),
                whole((1, width)),
                pl.BlockSpec((1, tile), lambda j, c: (0, j)),
                pl.BlockSpec((parts, shard, tile), lambda j, c: (0, j // per, j % per)),
                pl.BlockSpec((spread, tall, width), lambda j, c: (j, 1, 0)),
            ],
            out_specs=[
                whole((rows, width)),
                whole((rows, width)),
                pl.BlockSpec(memory_space=pl.ANY),
                pl.BlockSpec(memory_space=pl.ANY),
                whole((8, width)),
                pl.BlockSpec((1, tile), lambda j, c: (0, j)),
            ],
            scratch_shapes=[
                pltpu.VMEM((rows, width), f32),
                pltpu.VMEM((rows, width), bf16),
                pltpu.VMEM((width, rows), bf16),
                pltpu.VMEM((rows, width), f32),
                pltpu.VMEM((rows, width), f32),
                pltpu.VMEM((rows, 1), f32),
                pltpu.VMEM((2, 2, parts // 2, shard, tile), bf16),
                pltpu.VMEM((2, 2, spread // 2, tall, width), bf16),
                pltpu.SemaphoreType.DMA((4, 2)),
            ],
        ),
        out_shape=[
            jax.ShapeDtypeStruct((rows, width), bf16),
            jax.ShapeDtypeStruct((rows, width), f32),
            jax.ShapeDtypeStruct((parts // 2, 2 * tall, width), bf16),
            jax.ShapeDtypeStruct((parts // 2, 2 * tall, width), bf16),
            jax.ShapeDtypeStruct((8, width), f32),
            jax.ShapeDtypeStruct((1, hidden), f32),
        ],
        compiler_params=params(),
        name="feed_forward",
        cost_estimate=pl.CostEstimate(flops=1, bytes_accessed=1, transcendentals=0),
    )(core, third, cot, gain, shift, down_bias, up_bias, packed, packed)


def grads_kernel(jobs, core_ref, *refs):
    ins, (keep_ref, send_ref) = refs[:-2], refs[-2:]
    step = pl.program_id(0)
    half, room, width = keep_ref.shape

    def store(block, rows):
        block = block.astype(bf16).reshape(half, 2, rows, width)
        keep_ref[:, :rows] = block[:, 0]
        send_ref[:, :rows] = block[:, 1]

    def swapped(block, rows):
        block = block.astype(bf16).reshape(half, 2, rows, width)
        keep_ref[:, :rows] = block[:, 1]
        send_ref[:, :rows] = block[:, 0]

    for at, (left, right, column) in enumerate(jobs):

        @pl.when(step == at)
        def _():
            rows = ins[left].shape[1] // (2 * half)
            if rows < room:
                keep_ref[...] = jnp.zeros_like(keep_ref)
                send_ref[...] = jnp.zeros_like(send_ref)
            block = dot(ins[left][...], ins[right][:, column * width : (column + 1) * width], TN)

            @pl.when(core_ref[0] == 0)
            def _():
                store(block, rows)

            @pl.when(core_ref[0] == 1)
            def _():
                swapped(block, rows)


def weight_grads(core, arrays, jobs, parts, shard, width):
    count = len(jobs)
    whole = lambda array: pl.BlockSpec(array.shape, lambda j, c: (0, 0))
    out = pl.BlockSpec((parts // 2, shard, width), lambda j, c: (0, j, 0))
    flops = sum(2 * arrays[i].shape[0] * arrays[i].shape[1] * width for i, _, _ in jobs)
    return pl.pallas_call(
        partial(grads_kernel, jobs),
        grid_spec=pltpu.PrefetchScalarGridSpec(
            num_scalar_prefetch=1,
            grid=(count,),
            in_specs=[whole(array) for array in arrays],
            out_specs=[out, out],
        ),
        out_shape=[jax.ShapeDtypeStruct((parts // 2, count * shard, width), bf16)] * 2,
        compiler_params=params(),
        name="weight_grads",
        cost_estimate=pl.CostEstimate(flops=1, bytes_accessed=1, transcendentals=0),
    )(core, *arrays)


class Grid:
    def __init__(self, mesh):
        self.obj, self.seq = mesh.shape["obj"], mesh.shape["ring"] * 2
        self.all = self.obj * self.seq
        self.place = lax.axis_index("ring") * 2 + lax.axis_index("core")
        self.me = lax.axis_index("obj") * self.seq + self.place
        self.group = [m for m in (1 << k for k in range(20)) if m < self.seq // 2]
        self.far = self.seq // 2

    def swap(self, value, mask):
        return lax.ppermute(value, BOTH, [(i, i ^ mask) for i in range(self.all)])

    def bit(self, mask):
        return (self.me // mask) % 2

    def gather_group(self, value):
        found = {0: value}
        for mask in self.group[1:][::-1] + self.group[:1]:
            found.update({d ^ mask: self.swap(v, mask) for d, v in list(found.items())})
        return [found[d] for d in range(self.seq // 2)]

    def in_order(self, terms):
        spot = self.place % len(terms)
        stacked = jnp.stack(terms)
        return [
            lax.dynamic_index_in_dim(stacked, spot ^ j, 0, keepdims=False) for j in range(len(terms))
        ]

    def exchange(self, blocks):
        spot = self.place % blocks.shape[0]
        found = []
        for d in range(blocks.shape[0]):
            block = lax.dynamic_index_in_dim(blocks, spot ^ d, 0, keepdims=False)
            found.append(self.swap(block, d) if d else block)
        return found

    def gather_self(self, blocks):
        found = yield self.exchange(blocks)
        found = jnp.stack(self.in_order(found))
        for mask in [m for m in (1 << k for k in range(20)) if self.far <= m < self.all]:
            moved = yield self.swap(found, mask)
            found = jnp.where(
                self.bit(mask) == 0, jnp.concatenate([found, moved]), jnp.concatenate([moved, found])
            )
        yield found

    def scatter_self(self, grad):
        terms = [grad]
        for mask in [m for m in (1 << k for k in range(20)) if self.far <= m < self.all][::-1]:
            terms = [t.reshape(2, t.shape[0] // 2, *t.shape[1:]) for t in terms]
            pick = lambda t, which: lax.dynamic_index_in_dim(t, which, 0, keepdims=False)
            moved = yield self.swap(add([pick(t, 1 - self.bit(mask)) for t in terms]), mask)
            terms = [pick(t, self.bit(mask)) for t in terms] + [moved]
        found = yield self.exchange(add(terms))
        yield jnp.stack(self.in_order(found), 1)

    def scatter(self, keep, send, whole):
        moved = yield self.swap(send, 1)
        total = add([keep, moved]).reshape(self.obj, self.seq // 2, *keep.shape[1:])
        total = yield total
        total = yield lax.psum_scatter(total, "obj", scatter_dimension=0, tiled=False)
        if whole:
            moved = yield lax.all_to_all(total, "ring", 0, 0, tiled=True)
            yield jnp.sum(moved.astype(f32), 0)
            return
        terms = [total]
        for mask in self.group[1:] + [self.far]:
            terms = [t.reshape(t.shape[0] // 2, 2, *t.shape[1:]) for t in terms]
            pick = lambda t, which: lax.dynamic_index_in_dim(t, which, 1, keepdims=False)
            moved = self.swap(add([pick(t, 1 - self.bit(mask)) for t in terms]), mask)
            if 4 * mask >= self.seq:
                moved = yield moved
            terms = [pick(t, self.bit(mask)) for t in terms] + [moved]
        yield sum(t[0].astype(f32) for t in terms)

    def exchange_core(self, terms):
        return [self.swap(t, 1) for t in terms[1::2]]

    def exchange_line(self, terms, moved):
        pairs = [add([t, m]) for t, m in zip(terms[::2], moved)]
        step = len(pairs) // 2
        while step > 1:
            pairs = [add([pairs[k], self.swap(pairs[k + step], 2 * step)]) for k in range(step)]
            step //= 2
        return pairs[0], self.swap(pairs[1], 2)


together = lax.optimization_barrier


def add(terms):
    if len(terms) == 1:
        return terms[0]
    return sum(t.astype(f32) for t in terms).astype(bf16)


def split_pairs(matrix):
    rows, width = matrix.shape
    return matrix.reshape(rows, 2, width // (2 * PAIR), PAIR).transpose(0, 2, 1, 3).reshape(rows, width)


def join_pairs(matrix):
    rows, width = matrix.shape
    return matrix.reshape(rows, width // (2 * PAIR), 2, PAIR).transpose(0, 2, 1, 3).reshape(rows, width)


def stack_columns(matrix, width):
    rows = matrix.shape[0]
    return matrix.reshape(rows, -1, width).transpose(1, 0, 2).reshape(-1, width)


def unstack_columns(matrix, rows):
    width = matrix.shape[1]
    return matrix.reshape(-1, rows, width).transpose(1, 0, 2).reshape(rows, -1)


def pad_rows(matrix, rows):
    return jnp.pad(matrix, ((0, rows - matrix.shape[0]), (0, 0)))


def on_device(
    mesh,
    tokens,
    camera,
    patches,
    patch_count,
    patch_index,
    cotangent,
    camera_weight,
    self_weight,
    self_output,
    mid_gain,
    mid_bias,
    patch_weight,
    view_table,
    cross_query,
    cross_memory,
    cross_output,
    last_gain,
    last_bias,
    up_weight,
    up_bias,
    down_weight,
    down_bias,
):
    grid = Grid(mesh)
    parts = grid.all
    width = self_output.shape[1]
    low = lambda v: v.astype(bf16)
    factor = HEAD_DIM**-0.5
    core = grid.bit(1)
    half = grid.bit(grid.far)

    def compact(value):
        mine = lax.dynamic_index_in_dim(value, half, 0, keepdims=False)
        other = lax.dynamic_index_in_dim(value, 1 - half, 0, keepdims=False)
        return jnp.concatenate([mine, grid.swap(other, grid.far)], 0)

    def spread(mine, other):
        mine = mine[: other.shape[0]]
        return jnp.where(half == 0, jnp.stack([mine, other]), jnp.stack([other, mine]))

    def chunks(terms):
        return jnp.split(terms, grid.seq // 2, 0)

    shard = self_output.shape[0]
    self_mixed = jnp.concatenate(
        [low(self_weight[:, :width]), split_pairs(low(self_weight[:, width:]))], 1
    )
    small = jnp.concatenate(
        [
            low(camera_weight).reshape(-1),
            low(view_table).reshape(-1),
            low(mid_gain),
            low(mid_bias),
            low(last_gain),
            low(last_bias),
            low(down_bias),
            low(up_bias),
        ]
    )
    small_sizes = [
        camera_weight.size,
        view_table.size,
        shard,
        shard,
        shard,
        shard,
        shard,
        up_bias.size,
    ]
    patch_rows = patch_weight.shape[0]
    group = grid.seq // 2
    lot = 3 * width // group
    few = width // group
    small_count = -(-small.size // lot)
    small_rows = jnp.pad(small, (0, small_count * lot - small.size)).reshape(-1, lot)
    blocks = jnp.concatenate(
        [
            self_mixed[:, :width].reshape(shard, group, few),
            self_mixed[:, width:].reshape(shard, group, 2 * few),
        ],
        2,
    ).transpose(1, 0, 2)
    blocks = jnp.concatenate(
        [blocks, jnp.broadcast_to(pad_rows(small_rows, -(-small_count // 8) * 8), (group, -(-small_count // 8) * 8, lot))], 1
    )
    patch_room = -(-patch_rows // shard) * shard
    first = jnp.concatenate(
        [
            low(self_output),
            low(cross_query),
            low(cross_output),
            stack_columns(split_pairs(low(cross_memory)), width),
            pad_rows(low(patch_weight), patch_room),
        ],
        0,
    )
    own_gather = grid.gather_self(blocks)
    blocks = next(own_gather)
    tokens_all = jnp.concatenate(grid.gather_group(compact(tokens)), 0)
    first = lax.all_gather(first, BOTH, axis=0, tiled=False)
    ffn_mine = jnp.concatenate([stack_columns(low(up_weight), width), low(down_weight)], 0)
    while isinstance(blocks, list) or blocks.shape[0] < parts:
        blocks = own_gather.send(blocks)
        if isinstance(blocks, list) or blocks.shape[0] == parts // 2:
            break
    blocks, tokens_all, ffn_mine, patches, patch_index = together(
        (blocks, tokens_all, ffn_mine, patches, patch_index)
    )
    packed = lax.all_gather(ffn_mine, BOTH, axis=0, tiled=False)
    feats_all = jnp.concatenate(grid.gather_group(compact(patches)), 0)
    views_all = jnp.concatenate(grid.gather_group(compact(patch_index)), 0) // VIEW_PATCHES
    blocks = own_gather.send(blocks)
    self_own = blocks[:, :shard].reshape(parts * shard, lot)
    tiny = blocks[:, shard : shard + small_count].reshape(parts, -1)
    pieces = []
    at = 0
    for size in small_sizes:
        pieces.append(tiny[:, at : at + size].astype(f32))
        at += size
    full_camera = pieces[0].reshape(parts, 16, -1).transpose(1, 0, 2).reshape(16, -1)
    full_view = pieces[1].reshape(parts, VIEWS, -1).transpose(1, 0, 2).reshape(VIEWS, -1)
    g_mid, b_mid, g_last, b_last, b_down, b_up = (p.reshape(1, -1) for p in pieces[2:])

    own = tokens_all.shape[0] // (grid.seq // 2)
    slots_own = feats_all.shape[0] // (grid.seq // 2)
    x_all = tokens_all.astype(f32)
    x = x_all[:own]
    camera_mine = lax.dynamic_index_in_dim(camera, half, 0, keepdims=False)
    live = lax.dynamic_index_in_dim(patch_count, half, 0, keepdims=False)
    modulation = jnp.sum(camera_mine[:, None] * full_camera, 0)
    scale1, shift1 = 1.0 + modulation[None, :width], modulation[None, width:]
    hidden_all = low(norm_parts(x_all)[0] * scale1 + shift1)
    triple = low(dot(hidden_all, self_own))
    query = low(triple[:, :few].astype(f32) * factor)
    kv = triple[:, few:]
    query, kv, feats_all, views_all, cotangent = together((query, kv, feats_all, views_all, cotangent))
    attended_own, lse1 = attend(query, kv, None)
    attended_own, first = together((attended_own, first))
    cot = compact(cotangent)
    attended = grid.exchange(jnp.stack(grid.in_order(chunks(attended_own))))

    def square(start, rows=shard):
        return first[:, start : start + rows].reshape(parts * rows, width)

    full_out = square(0)
    full_cq = square(shard)
    full_co = square(2 * shard)
    full_mem = jnp.concatenate([square(3 * shard), square(4 * shard)], 1)
    full_patch = square(5 * shard, patch_rows)
    hot_all = (views_all[:, None] == jnp.arange(VIEWS)[None, :]).astype(f32)
    view_part = sum(hot_all[:, v : v + 1] * full_view[v : v + 1] for v in range(VIEWS))
    embedded_all = low(dot(feats_all, full_patch) + view_part)
    mem = low(dot(embedded_all, full_mem))
    attended, mem = together((attended, mem))
    attended = jnp.concatenate(grid.in_order(attended), 1)
    place = grid.place
    chunk = patches.shape[1]
    lane = jnp.arange(chunk)
    slots = jnp.concatenate(
        [
            chunk * (place ^ d ^ far) + lane
            for d in range(grid.seq // 2)
            for far in (0, grid.far)
        ]
    )
    bias = jnp.where(slots < live, 0.0, -1e30).astype(f32).reshape(1, -1)

    second = x + dot(attended, full_out)
    unit2, rstd2 = norm_parts(second)
    normed = low(unit2 * g_mid + b_mid)
    asked = low(low(dot(normed, full_cq)).astype(f32) * factor)
    crossed, lse2 = attend(asked, mem, bias)
    third = second + dot(crossed, full_co)
    third, cot = together((third, cot))
    core_now = core.reshape(1).astype(jnp.int32)
    result, third_grad, ffn_keep, ffn_send, last_vectors, up_bias_grad = feed_forward(
        core_now, third, cot, g_last, b_last, b_down, b_up, packed, shard
    )
    tall = down_weight.shape[0]

    ffn = grid.scatter(ffn_keep, ffn_send, True)
    ffn_moved = next(ffn)
    half_rows = result.shape[0] // 2
    third_low = low(third_grad)
    crossed_grad = low(dot(third_low, full_co, NT))
    ffn_moved, crossed_grad = together((ffn_moved, crossed_grad))
    ffn_moved = ffn.send(ffn_moved)
    ffn_moved, crossed_grad = together((ffn_moved, crossed_grad))

    ffn_moved = ffn.send(ffn_moved)
    result_moved = grid.swap(result[half_rows:], grid.far)
    asked_grad, mem_terms = attend_back(asked, mem, crossed, crossed_grad, lse2, bias)
    asked_grad, mem_terms, result_moved = together((asked_grad, mem_terms, result_moved))
    normed_grad = dot(asked_grad, full_cq, NT)
    second_grad = third_grad + norm_back(unit2, rstd2, normed_grad * g_mid)
    second_low = low(second_grad)
    attended_grad = low(dot(second_low, full_out, NT))
    embedded_grad = low(dot(mem_terms, full_mem, NT))
    arrays = [
        crossed,
        third_low,
        normed,
        asked_grad,
        attended,
        second_low,
        embedded_all,
        mem_terms,
        feats_all,
        embedded_grad,
    ]
    jobs = ((0, 1, 0), (2, 3, 0), (4, 5, 0), (6, 7, 0), (6, 7, 1), (8, 9, 0))
    attended_grad, arrays = together((attended_grad, arrays))
    grad_moved = []
    for d in range(group):
        at = ((grid.place % group) ^ d) * few
        part = lax.dynamic_slice_in_dim(attended_grad, at, few, 1)
        grad_moved.append(grid.swap(part, d) if d else part)
    keep, send = weight_grads(core_now, arrays, jobs, parts, shard, width)
    grad_moved, keep, send = together((grad_moved, keep, send))
    rest = grid.scatter(keep, send, False)
    moved = next(rest)
    patch_terms = chunks(low(dot(embedded_grad, full_patch, NT)))
    grad_own = jnp.concatenate(grad_moved, 0)
    grad_own, patch_terms, moved = together((grad_own, patch_terms, moved))
    moved = rest.send(moved)
    patch_moved = grid.exchange_core(patch_terms)
    grad_own, patch_moved, moved, ffn_moved = together((grad_own, patch_moved, moved, ffn_moved))

    moved = rest.send(moved)
    ffn_moved = ffn.send(ffn_moved)
    patch_mine, patch_moved = grid.exchange_line(patch_terms, patch_moved)
    query_grad, pair_grad = attend_back(query, kv, attended_own, grad_own, lse1, None)
    patch_moved, query_grad, pair_grad = together((patch_moved, query_grad, pair_grad))

    triple_grad = jnp.concatenate([query_grad, pair_grad], 1)
    hidden_terms = chunks(low(dot(triple_grad, self_own, NT)))
    hidden_terms, triple_grad = together((hidden_terms, triple_grad))
    hidden_moved = grid.exchange_core(hidden_terms)
    self_grad = low(dot(hidden_all, triple_grad, TN))
    self_grad, hidden_moved = together((self_grad, hidden_moved))

    own_scatter = grid.scatter_self(self_grad.reshape(parts, shard, lot))
    own_moved = next(own_scatter)
    hidden_mine, hidden_moved = grid.exchange_line(hidden_terms, hidden_moved)
    patch_low = low(patch_mine.astype(f32) + patch_moved.astype(f32))
    patch_half = patch_low.shape[0] // 2
    patch_moved = grid.swap(patch_low[patch_half:], grid.far)
    result = spread(result, result_moved)
    view_grad = jnp.stack(
        [jnp.sum(hot_all[:, v : v + 1] * embedded_grad.astype(f32), 0) for v in range(VIEWS)]
    )
    mid_vectors = jnp.stack([jnp.sum(normed_grad * unit2, 0), jnp.sum(normed_grad, 0)])
    own_moved, hidden_moved, patch_moved, result, view_grad, mid_vectors, last_vectors, up_bias_grad = together(
        (own_moved, hidden_moved, patch_moved, result, view_grad, mid_vectors, last_vectors, up_bias_grad)
    )

    unit1, rstd1 = norm_parts(together(tokens_all[:own]).astype(f32))
    hidden_grad = hidden_mine.astype(f32) + hidden_moved.astype(f32)
    token_grad = low(second_grad + norm_back(unit1, rstd1, hidden_grad * scale1))
    token_grad, hidden_grad, own_moved, moved, ffn_moved = together(
        (token_grad, hidden_grad, own_moved, moved, ffn_moved)
    )
    token_moved = grid.swap(token_grad[half_rows:], grid.far)
    moved = rest.send(moved)
    own_moved = own_scatter.send(own_moved)
    modulation_grad = jnp.concatenate(
        [jnp.sum(hidden_grad * unit1, 0), jnp.sum(hidden_grad, 0)]
    )
    camera_grad = camera_mine[:, None] * modulation_grad[None]
    vectors = jnp.concatenate(
        [
            view_grad,
            mid_vectors,
            last_vectors[0:3],
        ],
        0,
    )
    small_grad = jnp.concatenate(
        [
            low(camera_grad).reshape(16, parts, -1).transpose(1, 0, 2).reshape(parts, -1),
            low(vectors).reshape(VIEWS + 5, parts, -1).transpose(1, 0, 2).reshape(parts, -1),
            low(up_bias_grad).reshape(parts, -1),
        ],
        1,
    )
    small_grad = jnp.pad(small_grad, ((0, 0), (0, small_count * lot - small_grad.shape[1])))
    small_grad, own_moved, token_moved, moved = together((small_grad, own_moved, token_moved, moved))
    while not isinstance(own_moved, list):
        own_moved = own_scatter.send(own_moved)
        if own_moved.shape[0] == group:
            break
    moved = rest.send(moved)
    small_grad = lax.all_to_all(small_grad.reshape(parts, small_count, lot), BOTH, 0, 0, tiled=True)
    token_grad = spread(token_grad, token_moved)
    ffn_grad = ffn.send(ffn_moved)
    ffn_up, ffn_down = unstack_columns(ffn_grad[:tall], shard), ffn_grad[tall:]
    patch_grad = spread(patch_low, patch_moved)
    own_moved, moved, token_grad, small_grad, patch_grad, ffn_up, ffn_down = together(
        (own_moved, moved, token_grad, small_grad, patch_grad, ffn_up, ffn_down)
    )
    own_moved = own_scatter.send(own_moved)
    tiny = jnp.sum(small_grad.astype(f32), 0).reshape(-1)
    rest_sum = rest.send(moved)
    self_sum = own_scatter.send(own_moved).astype(f32)
    pieces = []
    at = 0
    for size in small_sizes:
        pieces.append(tiny[at : at + size])
        at += size
    self_sum = jnp.concatenate(
        [
            self_sum[:, :, :few].reshape(shard, width),
            join_pairs(self_sum[:, :, few:].reshape(shard, 2 * width)),
        ],
        1,
    )
    return (
        result,
        token_grad,
        patch_grad,
        pieces[0].reshape(camera_weight.shape),
        self_sum,
        rest_sum[2 * shard : 3 * shard],
        pieces[2],
        pieces[3],
        rest_sum[5 * shard : 5 * shard + patch_rows],
        pieces[1].reshape(view_table.shape),
        rest_sum[shard : 2 * shard],
        join_pairs(unstack_columns(rest_sum[3 * shard : 5 * shard], shard)),
        rest_sum[:shard],
        pieces[4],
        pieces[5],
        ffn_up,
        pieces[7],
        ffn_down,
        pieces[6],
    )


def solution(mesh):
    line = mesh.shape["seq"] // 2
    mesh = jax.sharding.Mesh(
        mesh.devices.reshape(mesh.shape["obj"], line, 2), ("obj", "ring", "core")
    )
    rows, flat, lanes = P(BOTH, None), P(BOTH), P(None, BOTH)
    sequence = P("obj", SEQ, None)
    in_specs = (
        sequence,
        P("obj", None),
        sequence,
        P("obj"),
        P("obj", SEQ),
        sequence,
        lanes,
        rows,
        rows,
        flat,
        flat,
        rows,
        lanes,
        rows,
        rows,
        rows,
        flat,
        flat,
        rows,
        flat,
        rows,
        flat,
    )
    out_specs = (
        sequence,
        sequence,
        sequence,
        lanes,
        rows,
        rows,
        flat,
        flat,
        rows,
        lanes,
        rows,
        rows,
        rows,
        flat,
        flat,
        rows,
        flat,
        rows,
        flat,
    )
    return jax.shard_map(
        partial(on_device, mesh),
        mesh=mesh,
        in_specs=in_specs,
        out_specs=out_specs,
        check_vma=False,
    )
```

```python
from functools import partial

import jax
import jax.numpy as jnp
from jax import lax
from jax.experimental import pallas as pl
from jax.experimental.pallas import tpu as pltpu
from jax.sharding import PartitionSpec as P

HEAD_DIM = 64
PAIR = 2 * HEAD_DIM
VIEWS = 4
VIEW_PATCHES = 1024
BOTH = ("obj", "ring", "core")
SEQ = ("ring", "core")

epsilon = 1e-05
f32 = jnp.float32
bf16 = jnp.bfloat16
NN = (((1,), (0,)), ((), ()))
NT = (((1,), (1,)), ((), ()))
TN = (((0,), (0,)), ((), ()))


def dot(left, right, dims=NN):
    return lax.dot_general(left, right, dims, preferred_element_type=f32)


def params(megabytes=56):
    return pltpu.CompilerParams(vmem_limit_bytes=megabytes * 2**20)


def norm_parts(values):
    center = values - jnp.mean(values, -1, keepdims=True)
    spread = jnp.mean(center * center, -1, keepdims=True)
    scale = lax.rsqrt(spread + epsilon)
    return center * scale, scale


def norm_back(unit, scale, grad):
    return scale * (
        grad - jnp.mean(grad, -1, keepdims=True) - unit * jnp.mean(grad * unit, -1, keepdims=True)
    )


def attend_kernel(masked, *refs):
    q_ref, kv_ref = refs[:2]
    bias = refs[2] if masked else None
    o_ref, lse_ref = refs[-2:]
    query = q_ref[...]
    keys, values = kv_ref[:, :PAIR], kv_ref[:, PAIR:]
    low = lax.broadcasted_iota(jnp.int32, query.shape, 1) < HEAD_DIM
    outs, lses = [], []
    for head in range(2):
        mine = low if head == 0 else ~low
        score = dot(jnp.where(mine, query, jnp.zeros_like(query)), keys, NT)
        if masked:
            score = score + bias[...]
        top = jnp.max(score, 1, keepdims=True)
        lifted = jnp.exp(score - top)
        total = jnp.sum(lifted, 1, keepdims=True)
        outs.append(dot(lifted.astype(bf16), values) * (1.0 / total))
        lses.append(top + jnp.log(total))
    o_ref[...] = jnp.where(low, outs[0], outs[1]).astype(bf16)
    lse_ref[...] = jnp.where(low, lses[0], lses[1])[None]


def attend(query, kv, bias):
    rows, width = query.shape
    slots, pairs = kv.shape[0], width // PAIR
    tile = min(rows, 384)
    row = pl.BlockSpec((tile, PAIR), lambda i, r: (r, i))
    masked = bias is not None
    return pl.pallas_call(
        partial(attend_kernel, masked),
        grid=(pairs, rows // tile),
        in_specs=[row, pl.BlockSpec((slots, 2 * PAIR), lambda i, r: (0, i))]
        + [pl.BlockSpec((1, slots), lambda i, r: (0, 0))] * masked,
        out_specs=[row, pl.BlockSpec((1, tile, PAIR), lambda i, r: (i, r, 0))],
        out_shape=[
            jax.ShapeDtypeStruct((rows, width), bf16),
            jax.ShapeDtypeStruct((pairs, rows, PAIR), f32),
        ],
        compiler_params=params(),
        name="attend",
        cost_estimate=pl.CostEstimate(
            flops=16 * rows * slots * width,
            bytes_accessed=4 * width * (rows + slots),
            transcendentals=2 * pairs * rows * slots,
        ),
    )(query, kv, *([bias] if masked else []))


def attend_back_kernel(masked, *refs):
    q_ref, kv_ref, o_ref, do_ref, lse_ref = refs[:5]
    bias = refs[5] if masked else None
    dq_ref, dkv_ref, dk_s, dv_s = refs[-4:]
    query, grad = q_ref[...], do_ref[...]
    keys, values = kv_ref[:, :PAIR], kv_ref[:, PAIR:]
    low = lax.broadcasted_iota(jnp.int32, query.shape, 1) < HEAD_DIM
    lse = lse_ref[0]
    product = o_ref[...].astype(f32) * grad.astype(f32)
    dk = dv = 0.0
    dqs = []
    for head in range(2):
        mine = low if head == 0 else ~low
        head_query = jnp.where(mine, query, jnp.zeros_like(query))
        head_grad = jnp.where(mine, grad, jnp.zeros_like(grad))
        score = dot(head_query, keys, NT)
        if masked:
            score = score + bias[...]
        probs = jnp.exp(score - lse[:, HEAD_DIM * head : HEAD_DIM * head + 1])
        delta = jnp.sum(jnp.where(mine, product, 0.0), 1, keepdims=True)
        score_grad = (probs * (dot(head_grad, values, NT) - delta)).astype(bf16)
        dk = dk + dot(jnp.transpose(head_query), score_grad)
        dv = dv + dot(jnp.transpose(head_grad), probs.astype(bf16))
        dqs.append(dot(score_grad, keys))
    dq_ref[...] = (jnp.where(low, dqs[0], dqs[1]) * HEAD_DIM**-0.5).astype(bf16)
    step = pl.program_id(1)

    @pl.when(step == 0)
    def _():
        dk_s[...] = dk
        dv_s[...] = dv

    @pl.when(step > 0)
    def _():
        dk_s[...] += dk
        dv_s[...] += dv

    @pl.when(step == pl.num_programs(1) - 1)
    def _():
        dkv_ref[:, :PAIR] = jnp.transpose(dk_s[...]).astype(bf16)
        dkv_ref[:, PAIR:] = jnp.transpose(dv_s[...]).astype(bf16)


def attend_back(query, kv, out, grad, lse, bias):
    rows, width = query.shape
    slots, pairs = kv.shape[0], width // PAIR
    tile = min(rows, 384)
    row = pl.BlockSpec((tile, PAIR), lambda i, r: (r, i))
    slot = pl.BlockSpec((slots, 2 * PAIR), lambda i, r: (0, i))
    masked = bias is not None
    return pl.pallas_call(
        partial(attend_back_kernel, masked),
        grid=(pairs, rows // tile),
        in_specs=[row, slot, row, row, pl.BlockSpec((1, tile, PAIR), lambda i, r: (i, r, 0))]
        + [pl.BlockSpec((1, slots), lambda i, r: (0, 0))] * masked,
        out_specs=[row, slot],
        out_shape=[
            jax.ShapeDtypeStruct((rows, width), bf16),
            jax.ShapeDtypeStruct((slots, 2 * width), bf16),
        ],
        scratch_shapes=[pltpu.VMEM((PAIR, slots), f32)] * 2,
        compiler_params=params(),
        name="attend_back",
        cost_estimate=pl.CostEstimate(
            flops=40 * rows * slots * width,
            bytes_accessed=8 * width * (rows + slots),
            transcendentals=2 * pairs * rows * slots,
        ),
    )(query, kv, out, grad, lse, *([bias] if masked else []))


def block_kernel(core_ref, third_ref, cot_ref, gain_ref, shift_ref, dbias_ref, ubias_ref, up_ref, down_ref,
                 result_ref, tgrad_ref, keep_ref, send_ref, vec_ref, ubgrad_ref,
                 unit_s, final_s, final_t, out_s, fgrad_s, scale_s, wide_s, tall_s, sems):
    step = pl.program_id(0)
    last = pl.num_programs(0) - 1
    slot = lax.rem(step, 2)
    core = core_ref[0]
    _, _, half, shard, tile = wide_s.shape
    _, _, few, tall, width = tall_s.shape
    per = width // tile

    def copies(at, place):
        row = pl.multiple_of((at // per) * shard, shard)
        lane = pl.multiple_of(lax.rem(at, per) * tile, tile)
        found = []
        for which, ref in enumerate((keep_ref, send_ref)):
            found += [
                pltpu.make_async_copy(
                    wide_s.at[place, which],
                    ref.at[:, pl.ds(row, shard), pl.ds(lane, tile)],
                    sems.at[which, place],
                ),
                pltpu.make_async_copy(
                    tall_s.at[place, which],
                    ref.at[pl.ds(at * few, few), pl.ds(tall, tall), :],
                    sems.at[2 + which, place],
                ),
            ]
        return found

    @pl.when(step == 0)
    def _():
        unit, scale = norm_parts(third_ref[...])
        unit_s[...] = unit
        scale_s[...] = scale
        final = (unit * gain_ref[...] + shift_ref[...]).astype(bf16)
        final_s[...] = final
        final_t[...] = jnp.transpose(final)
        out_s[...] = jnp.zeros_like(out_s)
        fgrad_s[...] = jnp.zeros_like(fgrad_s)

    @pl.when(step >= 2)
    def _():
        for copy in copies(step - 2, slot):
            copy.wait()

    cot = cot_ref[...]
    up = up_ref[...].reshape(-1, up_ref.shape[-1])
    down = down_ref[...].reshape(-1, down_ref.shape[-1])
    upper = dot(final_s[...], up) + ubias_ref[...]
    cdf = 0.5 * (1.0 + lax.erf(upper * (0.5**0.5)))
    active = (upper * cdf).astype(bf16)
    slope = cdf + upper * (jnp.exp(-0.5 * upper * upper) * 0.3989422804014327)
    ugrad = (slope * dot(cot, down, NT)).astype(bf16)
    out_s[...] += dot(active, down)
    fgrad_s[...] += dot(ugrad, up, NT)
    ubgrad_ref[...] = jnp.sum(ugrad.astype(f32), 0, keepdims=True)
    wide = dot(final_t[...], ugrad).astype(bf16).reshape(half, 2, shard, tile)
    wide_s[slot, core] = wide[:, 0]
    wide_s[slot, 1 - core] = wide[:, 1]
    slim = dot(jnp.transpose(active), cot).astype(bf16).reshape(few, 2, tall, width)
    tall_s[slot, core] = slim[:, 0]
    tall_s[slot, 1 - core] = slim[:, 1]
    for copy in copies(step, slot):
        copy.start()

    @pl.when(step == last)
    def _():
        result_ref[...] = (third_ref[...] + (out_s[...] + dbias_ref[...])).astype(bf16)
        unit, fgrad, cotf = unit_s[...], fgrad_s[...], cot.astype(f32)
        tgrad_ref[...] = cotf + norm_back(unit, scale_s[...], fgrad * gain_ref[...])
        vec_ref[...] = jnp.zeros_like(vec_ref)
        vec_ref[0:1, :] = jnp.sum(fgrad * unit, 0, keepdims=True)
        vec_ref[1:2, :] = jnp.sum(fgrad, 0, keepdims=True)
        vec_ref[2:3, :] = jnp.sum(cotf, 0, keepdims=True)
        for copy in copies(step - 1, 1 - slot) + copies(step, slot):
            copy.wait()


def feed_forward(core, third, cot, gain, shift, down_bias, up_bias, packed, shard):
    rows, width = third.shape
    parts = packed.shape[0]
    hidden = up_bias.shape[1]
    tile = 512
    per = width // tile
    tall = hidden // parts
    spread = tile // tall
    steps = hidden // tile
    whole = lambda shape: pl.BlockSpec(shape, lambda j, c: (0,) * len(shape))
    return pl.pallas_call(
        block_kernel,
        grid_spec=pltpu.PrefetchScalarGridSpec(
            num_scalar_prefetch=1,
            grid=(steps,),
            in_specs=[
                whole((rows, width)),
                whole((rows, width)),
                whole((1, width)),
                whole((1, width)),
                whole((1, width)),
                pl.BlockSpec((1, tile), lambda j, c: (0, j)),
                pl.BlockSpec((parts, shard, tile), lambda j, c: (0, j // per, j % per)),
                pl.BlockSpec((spread, tall, width), lambda j, c: (j, 1, 0)),
            ],
            out_specs=[
                whole((rows, width)),
                whole((rows, width)),
                pl.BlockSpec(memory_space=pl.ANY),
                pl.BlockSpec(memory_space=pl.ANY),
                whole((8, width)),
                pl.BlockSpec((1, tile), lambda j, c: (0, j)),
            ],
            scratch_shapes=[
                pltpu.VMEM((rows, width), f32),
                pltpu.VMEM((rows, width), bf16),
                pltpu.VMEM((width, rows), bf16),
                pltpu.VMEM((rows, width), f32),
                pltpu.VMEM((rows, width), f32),
                pltpu.VMEM((rows, 1), f32),
                pltpu.VMEM((2, 2, parts // 2, shard, tile), bf16),
                pltpu.VMEM((2, 2, spread // 2, tall, width), bf16),
                pltpu.SemaphoreType.DMA((4, 2)),
            ],
        ),
        out_shape=[
            jax.ShapeDtypeStruct((rows, width), bf16),
            jax.ShapeDtypeStruct((rows, width), f32),
            jax.ShapeDtypeStruct((parts // 2, 2 * tall, width), bf16),
            jax.ShapeDtypeStruct((parts // 2, 2 * tall, width), bf16),
            jax.ShapeDtypeStruct((8, width), f32),
            jax.ShapeDtypeStruct((1, hidden), f32),
        ],
        compiler_params=params(),
        name="feed_forward",
        cost_estimate=pl.CostEstimate(flops=1, bytes_accessed=1, transcendentals=0),
    )(core, third, cot, gain, shift, down_bias, up_bias, packed, packed)


def grads_kernel(jobs, core_ref, *refs):
    ins, (keep_ref, send_ref) = refs[:-2], refs[-2:]
    step = pl.program_id(0)
    half, room, width = keep_ref.shape

    def store(block, rows):
        block = block.astype(bf16).reshape(half, 2, rows, width)
        keep_ref[:, :rows] = block[:, 0]
        send_ref[:, :rows] = block[:, 1]

    def swapped(block, rows):
        block = block.astype(bf16).reshape(half, 2, rows, width)
        keep_ref[:, :rows] = block[:, 1]
        send_ref[:, :rows] = block[:, 0]

    for at, (left, right, column) in enumerate(jobs):

        @pl.when(step == at)
        def _():
            rows = ins[left].shape[1] // (2 * half)
            if rows < room:
                keep_ref[...] = jnp.zeros_like(keep_ref)
                send_ref[...] = jnp.zeros_like(send_ref)
            block = dot(ins[left][...], ins[right][:, column * width : (column + 1) * width], TN)

            @pl.when(core_ref[0] == 0)
            def _():
                store(block, rows)

            @pl.when(core_ref[0] == 1)
            def _():
                swapped(block, rows)


def weight_grads(core, arrays, jobs, parts, shard, width):
    count = len(jobs)
    whole = lambda array: pl.BlockSpec(array.shape, lambda j, c: (0, 0))
    out = pl.BlockSpec((parts // 2, shard, width), lambda j, c: (0, j, 0))
    flops = sum(2 * arrays[i].shape[0] * arrays[i].shape[1] * width for i, _, _ in jobs)
    return pl.pallas_call(
        partial(grads_kernel, jobs),
        grid_spec=pltpu.PrefetchScalarGridSpec(
            num_scalar_prefetch=1,
            grid=(count,),
            in_specs=[whole(array) for array in arrays],
            out_specs=[out, out],
        ),
        out_shape=[jax.ShapeDtypeStruct((parts // 2, count * shard, width), bf16)] * 2,
        compiler_params=params(),
        name="weight_grads",
        cost_estimate=pl.CostEstimate(flops=1, bytes_accessed=1, transcendentals=0),
    )(core, *arrays)


class Grid:
    def __init__(self, mesh):
        self.obj, self.seq = mesh.shape["obj"], mesh.shape["ring"] * 2
        self.all = self.obj * self.seq
        self.place = lax.axis_index("ring") * 2 + lax.axis_index("core")
        self.me = lax.axis_index("obj") * self.seq + self.place
        self.group = [m for m in (1 << k for k in range(20)) if m < self.seq // 2]
        self.far = self.seq // 2

    def swap(self, value, mask):
        return lax.ppermute(value, BOTH, [(i, i ^ mask) for i in range(self.all)])

    def bit(self, mask):
        return (self.me // mask) % 2

    def gather_group(self, value):
        found = {0: value}
        for mask in self.group[1:][::-1] + self.group[:1]:
            found.update({d ^ mask: self.swap(v, mask) for d, v in list(found.items())})
        return [found[d] for d in range(self.seq // 2)]

    def in_order(self, terms):
        spot = self.place % len(terms)
        stacked = jnp.stack(terms)
        return [
            lax.dynamic_index_in_dim(stacked, spot ^ j, 0, keepdims=False) for j in range(len(terms))
        ]

    def exchange(self, blocks):
        spot = self.place % blocks.shape[0]
        found = []
        for d in range(blocks.shape[0]):
            block = lax.dynamic_index_in_dim(blocks, spot ^ d, 0, keepdims=False)
            found.append(self.swap(block, d) if d else block)
        return found

    def gather_self(self, blocks):
        found = yield self.exchange(blocks)
        found = jnp.stack(self.in_order(found))
        for mask in [m for m in (1 << k for k in range(20)) if self.far <= m < self.all]:
            moved = yield self.swap(found, mask)
            found = jnp.where(
                self.bit(mask) == 0, jnp.concatenate([found, moved]), jnp.concatenate([moved, found])
            )
        yield found

    def scatter_self(self, grad):
        terms = [grad]
        for mask in [m for m in (1 << k for k in range(20)) if self.far <= m < self.all][::-1]:
            terms = [t.reshape(2, t.shape[0] // 2, *t.shape[1:]) for t in terms]
            pick = lambda t, which: lax.dynamic_index_in_dim(t, which, 0, keepdims=False)
            moved = yield self.swap(add([pick(t, 1 - self.bit(mask)) for t in terms]), mask)
            terms = [pick(t, self.bit(mask)) for t in terms] + [moved]
        found = yield self.exchange(add(terms))
        yield jnp.stack(self.in_order(found), 1)

    def scatter(self, keep, send, whole):
        moved = yield self.swap(send, 1)
        total = add([keep, moved]).reshape(self.obj, self.seq // 2, *keep.shape[1:])
        total = yield total
        total = yield lax.psum_scatter(total, "obj", scatter_dimension=0, tiled=False)
        if whole:
            moved = yield lax.all_to_all(total, "ring", 0, 0, tiled=True)
            yield jnp.sum(moved.astype(f32), 0)
            return
        terms = [total]
        for mask in self.group[1:] + [self.far]:
            terms = [t.reshape(t.shape[0] // 2, 2, *t.shape[1:]) for t in terms]
            pick = lambda t, which: lax.dynamic_index_in_dim(t, which, 1, keepdims=False)
            moved = self.swap(add([pick(t, 1 - self.bit(mask)) for t in terms]), mask)
            if 4 * mask >= self.seq:
                moved = yield moved
            terms = [pick(t, self.bit(mask)) for t in terms] + [moved]
        yield sum(t[0].astype(f32) for t in terms)

    def exchange_core(self, terms):
        return [self.swap(t, 1) for t in terms[1::2]]

    def exchange_line(self, terms, moved):
        pairs = [add([t, m]) for t, m in zip(terms[::2], moved)]
        step = len(pairs) // 2
        while step > 1:
            pairs = [add([pairs[k], self.swap(pairs[k + step], 2 * step)]) for k in range(step)]
            step //= 2
        return pairs[0], self.swap(pairs[1], 2)


together = lax.optimization_barrier


def add(terms):
    if len(terms) == 1:
        return terms[0]
    return sum(t.astype(f32) for t in terms).astype(bf16)


def split_pairs(matrix):
    rows, width = matrix.shape
    return matrix.reshape(rows, 2, width // (2 * PAIR), PAIR).transpose(0, 2, 1, 3).reshape(rows, width)


def join_pairs(matrix):
    rows, width = matrix.shape
    return matrix.reshape(rows, width // (2 * PAIR), 2, PAIR).transpose(0, 2, 1, 3).reshape(rows, width)


def stack_columns(matrix, width):
    rows = matrix.shape[0]
    return matrix.reshape(rows, -1, width).transpose(1, 0, 2).reshape(-1, width)


def unstack_columns(matrix, rows):
    width = matrix.shape[1]
    return matrix.reshape(-1, rows, width).transpose(1, 0, 2).reshape(rows, -1)


def pad_rows(matrix, rows):
    return jnp.pad(matrix, ((0, rows - matrix.shape[0]), (0, 0)))


def on_device(
    mesh,
    tokens,
    camera,
    patches,
    patch_count,
    patch_index,
    cotangent,
    camera_weight,
    self_weight,
    self_output,
    mid_gain,
    mid_bias,
    patch_weight,
    view_table,
    cross_query,
    cross_memory,
    cross_output,
    last_gain,
    last_bias,
    up_weight,
    up_bias,
    down_weight,
    down_bias,
):
    grid = Grid(mesh)
    parts = grid.all
    width = self_output.shape[1]
    low = lambda v: v.astype(bf16)
    factor = HEAD_DIM**-0.5
    core = grid.bit(1)
    half = grid.bit(grid.far)

    def compact(value):
        mine = lax.dynamic_index_in_dim(value, half, 0, keepdims=False)
        other = lax.dynamic_index_in_dim(value, 1 - half, 0, keepdims=False)
        return jnp.concatenate([mine, grid.swap(other, grid.far)], 0)

    def spread(mine, other):
        mine = mine[: other.shape[0]]
        return jnp.where(half == 0, jnp.stack([mine, other]), jnp.stack([other, mine]))

    def chunks(terms):
        return jnp.split(terms, grid.seq // 2, 0)

    shard = self_output.shape[0]
    self_mixed = jnp.concatenate(
        [low(self_weight[:, :width]), split_pairs(low(self_weight[:, width:]))], 1
    )
    small = jnp.concatenate(
        [
            low(camera_weight).reshape(-1),
            low(view_table).reshape(-1),
            low(mid_gain),
            low(mid_bias),
            low(last_gain),
            low(last_bias),
            low(down_bias),
            low(up_bias),
        ]
    )
    small_sizes = [
        camera_weight.size,
        view_table.size,
        shard,
        shard,
        shard,
        shard,
        shard,
        up_bias.size,
    ]
    patch_rows = patch_weight.shape[0]
    group = grid.seq // 2
    lot = 3 * width // group
    few = width // group
    small_count = -(-small.size // lot)
    small_rows = jnp.pad(small, (0, small_count * lot - small.size)).reshape(-1, lot)
    blocks = jnp.concatenate(
        [
            self_mixed[:, :width].reshape(shard, group, few),
            self_mixed[:, width:].reshape(shard, group, 2 * few),
        ],
        2,
    ).transpose(1, 0, 2)
    blocks = jnp.concatenate(
        [blocks, jnp.broadcast_to(pad_rows(small_rows, -(-small_count // 8) * 8), (group, -(-small_count // 8) * 8, lot))], 1
    )
    patch_room = -(-patch_rows // shard) * shard
    first = jnp.concatenate(
        [
            stack_columns(low(up_weight), width),
            low(down_weight),
            low(self_output),
            low(cross_query),
            low(cross_output),
            stack_columns(split_pairs(low(cross_memory)), width),
            pad_rows(low(patch_weight), patch_room),
        ],
        0,
    )
    own_gather = grid.gather_self(blocks)
    blocks = next(own_gather)
    tokens_all = jnp.concatenate(grid.gather_group(compact(tokens)), 0)
    first = lax.all_gather(first, BOTH, axis=0, tiled=False)
    while isinstance(blocks, list) or blocks.shape[0] < parts:
        blocks = own_gather.send(blocks)
        if isinstance(blocks, list) or blocks.shape[0] == parts // 2:
            break
    blocks, tokens_all, patches, patch_index = together((blocks, tokens_all, patches, patch_index))
    feats_all = jnp.concatenate(grid.gather_group(compact(patches)), 0)
    views_all = jnp.concatenate(grid.gather_group(compact(patch_index)), 0) // VIEW_PATCHES
    blocks = own_gather.send(blocks)
    self_own = blocks[:, :shard].reshape(parts * shard, lot)
    tiny = blocks[:, shard : shard + small_count].reshape(parts, -1)
    pieces = []
    at = 0
    for size in small_sizes:
        pieces.append(tiny[:, at : at + size].astype(f32))
        at += size
    full_camera = pieces[0].reshape(parts, 16, -1).transpose(1, 0, 2).reshape(16, -1)
    full_view = pieces[1].reshape(parts, VIEWS, -1).transpose(1, 0, 2).reshape(VIEWS, -1)
    g_mid, b_mid, g_last, b_last, b_down, b_up = (p.reshape(1, -1) for p in pieces[2:])

    own = tokens_all.shape[0] // (grid.seq // 2)
    slots_own = feats_all.shape[0] // (grid.seq // 2)
    x_all = tokens_all.astype(f32)
    x = x_all[:own]
    camera_mine = lax.dynamic_index_in_dim(camera, half, 0, keepdims=False)
    live = lax.dynamic_index_in_dim(patch_count, half, 0, keepdims=False)
    modulation = jnp.sum(camera_mine[:, None] * full_camera, 0)
    scale1, shift1 = 1.0 + modulation[None, :width], modulation[None, width:]
    hidden_all = low(norm_parts(x_all)[0] * scale1 + shift1)
    triple = low(dot(hidden_all, self_own))
    query = low(triple[:, :few].astype(f32) * factor)
    kv = triple[:, few:]
    query, kv, feats_all, views_all, cotangent = together((query, kv, feats_all, views_all, cotangent))
    attended_own, lse1 = attend(query, kv, None)
    attended_own, first = together((attended_own, first))
    cot = compact(cotangent)
    attended = grid.exchange(jnp.stack(grid.in_order(chunks(attended_own))))

    packed = first

    def square(start, rows=shard):
        start += 2 * down_weight.shape[0]
        return first[:, start : start + rows].reshape(parts * rows, width)

    full_out = square(0)
    full_cq = square(shard)
    full_co = square(2 * shard)
    full_mem = jnp.concatenate([square(3 * shard), square(4 * shard)], 1)
    full_patch = square(5 * shard, patch_rows)
    hot_all = (views_all[:, None] == jnp.arange(VIEWS)[None, :]).astype(f32)
    view_part = sum(hot_all[:, v : v + 1] * full_view[v : v + 1] for v in range(VIEWS))
    embedded_all = low(dot(feats_all, full_patch) + view_part)
    mem = low(dot(embedded_all, full_mem))
    attended, mem = together((attended, mem))
    attended = jnp.concatenate(grid.in_order(attended), 1)
    place = grid.place
    chunk = patches.shape[1]
    lane = jnp.arange(chunk)
    slots = jnp.concatenate(
        [
            chunk * (place ^ d ^ far) + lane
            for d in range(grid.seq // 2)
            for far in (0, grid.far)
        ]
    )
    bias = jnp.where(slots < live, 0.0, -1e30).astype(f32).reshape(1, -1)

    second = x + dot(attended, full_out)
    unit2, rstd2 = norm_parts(second)
    normed = low(unit2 * g_mid + b_mid)
    asked = low(low(dot(normed, full_cq)).astype(f32) * factor)
    crossed, lse2 = attend(asked, mem, bias)
    third = second + dot(crossed, full_co)
    third, cot = together((third, cot))
    core_now = core.reshape(1).astype(jnp.int32)
    result, third_grad, ffn_keep, ffn_send, last_vectors, up_bias_grad = feed_forward(
        core_now, third, cot, g_last, b_last, b_down, b_up, packed, shard
    )
    tall = down_weight.shape[0]

    ffn = grid.scatter(ffn_keep, ffn_send, True)
    ffn_moved = next(ffn)
    half_rows = result.shape[0] // 2
    third_low = low(third_grad)
    crossed_grad = low(dot(third_low, full_co, NT))
    ffn_moved, crossed_grad = together((ffn_moved, crossed_grad))
    ffn_moved = ffn.send(ffn_moved)
    ffn_moved, crossed_grad = together((ffn_moved, crossed_grad))

    ffn_moved = ffn.send(ffn_moved)
    result_moved = grid.swap(result[half_rows:], grid.far)
    asked_grad, mem_terms = attend_back(asked, mem, crossed, crossed_grad, lse2, bias)
    asked_grad, mem_terms, result_moved = together((asked_grad, mem_terms, result_moved))
    normed_grad = dot(asked_grad, full_cq, NT)
    second_grad = third_grad + norm_back(unit2, rstd2, normed_grad * g_mid)
    second_low = low(second_grad)
    attended_grad = low(dot(second_low, full_out, NT))
    embedded_grad = low(dot(mem_terms, full_mem, NT))
    arrays = [
        crossed,
        third_low,
        normed,
        asked_grad,
        attended,
        second_low,
        embedded_all,
        mem_terms,
        feats_all,
        embedded_grad,
    ]
    jobs = ((0, 1, 0), (2, 3, 0), (4, 5, 0), (6, 7, 0), (6, 7, 1), (8, 9, 0))
    attended_grad, arrays = together((attended_grad, arrays))
    grad_moved = []
    for d in range(group):
        at = ((grid.place % group) ^ d) * few
        part = lax.dynamic_slice_in_dim(attended_grad, at, few, 1)
        grad_moved.append(grid.swap(part, d) if d else part)
    keep, send = weight_grads(core_now, arrays, jobs, parts, shard, width)
    grad_moved, keep, send = together((grad_moved, keep, send))
    rest = grid.scatter(keep, send, False)
    moved = next(rest)
    patch_terms = chunks(low(dot(embedded_grad, full_patch, NT)))
    grad_own = jnp.concatenate(grad_moved, 0)
    grad_own, patch_terms, moved = together((grad_own, patch_terms, moved))
    moved = rest.send(moved)
    patch_moved = grid.exchange_core(patch_terms)
    grad_own, patch_moved, moved, ffn_moved = together((grad_own, patch_moved, moved, ffn_moved))

    moved = rest.send(moved)
    ffn_moved = ffn.send(ffn_moved)
    patch_mine, patch_moved = grid.exchange_line(patch_terms, patch_moved)
    query_grad, pair_grad = attend_back(query, kv, attended_own, grad_own, lse1, None)
    patch_moved, query_grad, pair_grad = together((patch_moved, query_grad, pair_grad))

    triple_grad = jnp.concatenate([query_grad, pair_grad], 1)
    hidden_terms = chunks(low(dot(triple_grad, self_own, NT)))
    hidden_terms, triple_grad = together((hidden_terms, triple_grad))
    hidden_moved = grid.exchange_core(hidden_terms)
    self_grad = low(dot(hidden_all, triple_grad, TN))
    self_grad, hidden_moved = together((self_grad, hidden_moved))

    own_scatter = grid.scatter_self(self_grad.reshape(parts, shard, lot))
    own_moved = next(own_scatter)
    hidden_mine, hidden_moved = grid.exchange_line(hidden_terms, hidden_moved)
    patch_low = low(patch_mine.astype(f32) + patch_moved.astype(f32))
    patch_half = patch_low.shape[0] // 2
    patch_moved = grid.swap(patch_low[patch_half:], grid.far)
    result = spread(result, result_moved)
    view_grad = jnp.stack(
        [jnp.sum(hot_all[:, v : v + 1] * embedded_grad.astype(f32), 0) for v in range(VIEWS)]
    )
    mid_vectors = jnp.stack([jnp.sum(normed_grad * unit2, 0), jnp.sum(normed_grad, 0)])
    own_moved, hidden_moved, patch_moved, result, view_grad, mid_vectors, last_vectors, up_bias_grad = together(
        (own_moved, hidden_moved, patch_moved, result, view_grad, mid_vectors, last_vectors, up_bias_grad)
    )

    unit1, rstd1 = norm_parts(together(tokens_all[:own]).astype(f32))
    hidden_grad = hidden_mine.astype(f32) + hidden_moved.astype(f32)
    token_grad = low(second_grad + norm_back(unit1, rstd1, hidden_grad * scale1))
    token_grad, hidden_grad, own_moved, moved, ffn_moved = together(
        (token_grad, hidden_grad, own_moved, moved, ffn_moved)
    )
    token_moved = grid.swap(token_grad[half_rows:], grid.far)
    moved = rest.send(moved)
    own_moved = own_scatter.send(own_moved)
    modulation_grad = jnp.concatenate(
        [jnp.sum(hidden_grad * unit1, 0), jnp.sum(hidden_grad, 0)]
    )
    camera_grad = camera_mine[:, None] * modulation_grad[None]
    vectors = jnp.concatenate(
        [
            view_grad,
            mid_vectors,
            last_vectors[0:3],
        ],
        0,
    )
    small_grad = jnp.concatenate(
        [
            low(camera_grad).reshape(16, parts, -1).transpose(1, 0, 2).reshape(parts, -1),
            low(vectors).reshape(VIEWS + 5, parts, -1).transpose(1, 0, 2).reshape(parts, -1),
            low(up_bias_grad).reshape(parts, -1),
        ],
        1,
    )
    small_grad = jnp.pad(small_grad, ((0, 0), (0, small_count * lot - small_grad.shape[1])))
    small_grad, own_moved, token_moved, moved = together((small_grad, own_moved, token_moved, moved))
    while not isinstance(own_moved, list):
        own_moved = own_scatter.send(own_moved)
        if own_moved.shape[0] == group:
            break
    moved = rest.send(moved)
    small_grad = lax.all_to_all(small_grad.reshape(parts, small_count, lot), BOTH, 0, 0, tiled=True)
    token_grad = spread(token_grad, token_moved)
    ffn_grad = ffn.send(ffn_moved)
    ffn_up, ffn_down = unstack_columns(ffn_grad[:tall], shard), ffn_grad[tall:]
    patch_grad = spread(patch_low, patch_moved)
    own_moved, moved, token_grad, small_grad, patch_grad, ffn_up, ffn_down = together(
        (own_moved, moved, token_grad, small_grad, patch_grad, ffn_up, ffn_down)
    )
    own_moved = own_scatter.send(own_moved)
    tiny = jnp.sum(small_grad.astype(f32), 0).reshape(-1)
    rest_sum = rest.send(moved)
    self_sum = own_scatter.send(own_moved).astype(f32)
    pieces = []
    at = 0
    for size in small_sizes:
        pieces.append(tiny[at : at + size])
        at += size
    self_sum = jnp.concatenate(
        [
            self_sum[:, :, :few].reshape(shard, width),
            join_pairs(self_sum[:, :, few:].reshape(shard, 2 * width)),
        ],
        1,
    )
    return (
        result,
        token_grad,
        patch_grad,
        pieces[0].reshape(camera_weight.shape),
        self_sum,
        rest_sum[2 * shard : 3 * shard],
        pieces[2],
        pieces[3],
        rest_sum[5 * shard : 5 * shard + patch_rows],
        pieces[1].reshape(view_table.shape),
        rest_sum[shard : 2 * shard],
        join_pairs(unstack_columns(rest_sum[3 * shard : 5 * shard], shard)),
        rest_sum[:shard],
        pieces[4],
        pieces[5],
        ffn_up,
        pieces[7],
        ffn_down,
        pieces[6],
    )


def solution(mesh):
    line = mesh.shape["seq"] // 2
    mesh = jax.sharding.Mesh(
        mesh.devices.reshape(mesh.shape["obj"], line, 2), ("obj", "ring", "core")
    )
    rows, flat, lanes = P(BOTH, None), P(BOTH), P(None, BOTH)
    sequence = P("obj", SEQ, None)
    in_specs = (
        sequence,
        P("obj", None),
        sequence,
        P("obj"),
        P("obj", SEQ),
        sequence,
        lanes,
        rows,
        rows,
        flat,
        flat,
        rows,
        lanes,
        rows,
        rows,
        rows,
        flat,
        flat,
        rows,
        flat,
        rows,
        flat,
    )
    out_specs = (
        sequence,
        sequence,
        sequence,
        lanes,
        rows,
        rows,
        flat,
        flat,
        rows,
        lanes,
        rows,
        rows,
        rows,
        flat,
        flat,
        rows,
        flat,
        rows,
        flat,
    )
    return jax.shard_map(
        partial(on_device, mesh),
        mesh=mesh,
        in_specs=in_specs,
        out_specs=out_specs,
        check_vma=False,
    )
```

```python
from functools import partial

import jax
import jax.numpy as jnp
from jax import lax
from jax.experimental import pallas as pl
from jax.experimental.pallas import tpu as pltpu
from jax.sharding import PartitionSpec as P

HEAD_DIM = 64
PAIR = 2 * HEAD_DIM
VIEWS = 4
VIEW_PATCHES = 1024
BOTH = ("obj", "ring", "core")
SEQ = ("ring", "core")

epsilon = 1e-05
f32 = jnp.float32
bf16 = jnp.bfloat16
NN = (((1,), (0,)), ((), ()))
NT = (((1,), (1,)), ((), ()))
TN = (((0,), (0,)), ((), ()))


def dot(left, right, dims=NN):
    return lax.dot_general(left, right, dims, preferred_element_type=f32)


def params(megabytes=56):
    return pltpu.CompilerParams(vmem_limit_bytes=megabytes * 2**20)


def norm_parts(values):
    center = values - jnp.mean(values, -1, keepdims=True)
    spread = jnp.mean(center * center, -1, keepdims=True)
    scale = lax.rsqrt(spread + epsilon)
    return center * scale, scale


def norm_back(unit, scale, grad):
    return scale * (
        grad - jnp.mean(grad, -1, keepdims=True) - unit * jnp.mean(grad * unit, -1, keepdims=True)
    )


def attend_kernel(masked, *refs):
    q_ref, kv_ref = refs[:2]
    bias = refs[2] if masked else None
    o_ref, lse_ref = refs[-2:]
    query = q_ref[...]
    keys, values = kv_ref[:, :PAIR], kv_ref[:, PAIR:]
    low = lax.broadcasted_iota(jnp.int32, query.shape, 1) < HEAD_DIM
    outs, lses = [], []
    for head in range(2):
        mine = low if head == 0 else ~low
        score = dot(jnp.where(mine, query, jnp.zeros_like(query)), keys, NT)
        if masked:
            score = score + bias[...]
        top = jnp.max(score, 1, keepdims=True)
        lifted = jnp.exp(score - top)
        total = jnp.sum(lifted, 1, keepdims=True)
        outs.append(dot(lifted.astype(bf16), values) * (1.0 / total))
        lses.append(top + jnp.log(total))
    o_ref[...] = jnp.where(low, outs[0], outs[1]).astype(bf16)
    lse_ref[...] = jnp.where(low, lses[0], lses[1])[None]


def attend(query, kv, bias):
    rows, width = query.shape
    slots, pairs = kv.shape[0], width // PAIR
    tile = min(rows, 384)
    row = pl.BlockSpec((tile, PAIR), lambda i, r: (r, i))
    masked = bias is not None
    return pl.pallas_call(
        partial(attend_kernel, masked),
        grid=(pairs, rows // tile),
        in_specs=[row, pl.BlockSpec((slots, 2 * PAIR), lambda i, r: (0, i))]
        + [pl.BlockSpec((1, slots), lambda i, r: (0, 0))] * masked,
        out_specs=[row, pl.BlockSpec((1, tile, PAIR), lambda i, r: (i, r, 0))],
        out_shape=[
            jax.ShapeDtypeStruct((rows, width), bf16),
            jax.ShapeDtypeStruct((pairs, rows, PAIR), f32),
        ],
        compiler_params=params(),
        name="attend",
        cost_estimate=pl.CostEstimate(
            flops=16 * rows * slots * width,
            bytes_accessed=4 * width * (rows + slots),
            transcendentals=2 * pairs * rows * slots,
        ),
    )(query, kv, *([bias] if masked else []))


def attend_back_kernel(masked, *refs):
    q_ref, kv_ref, o_ref, do_ref, lse_ref = refs[:5]
    bias = refs[5] if masked else None
    dq_ref, dkv_ref, dk_s, dv_s = refs[-4:]
    query, grad = q_ref[...], do_ref[...]
    keys, values = kv_ref[:, :PAIR], kv_ref[:, PAIR:]
    low = lax.broadcasted_iota(jnp.int32, query.shape, 1) < HEAD_DIM
    lse = lse_ref[0]
    product = o_ref[...].astype(f32) * grad.astype(f32)
    dk = dv = 0.0
    dqs = []
    for head in range(2):
        mine = low if head == 0 else ~low
        head_query = jnp.where(mine, query, jnp.zeros_like(query))
        head_grad = jnp.where(mine, grad, jnp.zeros_like(grad))
        score = dot(head_query, keys, NT)
        if masked:
            score = score + bias[...]
        probs = jnp.exp(score - lse[:, HEAD_DIM * head : HEAD_DIM * head + 1])
        delta = jnp.sum(jnp.where(mine, product, 0.0), 1, keepdims=True)
        score_grad = (probs * (dot(head_grad, values, NT) - delta)).astype(bf16)
        dk = dk + dot(jnp.transpose(head_query), score_grad)
        dv = dv + dot(jnp.transpose(head_grad), probs.astype(bf16))
        dqs.append(dot(score_grad, keys))
    dq_ref[...] = (jnp.where(low, dqs[0], dqs[1]) * HEAD_DIM**-0.5).astype(bf16)
    step = pl.program_id(1)

    @pl.when(step == 0)
    def _():
        dk_s[...] = dk
        dv_s[...] = dv

    @pl.when(step > 0)
    def _():
        dk_s[...] += dk
        dv_s[...] += dv

    @pl.when(step == pl.num_programs(1) - 1)
    def _():
        dkv_ref[:, :PAIR] = jnp.transpose(dk_s[...]).astype(bf16)
        dkv_ref[:, PAIR:] = jnp.transpose(dv_s[...]).astype(bf16)


def attend_back(query, kv, out, grad, lse, bias):
    rows, width = query.shape
    slots, pairs = kv.shape[0], width // PAIR
    tile = min(rows, 384)
    row = pl.BlockSpec((tile, PAIR), lambda i, r: (r, i))
    slot = pl.BlockSpec((slots, 2 * PAIR), lambda i, r: (0, i))
    masked = bias is not None
    return pl.pallas_call(
        partial(attend_back_kernel, masked),
        grid=(pairs, rows // tile),
        in_specs=[row, slot, row, row, pl.BlockSpec((1, tile, PAIR), lambda i, r: (i, r, 0))]
        + [pl.BlockSpec((1, slots), lambda i, r: (0, 0))] * masked,
        out_specs=[row, slot],
        out_shape=[
            jax.ShapeDtypeStruct((rows, width), bf16),
            jax.ShapeDtypeStruct((slots, 2 * width), bf16),
        ],
        scratch_shapes=[pltpu.VMEM((PAIR, slots), f32)] * 2,
        compiler_params=params(),
        name="attend_back",
        cost_estimate=pl.CostEstimate(
            flops=40 * rows * slots * width,
            bytes_accessed=8 * width * (rows + slots),
            transcendentals=2 * pairs * rows * slots,
        ),
    )(query, kv, out, grad, lse, *([bias] if masked else []))


def block_kernel(core_ref, third_ref, cot_ref, gain_ref, shift_ref, dbias_ref, ubias_ref, up_ref, down_ref,
                 result_ref, tgrad_ref, keep_ref, send_ref, vec_ref, ubgrad_ref,
                 unit_s, final_s, final_t, out_s, fgrad_s, scale_s, wide_s, tall_s, sems):
    step = pl.program_id(0)
    last = pl.num_programs(0) - 1
    slot = lax.rem(step, 2)
    core = core_ref[0]
    _, _, half, shard, tile = wide_s.shape
    _, _, few, tall, width = tall_s.shape
    per = width // tile

    def copies(at, place):
        row = pl.multiple_of((at // per) * shard, shard)
        lane = pl.multiple_of(lax.rem(at, per) * tile, tile)
        found = []
        for which, ref in enumerate((keep_ref, send_ref)):
            found += [
                pltpu.make_async_copy(
                    wide_s.at[place, which],
                    ref.at[:, pl.ds(row, shard), pl.ds(lane, tile)],
                    sems.at[which, place],
                ),
                pltpu.make_async_copy(
                    tall_s.at[place, which],
                    ref.at[pl.ds(at * few, few), pl.ds(tall, tall), :],
                    sems.at[2 + which, place],
                ),
            ]
        return found

    @pl.when(step == 0)
    def _():
        unit, scale = norm_parts(third_ref[...])
        unit_s[...] = unit
        scale_s[...] = scale
        final = (unit * gain_ref[...] + shift_ref[...]).astype(bf16)
        final_s[...] = final
        final_t[...] = jnp.transpose(final)
        out_s[...] = jnp.zeros_like(out_s)
        fgrad_s[...] = jnp.zeros_like(fgrad_s)

    @pl.when(step >= 2)
    def _():
        for copy in copies(step - 2, slot):
            copy.wait()

    cot = cot_ref[...]
    up = up_ref[...].reshape(-1, up_ref.shape[-1])
    down = down_ref[...].reshape(-1, down_ref.shape[-1])
    upper = dot(final_s[...], up) + ubias_ref[...]
    cdf = 0.5 * (1.0 + lax.erf(upper * (0.5**0.5)))
    active = (upper * cdf).astype(bf16)
    slope = cdf + upper * (jnp.exp(-0.5 * upper * upper) * 0.3989422804014327)
    ugrad = (slope * dot(cot, down, NT)).astype(bf16)
    out_s[...] += dot(active, down)
    fgrad_s[...] += dot(ugrad, up, NT)
    ubgrad_ref[...] = jnp.sum(ugrad.astype(f32), 0, keepdims=True)
    wide = dot(final_t[...], ugrad).astype(bf16).reshape(half, 2, shard, tile)
    wide_s[slot, core] = wide[:, 0]
    wide_s[slot, 1 - core] = wide[:, 1]
    slim = dot(jnp.transpose(active), cot).astype(bf16).reshape(few, 2, tall, width)
    tall_s[slot, core] = slim[:, 0]
    tall_s[slot, 1 - core] = slim[:, 1]
    for copy in copies(step, slot):
        copy.start()

    @pl.when(step == last)
    def _():
        result_ref[...] = (third_ref[...] + (out_s[...] + dbias_ref[...])).astype(bf16)
        unit, fgrad, cotf = unit_s[...], fgrad_s[...], cot.astype(f32)
        tgrad_ref[...] = cotf + norm_back(unit, scale_s[...], fgrad * gain_ref[...])
        vec_ref[...] = jnp.zeros_like(vec_ref)
        vec_ref[0:1, :] = jnp.sum(fgrad * unit, 0, keepdims=True)
        vec_ref[1:2, :] = jnp.sum(fgrad, 0, keepdims=True)
        vec_ref[2:3, :] = jnp.sum(cotf, 0, keepdims=True)
        for copy in copies(step - 1, 1 - slot) + copies(step, slot):
            copy.wait()


def feed_forward(core, third, cot, gain, shift, down_bias, up_bias, packed, shard):
    rows, width = third.shape
    parts = packed.shape[0]
    hidden = up_bias.shape[1]
    tile = 512
    per = width // tile
    tall = hidden // parts
    spread = tile // tall
    steps = hidden // tile
    whole = lambda shape: pl.BlockSpec(shape, lambda j, c: (0,) * len(shape))
    return pl.pallas_call(
        block_kernel,
        grid_spec=pltpu.PrefetchScalarGridSpec(
            num_scalar_prefetch=1,
            grid=(steps,),
            in_specs=[
                whole((rows, width)),
                whole((rows, width)),
                whole((1, width)),
                whole((1, width)),
                whole((1, width)),
                pl.BlockSpec((1, tile), lambda j, c: (0, j)),
                pl.BlockSpec((parts, shard, tile), lambda j, c: (0, j // per, j % per)),
                pl.BlockSpec((spread, tall, width), lambda j, c: (j, 1, 0)),
            ],
            out_specs=[
                whole((rows, width)),
                whole((rows, width)),
                pl.BlockSpec(memory_space=pl.ANY),
                pl.BlockSpec(memory_space=pl.ANY),
                whole((8, width)),
                pl.BlockSpec((1, tile), lambda j, c: (0, j)),
            ],
            scratch_shapes=[
                pltpu.VMEM((rows, width), f32),
                pltpu.VMEM((rows, width), bf16),
                pltpu.VMEM((width, rows), bf16),
                pltpu.VMEM((rows, width), f32),
                pltpu.VMEM((rows, width), f32),
                pltpu.VMEM((rows, 1), f32),
                pltpu.VMEM((2, 2, parts // 2, shard, tile), bf16),
                pltpu.VMEM((2, 2, spread // 2, tall, width), bf16),
                pltpu.SemaphoreType.DMA((4, 2)),
            ],
        ),
        out_shape=[
            jax.ShapeDtypeStruct((rows, width), bf16),
            jax.ShapeDtypeStruct((rows, width), f32),
            jax.ShapeDtypeStruct((parts // 2, 2 * tall, width), bf16),
            jax.ShapeDtypeStruct((parts // 2, 2 * tall, width), bf16),
            jax.ShapeDtypeStruct((8, width), f32),
            jax.ShapeDtypeStruct((1, hidden), f32),
        ],
        compiler_params=params(),
        name="feed_forward",
        cost_estimate=pl.CostEstimate(flops=1, bytes_accessed=1, transcendentals=0),
    )(core, third, cot, gain, shift, down_bias, up_bias, packed, packed)


def grads_kernel(jobs, core_ref, *refs):
    ins, (keep_ref, send_ref) = refs[:-2], refs[-2:]
    step = pl.program_id(0)
    half, room, width = keep_ref.shape

    def store(block, rows):
        block = block.astype(bf16).reshape(half, 2, rows, width)
        keep_ref[:, :rows] = block[:, 0]
        send_ref[:, :rows] = block[:, 1]

    def swapped(block, rows):
        block = block.astype(bf16).reshape(half, 2, rows, width)
        keep_ref[:, :rows] = block[:, 1]
        send_ref[:, :rows] = block[:, 0]

    for at, (left, right, column) in enumerate(jobs):

        @pl.when(step == at)
        def _():
            rows = ins[left].shape[1] // (2 * half)
            if rows < room:
                keep_ref[...] = jnp.zeros_like(keep_ref)
                send_ref[...] = jnp.zeros_like(send_ref)
            block = dot(ins[left][...], ins[right][:, column * width : (column + 1) * width], TN)

            @pl.when(core_ref[0] == 0)
            def _():
                store(block, rows)

            @pl.when(core_ref[0] == 1)
            def _():
                swapped(block, rows)


def weight_grads(core, arrays, jobs, parts, shard, width):
    count = len(jobs)
    whole = lambda array: pl.BlockSpec(array.shape, lambda j, c: (0, 0))
    out = pl.BlockSpec((parts // 2, shard, width), lambda j, c: (0, j, 0))
    flops = sum(2 * arrays[i].shape[0] * arrays[i].shape[1] * width for i, _, _ in jobs)
    return pl.pallas_call(
        partial(grads_kernel, jobs),
        grid_spec=pltpu.PrefetchScalarGridSpec(
            num_scalar_prefetch=1,
            grid=(count,),
            in_specs=[whole(array) for array in arrays],
            out_specs=[out, out],
        ),
        out_shape=[jax.ShapeDtypeStruct((parts // 2, count * shard, width), bf16)] * 2,
        compiler_params=params(),
        name="weight_grads",
        cost_estimate=pl.CostEstimate(flops=1, bytes_accessed=1, transcendentals=0),
    )(core, *arrays)


class Grid:
    def __init__(self, mesh):
        self.obj, self.seq = mesh.shape["obj"], mesh.shape["ring"] * 2
        self.all = self.obj * self.seq
        self.place = lax.axis_index("ring") * 2 + lax.axis_index("core")
        self.me = lax.axis_index("obj") * self.seq + self.place
        self.group = [m for m in (1 << k for k in range(20)) if m < self.seq // 2]
        self.far = self.seq // 2

    def swap(self, value, mask):
        return lax.ppermute(value, BOTH, [(i, i ^ mask) for i in range(self.all)])

    def bit(self, mask):
        return (self.me // mask) % 2

    def gather_group(self, value):
        found = {0: value}
        for mask in self.group[1:][::-1] + self.group[:1]:
            found.update({d ^ mask: self.swap(v, mask) for d, v in list(found.items())})
        return [found[d] for d in range(self.seq // 2)]

    def in_order(self, terms):
        spot = self.place % len(terms)
        stacked = jnp.stack(terms)
        return [
            lax.dynamic_index_in_dim(stacked, spot ^ j, 0, keepdims=False) for j in range(len(terms))
        ]

    def exchange(self, blocks):
        spot = self.place % blocks.shape[0]
        found = []
        for d in range(blocks.shape[0]):
            block = lax.dynamic_index_in_dim(blocks, spot ^ d, 0, keepdims=False)
            found.append(self.swap(block, d) if d else block)
        return found

    def gather_self(self, blocks):
        found = yield self.exchange(blocks)
        found = jnp.stack(self.in_order(found))
        for mask in [m for m in (1 << k for k in range(20)) if self.far <= m < self.all]:
            moved = yield self.swap(found, mask)
            found = jnp.where(
                self.bit(mask) == 0, jnp.concatenate([found, moved]), jnp.concatenate([moved, found])
            )
        yield found

    def scatter_self(self, grad):
        terms = [grad]
        for mask in [m for m in (1 << k for k in range(20)) if self.far <= m < self.all][::-1]:
            terms = [t.reshape(2, t.shape[0] // 2, *t.shape[1:]) for t in terms]
            pick = lambda t, which: lax.dynamic_index_in_dim(t, which, 0, keepdims=False)
            moved = yield self.swap(add([pick(t, 1 - self.bit(mask)) for t in terms]), mask)
            terms = [pick(t, self.bit(mask)) for t in terms] + [moved]
        found = yield self.exchange(add(terms))
        yield jnp.stack(self.in_order(found), 1)

    def scatter(self, keep, send, whole):
        moved = yield self.swap(send, 1)
        total = add([keep, moved]).reshape(self.obj, self.seq // 2, *keep.shape[1:])
        total = yield total
        total = yield lax.psum_scatter(total, "obj", scatter_dimension=0, tiled=False)
        if whole:
            moved = yield lax.all_to_all(total, "ring", 0, 0, tiled=True)
            yield jnp.sum(moved.astype(f32), 0)
            return
        terms = [total]
        for mask in self.group[1:] + [self.far]:
            terms = [t.reshape(t.shape[0] // 2, 2, *t.shape[1:]) for t in terms]
            pick = lambda t, which: lax.dynamic_index_in_dim(t, which, 1, keepdims=False)
            moved = self.swap(add([pick(t, 1 - self.bit(mask)) for t in terms]), mask)
            if 4 * mask >= self.seq:
                moved = yield moved
            terms = [pick(t, self.bit(mask)) for t in terms] + [moved]
        yield sum(t[0].astype(f32) for t in terms)

    def exchange_core(self, terms):
        return [self.swap(t, 1) for t in terms[1::2]]

    def exchange_line(self, terms, moved):
        pairs = [add([t, m]) for t, m in zip(terms[::2], moved)]
        step = len(pairs) // 2
        while step > 1:
            pairs = [add([pairs[k], self.swap(pairs[k + step], 2 * step)]) for k in range(step)]
            step //= 2
        return pairs[0], self.swap(pairs[1], 2)


together = lax.optimization_barrier


def add(terms):
    if len(terms) == 1:
        return terms[0]
    return sum(t.astype(f32) for t in terms).astype(bf16)


def split_pairs(matrix):
    rows, width = matrix.shape
    return matrix.reshape(rows, 2, width // (2 * PAIR), PAIR).transpose(0, 2, 1, 3).reshape(rows, width)


def join_pairs(matrix):
    rows, width = matrix.shape
    return matrix.reshape(rows, width // (2 * PAIR), 2, PAIR).transpose(0, 2, 1, 3).reshape(rows, width)


def stack_columns(matrix, width):
    rows = matrix.shape[0]
    return matrix.reshape(rows, -1, width).transpose(1, 0, 2).reshape(-1, width)


def unstack_columns(matrix, rows):
    width = matrix.shape[1]
    return matrix.reshape(-1, rows, width).transpose(1, 0, 2).reshape(rows, -1)


def pad_rows(matrix, rows):
    return jnp.pad(matrix, ((0, rows - matrix.shape[0]), (0, 0)))


def on_device(
    mesh,
    tokens,
    camera,
    patches,
    patch_count,
    patch_index,
    cotangent,
    camera_weight,
    self_weight,
    self_output,
    mid_gain,
    mid_bias,
    patch_weight,
    view_table,
    cross_query,
    cross_memory,
    cross_output,
    last_gain,
    last_bias,
    up_weight,
    up_bias,
    down_weight,
    down_bias,
):
    grid = Grid(mesh)
    parts = grid.all
    width = self_output.shape[1]
    low = lambda v: v.astype(bf16)
    factor = HEAD_DIM**-0.5
    core = grid.bit(1)
    half = grid.bit(grid.far)

    def compact(value):
        mine = lax.dynamic_index_in_dim(value, half, 0, keepdims=False)
        other = lax.dynamic_index_in_dim(value, 1 - half, 0, keepdims=False)
        return jnp.concatenate([mine, grid.swap(other, grid.far)], 0)

    def spread(mine, other):
        mine = mine[: other.shape[0]]
        return jnp.where(half == 0, jnp.stack([mine, other]), jnp.stack([other, mine]))

    def chunks(terms):
        return jnp.split(terms, grid.seq // 2, 0)

    shard = self_output.shape[0]
    self_mixed = jnp.concatenate(
        [low(self_weight[:, :width]), split_pairs(low(self_weight[:, width:]))], 1
    )
    small = jnp.concatenate(
        [
            low(camera_weight).reshape(-1),
            low(view_table).reshape(-1),
            low(mid_gain),
            low(mid_bias),
            low(last_gain),
            low(last_bias),
            low(down_bias),
            low(up_bias),
        ]
    )
    small_sizes = [
        camera_weight.size,
        view_table.size,
        shard,
        shard,
        shard,
        shard,
        shard,
        up_bias.size,
    ]
    patch_rows = patch_weight.shape[0]
    group = grid.seq // 2
    lot = 3 * width // group
    few = width // group
    small_count = -(-small.size // lot)
    small_rows = jnp.pad(small, (0, small_count * lot - small.size)).reshape(-1, lot)
    blocks = jnp.concatenate(
        [
            self_mixed[:, :width].reshape(shard, group, few),
            self_mixed[:, width:].reshape(shard, group, 2 * few),
        ],
        2,
    ).transpose(1, 0, 2)
    blocks = jnp.concatenate(
        [blocks, jnp.broadcast_to(pad_rows(small_rows, -(-small_count // 8) * 8), (group, -(-small_count // 8) * 8, lot))], 1
    )
    patch_room = -(-patch_rows // shard) * shard
    first = jnp.concatenate(
        [
            stack_columns(low(up_weight), width),
            low(down_weight),
            low(self_output),
            low(cross_query),
            low(cross_output),
            stack_columns(split_pairs(low(cross_memory)), width),
            pad_rows(low(patch_weight), patch_room),
        ],
        0,
    )
    own_gather = grid.gather_self(blocks)
    blocks = next(own_gather)
    tokens_all = jnp.concatenate(grid.gather_group(compact(tokens)), 0)
    first = lax.all_gather(first, BOTH, axis=0, tiled=False)
    while isinstance(blocks, list) or blocks.shape[0] < parts:
        blocks = own_gather.send(blocks)
        if isinstance(blocks, list) or blocks.shape[0] == parts // 2:
            break
    blocks, tokens_all, patches, patch_index = together((blocks, tokens_all, patches, patch_index))
    feats_all = jnp.concatenate(grid.gather_group(compact(patches)), 0)
    views_all = jnp.concatenate(grid.gather_group(compact(patch_index)), 0) // VIEW_PATCHES
    blocks = own_gather.send(blocks)
    self_own = blocks[:, :shard].reshape(parts * shard, lot)
    tiny = blocks[:, shard : shard + small_count].reshape(parts, -1)
    pieces = []
    at = 0
    for size in small_sizes:
        pieces.append(tiny[:, at : at + size].astype(f32))
        at += size
    full_camera = pieces[0].reshape(parts, 16, -1).transpose(1, 0, 2).reshape(16, -1)
    full_view = pieces[1].reshape(parts, VIEWS, -1).transpose(1, 0, 2).reshape(VIEWS, -1)
    g_mid, b_mid, g_last, b_last, b_down, b_up = (p.reshape(1, -1) for p in pieces[2:])

    own = tokens_all.shape[0] // (grid.seq // 2)
    slots_own = feats_all.shape[0] // (grid.seq // 2)
    x_all = tokens_all.astype(f32)
    x = x_all[:own]
    camera_mine = lax.dynamic_index_in_dim(camera, half, 0, keepdims=False)
    live = lax.dynamic_index_in_dim(patch_count, half, 0, keepdims=False)
    modulation = jnp.sum(camera_mine[:, None] * full_camera, 0)
    scale1, shift1 = 1.0 + modulation[None, :width], modulation[None, width:]
    hidden_all = low(norm_parts(x_all)[0] * scale1 + shift1)
    triple = low(dot(hidden_all, self_own))
    query = low(triple[:, :few].astype(f32) * factor)
    kv = triple[:, few:]
    query, kv, feats_all, views_all, cotangent = together((query, kv, feats_all, views_all, cotangent))
    attended_own, lse1 = attend(query, kv, None)
    attended_own, first = together((attended_own, first))
    attended = grid.exchange(jnp.stack(grid.in_order(chunks(attended_own))))

    packed = first

    def square(start, rows=shard):
        start += 2 * down_weight.shape[0]
        return first[:, start : start + rows].reshape(parts * rows, width)

    full_out = square(0)
    full_cq = square(shard)
    full_co = square(2 * shard)
    full_mem = jnp.concatenate([square(3 * shard), square(4 * shard)], 1)
    full_patch = square(5 * shard, patch_rows)
    hot_all = (views_all[:, None] == jnp.arange(VIEWS)[None, :]).astype(f32)
    view_part = sum(hot_all[:, v : v + 1] * full_view[v : v + 1] for v in range(VIEWS))
    embedded_all = low(dot(feats_all, full_patch) + view_part)
    mem = low(dot(embedded_all, full_mem))
    attended, mem = together((attended, mem))
    attended = jnp.concatenate(grid.in_order(attended), 1)
    place = grid.place
    chunk = patches.shape[1]
    lane = jnp.arange(chunk)
    slots = jnp.concatenate(
        [
            chunk * (place ^ d ^ far) + lane
            for d in range(grid.seq // 2)
            for far in (0, grid.far)
        ]
    )
    bias = jnp.where(slots < live, 0.0, -1e30).astype(f32).reshape(1, -1)

    second = x + dot(attended, full_out)
    unit2, rstd2 = norm_parts(second)
    normed = low(unit2 * g_mid + b_mid)
    asked = low(low(dot(normed, full_cq)).astype(f32) * factor)
    asked, cotangent = together((asked, cotangent))
    cot = compact(cotangent)
    crossed, lse2 = attend(asked, mem, bias)
    third = second + dot(crossed, full_co)
    third, cot = together((third, cot))
    core_now = core.reshape(1).astype(jnp.int32)
    result, third_grad, ffn_keep, ffn_send, last_vectors, up_bias_grad = feed_forward(
        core_now, third, cot, g_last, b_last, b_down, b_up, packed, shard
    )
    tall = down_weight.shape[0]

    ffn = grid.scatter(ffn_keep, ffn_send, True)
    ffn_moved = next(ffn)
    half_rows = result.shape[0] // 2
    third_low = low(third_grad)
    crossed_grad = low(dot(third_low, full_co, NT))
    ffn_moved, crossed_grad = together((ffn_moved, crossed_grad))
    ffn_moved = ffn.send(ffn_moved)
    ffn_moved, crossed_grad = together((ffn_moved, crossed_grad))

    ffn_moved = ffn.send(ffn_moved)
    result_moved = grid.swap(result[half_rows:], grid.far)
    asked_grad, mem_terms = attend_back(asked, mem, crossed, crossed_grad, lse2, bias)
    asked_grad, mem_terms, result_moved = together((asked_grad, mem_terms, result_moved))
    normed_grad = dot(asked_grad, full_cq, NT)
    second_grad = third_grad + norm_back(unit2, rstd2, normed_grad * g_mid)
    second_low = low(second_grad)
    attended_grad = low(dot(second_low, full_out, NT))
    embedded_grad = low(dot(mem_terms, full_mem, NT))
    arrays = [
        crossed,
        third_low,
        normed,
        asked_grad,
        attended,
        second_low,
        embedded_all,
        mem_terms,
        feats_all,
        embedded_grad,
    ]
    jobs = ((0, 1, 0), (2, 3, 0), (4, 5, 0), (6, 7, 0), (6, 7, 1), (8, 9, 0))
    attended_grad, arrays = together((attended_grad, arrays))
    grad_moved = []
    for d in range(group):
        at = ((grid.place % group) ^ d) * few
        part = lax.dynamic_slice_in_dim(attended_grad, at, few, 1)
        grad_moved.append(grid.swap(part, d) if d else part)
    keep, send = weight_grads(core_now, arrays, jobs, parts, shard, width)
    grad_moved, keep, send = together((grad_moved, keep, send))
    rest = grid.scatter(keep, send, False)
    moved = next(rest)
    patch_terms = chunks(low(dot(embedded_grad, full_patch, NT)))
    grad_own = jnp.concatenate(grad_moved, 0)
    grad_own, patch_terms, moved = together((grad_own, patch_terms, moved))
    moved = rest.send(moved)
    patch_moved = grid.exchange_core(patch_terms)
    grad_own, patch_moved, moved, ffn_moved = together((grad_own, patch_moved, moved, ffn_moved))

    moved = rest.send(moved)
    ffn_moved = ffn.send(ffn_moved)
    patch_mine, patch_moved = grid.exchange_line(patch_terms, patch_moved)
    query_grad, pair_grad = attend_back(query, kv, attended_own, grad_own, lse1, None)
    patch_moved, query_grad, pair_grad = together((patch_moved, query_grad, pair_grad))

    triple_grad = jnp.concatenate([query_grad, pair_grad], 1)
    hidden_terms = chunks(low(dot(triple_grad, self_own, NT)))
    hidden_terms, triple_grad = together((hidden_terms, triple_grad))
    hidden_moved = grid.exchange_core(hidden_terms)
    self_grad = low(dot(hidden_all, triple_grad, TN))
    self_grad, hidden_moved = together((self_grad, hidden_moved))

    own_scatter = grid.scatter_self(self_grad.reshape(parts, shard, lot))
    own_moved = next(own_scatter)
    hidden_mine, hidden_moved = grid.exchange_line(hidden_terms, hidden_moved)
    patch_low = low(patch_mine.astype(f32) + patch_moved.astype(f32))
    patch_half = patch_low.shape[0] // 2
    patch_moved = grid.swap(patch_low[patch_half:], grid.far)
    result = spread(result, result_moved)
    view_grad = jnp.stack(
        [jnp.sum(hot_all[:, v : v + 1] * embedded_grad.astype(f32), 0) for v in range(VIEWS)]
    )
    mid_vectors = jnp.stack([jnp.sum(normed_grad * unit2, 0), jnp.sum(normed_grad, 0)])
    own_moved, hidden_moved, patch_moved, result, view_grad, mid_vectors, last_vectors, up_bias_grad = together(
        (own_moved, hidden_moved, patch_moved, result, view_grad, mid_vectors, last_vectors, up_bias_grad)
    )

    unit1, rstd1 = norm_parts(together(tokens_all[:own]).astype(f32))
    hidden_grad = hidden_mine.astype(f32) + hidden_moved.astype(f32)
    token_grad = low(second_grad + norm_back(unit1, rstd1, hidden_grad * scale1))
    token_grad, hidden_grad, own_moved, moved, ffn_moved = together(
        (token_grad, hidden_grad, own_moved, moved, ffn_moved)
    )
    token_moved = grid.swap(token_grad[half_rows:], grid.far)
    moved = rest.send(moved)
    own_moved = own_scatter.send(own_moved)
    modulation_grad = jnp.concatenate(
        [jnp.sum(hidden_grad * unit1, 0), jnp.sum(hidden_grad, 0)]
    )
    camera_grad = camera_mine[:, None] * modulation_grad[None]
    vectors = jnp.concatenate(
        [
            view_grad,
            mid_vectors,
            last_vectors[0:3],
        ],
        0,
    )
    small_grad = jnp.concatenate(
        [
            low(camera_grad).reshape(16, parts, -1).transpose(1, 0, 2).reshape(parts, -1),
            low(vectors).reshape(VIEWS + 5, parts, -1).transpose(1, 0, 2).reshape(parts, -1),
            low(up_bias_grad).reshape(parts, -1),
        ],
        1,
    )
    small_grad = jnp.pad(small_grad, ((0, 0), (0, small_count * lot - small_grad.shape[1])))
    small_grad, own_moved, token_moved, moved = together((small_grad, own_moved, token_moved, moved))
    while not isinstance(own_moved, list):
        own_moved = own_scatter.send(own_moved)
        if own_moved.shape[0] == group:
            break
    moved = rest.send(moved)
    small_grad = lax.all_to_all(small_grad.reshape(parts, small_count, lot), BOTH, 0, 0, tiled=True)
    token_grad = spread(token_grad, token_moved)
    ffn_grad = ffn.send(ffn_moved)
    ffn_up, ffn_down = unstack_columns(ffn_grad[:tall], shard), ffn_grad[tall:]
    patch_grad = spread(patch_low, patch_moved)
    own_moved = own_scatter.send(own_moved)
    own_moved, moved, token_grad, small_grad, patch_grad, ffn_up, ffn_down = together(
        (own_moved, moved, token_grad, small_grad, patch_grad, ffn_up, ffn_down)
    )
    tiny = jnp.sum(small_grad.astype(f32), 0).reshape(-1)
    rest_sum = rest.send(moved)
    self_sum = own_scatter.send(own_moved).astype(f32)
    pieces = []
    at = 0
    for size in small_sizes:
        pieces.append(tiny[at : at + size])
        at += size
    self_sum = jnp.concatenate(
        [
            self_sum[:, :, :few].reshape(shard, width),
            join_pairs(self_sum[:, :, few:].reshape(shard, 2 * width)),
        ],
        1,
    )
    return (
        result,
        token_grad,
        patch_grad,
        pieces[0].reshape(camera_weight.shape),
        self_sum,
        rest_sum[2 * shard : 3 * shard],
        pieces[2],
        pieces[3],
        rest_sum[5 * shard : 5 * shard + patch_rows],
        pieces[1].reshape(view_table.shape),
        rest_sum[shard : 2 * shard],
        join_pairs(unstack_columns(rest_sum[3 * shard : 5 * shard], shard)),
        rest_sum[:shard],
        pieces[4],
        pieces[5],
        ffn_up,
        pieces[7],
        ffn_down,
        pieces[6],
    )


def solution(mesh):
    line = mesh.shape["seq"] // 2
    mesh = jax.sharding.Mesh(
        mesh.devices.reshape(mesh.shape["obj"], line, 2), ("obj", "ring", "core")
    )
    rows, flat, lanes = P(BOTH, None), P(BOTH), P(None, BOTH)
    sequence = P("obj", SEQ, None)
    in_specs = (
        sequence,
        P("obj", None),
        sequence,
        P("obj"),
        P("obj", SEQ),
        sequence,
        lanes,
        rows,
        rows,
        flat,
        flat,
        rows,
        lanes,
        rows,
        rows,
        rows,
        flat,
        flat,
        rows,
        flat,
        rows,
        flat,
    )
    out_specs = (
        sequence,
        sequence,
        sequence,
        lanes,
        rows,
        rows,
        flat,
        flat,
        rows,
        lanes,
        rows,
        rows,
        rows,
        flat,
        flat,
        rows,
        flat,
        rows,
        flat,
    )
    return jax.shard_map(
        partial(on_device, mesh),
        mesh=mesh,
        in_specs=in_specs,
        out_specs=out_specs,
        check_vma=False,
    )
```

```python
from functools import partial

import jax
import jax.numpy as jnp
from jax import lax
from jax.experimental import pallas as pl
from jax.experimental.pallas import tpu as pltpu
from jax.sharding import PartitionSpec as P

HEAD_DIM = 64
PAIR = 2 * HEAD_DIM
VIEWS = 4
VIEW_PATCHES = 1024
BOTH = ("obj", "ring", "core")
SEQ = ("ring", "core")

epsilon = 1e-05
f32 = jnp.float32
bf16 = jnp.bfloat16
NN = (((1,), (0,)), ((), ()))
NT = (((1,), (1,)), ((), ()))
TN = (((0,), (0,)), ((), ()))


def dot(left, right, dims=NN):
    return lax.dot_general(left, right, dims, preferred_element_type=f32)


def params(megabytes=56):
    return pltpu.CompilerParams(vmem_limit_bytes=megabytes * 2**20)


def norm_parts(values):
    center = values - jnp.mean(values, -1, keepdims=True)
    spread = jnp.mean(center * center, -1, keepdims=True)
    scale = lax.rsqrt(spread + epsilon)
    return center * scale, scale


def norm_back(unit, scale, grad):
    return scale * (
        grad - jnp.mean(grad, -1, keepdims=True) - unit * jnp.mean(grad * unit, -1, keepdims=True)
    )


def attend_kernel(masked, *refs):
    q_ref, kv_ref = refs[:2]
    bias = refs[2] if masked else None
    o_ref, lse_ref = refs[-2:]
    query = q_ref[...]
    keys, values = kv_ref[:, :PAIR], kv_ref[:, PAIR:]
    low = lax.broadcasted_iota(jnp.int32, query.shape, 1) < HEAD_DIM
    outs, lses = [], []
    for head in range(2):
        mine = low if head == 0 else ~low
        score = dot(jnp.where(mine, query, jnp.zeros_like(query)), keys, NT)
        if masked:
            score = score + bias[...]
        top = jnp.max(score, 1, keepdims=True)
        lifted = jnp.exp(score - top)
        total = jnp.sum(lifted, 1, keepdims=True)
        outs.append(dot(lifted.astype(bf16), values) * (1.0 / total))
        lses.append(top + jnp.log(total))
    o_ref[...] = jnp.where(low, outs[0], outs[1]).astype(bf16)
    lse_ref[...] = jnp.where(low, lses[0], lses[1])[None]


def attend(query, kv, bias):
    rows, width = query.shape
    slots, pairs = kv.shape[0], width // PAIR
    tile = min(rows, 384)
    row = pl.BlockSpec((tile, PAIR), lambda i, r: (r, i))
    masked = bias is not None
    return pl.pallas_call(
        partial(attend_kernel, masked),
        grid=(pairs, rows // tile),
        in_specs=[row, pl.BlockSpec((slots, 2 * PAIR), lambda i, r: (0, i))]
        + [pl.BlockSpec((1, slots), lambda i, r: (0, 0))] * masked,
        out_specs=[row, pl.BlockSpec((1, tile, PAIR), lambda i, r: (i, r, 0))],
        out_shape=[
            jax.ShapeDtypeStruct((rows, width), bf16),
            jax.ShapeDtypeStruct((pairs, rows, PAIR), f32),
        ],
        compiler_params=params(),
        name="attend",
        cost_estimate=pl.CostEstimate(
            flops=16 * rows * slots * width,
            bytes_accessed=4 * width * (rows + slots),
            transcendentals=2 * pairs * rows * slots,
        ),
    )(query, kv, *([bias] if masked else []))


def attend_back_kernel(masked, *refs):
    q_ref, kv_ref, o_ref, do_ref, lse_ref = refs[:5]
    bias = refs[5] if masked else None
    dq_ref, dkv_ref, dk_s, dv_s = refs[-4:]
    query, grad = q_ref[...], do_ref[...]
    keys, values = kv_ref[:, :PAIR], kv_ref[:, PAIR:]
    low = lax.broadcasted_iota(jnp.int32, query.shape, 1) < HEAD_DIM
    lse = lse_ref[0]
    product = o_ref[...].astype(f32) * grad.astype(f32)
    dk = dv = 0.0
    dqs = []
    for head in range(2):
        mine = low if head == 0 else ~low
        head_query = jnp.where(mine, query, jnp.zeros_like(query))
        head_grad = jnp.where(mine, grad, jnp.zeros_like(grad))
        score = dot(head_query, keys, NT)
        if masked:
            score = score + bias[...]
        probs = jnp.exp(score - lse[:, HEAD_DIM * head : HEAD_DIM * head + 1])
        delta = jnp.sum(jnp.where(mine, product, 0.0), 1, keepdims=True)
        score_grad = (probs * (dot(head_grad, values, NT) - delta)).astype(bf16)
        dk = dk + dot(jnp.transpose(head_query), score_grad)
        dv = dv + dot(jnp.transpose(head_grad), probs.astype(bf16))
        dqs.append(dot(score_grad, keys))
    dq_ref[...] = (jnp.where(low, dqs[0], dqs[1]) * HEAD_DIM**-0.5).astype(bf16)
    step = pl.program_id(1)

    @pl.when(step == 0)
    def _():
        dk_s[...] = dk
        dv_s[...] = dv

    @pl.when(step > 0)
    def _():
        dk_s[...] += dk
        dv_s[...] += dv

    @pl.when(step == pl.num_programs(1) - 1)
    def _():
        dkv_ref[:, :PAIR] = jnp.transpose(dk_s[...]).astype(bf16)
        dkv_ref[:, PAIR:] = jnp.transpose(dv_s[...]).astype(bf16)


def attend_back(query, kv, out, grad, lse, bias):
    rows, width = query.shape
    slots, pairs = kv.shape[0], width // PAIR
    tile = min(rows, 384)
    row = pl.BlockSpec((tile, PAIR), lambda i, r: (r, i))
    slot = pl.BlockSpec((slots, 2 * PAIR), lambda i, r: (0, i))
    masked = bias is not None
    return pl.pallas_call(
        partial(attend_back_kernel, masked),
        grid=(pairs, rows // tile),
        in_specs=[row, slot, row, row, pl.BlockSpec((1, tile, PAIR), lambda i, r: (i, r, 0))]
        + [pl.BlockSpec((1, slots), lambda i, r: (0, 0))] * masked,
        out_specs=[row, slot],
        out_shape=[
            jax.ShapeDtypeStruct((rows, width), bf16),
            jax.ShapeDtypeStruct((slots, 2 * width), bf16),
        ],
        scratch_shapes=[pltpu.VMEM((PAIR, slots), f32)] * 2,
        compiler_params=params(),
        name="attend_back",
        cost_estimate=pl.CostEstimate(
            flops=40 * rows * slots * width,
            bytes_accessed=8 * width * (rows + slots),
            transcendentals=2 * pairs * rows * slots,
        ),
    )(query, kv, out, grad, lse, *([bias] if masked else []))


def block_kernel(core_ref, third_ref, cot_ref, gain_ref, shift_ref, dbias_ref, ubias_ref, up_ref, down_ref,
                 result_ref, tgrad_ref, keep_ref, send_ref, vec_ref, ubgrad_ref,
                 unit_s, final_s, final_t, out_s, fgrad_s, scale_s, wide_s, tall_s, sems):
    step = pl.program_id(0)
    last = pl.num_programs(0) - 1
    slot = lax.rem(step, 2)
    core = core_ref[0]
    _, _, half, shard, tile = wide_s.shape
    _, _, few, tall, width = tall_s.shape
    per = width // tile

    def copies(at, place):
        row = pl.multiple_of((at // per) * shard, shard)
        lane = pl.multiple_of(lax.rem(at, per) * tile, tile)
        found = []
        for which, ref in enumerate((keep_ref, send_ref)):
            found += [
                pltpu.make_async_copy(
                    wide_s.at[place, which],
                    ref.at[:, pl.ds(row, shard), pl.ds(lane, tile)],
                    sems.at[which, place],
                ),
                pltpu.make_async_copy(
                    tall_s.at[place, which],
                    ref.at[pl.ds(at * few, few), pl.ds(tall, tall), :],
                    sems.at[2 + which, place],
                ),
            ]
        return found

    @pl.when(step == 0)
    def _():
        unit, scale = norm_parts(third_ref[...])
        unit_s[...] = unit
        scale_s[...] = scale
        final = (unit * gain_ref[...] + shift_ref[...]).astype(bf16)
        final_s[...] = final
        final_t[...] = jnp.transpose(final)
        out_s[...] = jnp.zeros_like(out_s)
        fgrad_s[...] = jnp.zeros_like(fgrad_s)

    @pl.when(step >= 2)
    def _():
        for copy in copies(step - 2, slot):
            copy.wait()

    cot = cot_ref[...]
    up = up_ref[...].reshape(-1, up_ref.shape[-1])
    down = down_ref[...].reshape(-1, down_ref.shape[-1])
    upper = dot(final_s[...], up) + ubias_ref[...]
    cdf = 0.5 * (1.0 + lax.erf(upper * (0.5**0.5)))
    active = (upper * cdf).astype(bf16)
    slope = cdf + upper * (jnp.exp(-0.5 * upper * upper) * 0.3989422804014327)
    ugrad = (slope * dot(cot, down, NT)).astype(bf16)
    out_s[...] += dot(active, down)
    fgrad_s[...] += dot(ugrad, up, NT)
    ubgrad_ref[...] = jnp.sum(ugrad.astype(f32), 0, keepdims=True)
    wide = dot(final_t[...], ugrad).astype(bf16).reshape(half, 2, shard, tile)
    wide_s[slot, core] = wide[:, 0]
    wide_s[slot, 1 - core] = wide[:, 1]
    slim = dot(jnp.transpose(active), cot).astype(bf16).reshape(few, 2, tall, width)
    tall_s[slot, core] = slim[:, 0]
    tall_s[slot, 1 - core] = slim[:, 1]
    for copy in copies(step, slot):
        copy.start()

    @pl.when(step == last)
    def _():
        result_ref[...] = (third_ref[...] + (out_s[...] + dbias_ref[...])).astype(bf16)
        unit, fgrad, cotf = unit_s[...], fgrad_s[...], cot.astype(f32)
        tgrad_ref[...] = cotf + norm_back(unit, scale_s[...], fgrad * gain_ref[...])
        vec_ref[...] = jnp.zeros_like(vec_ref)
        vec_ref[0:1, :] = jnp.sum(fgrad * unit, 0, keepdims=True)
        vec_ref[1:2, :] = jnp.sum(fgrad, 0, keepdims=True)
        vec_ref[2:3, :] = jnp.sum(cotf, 0, keepdims=True)
        for copy in copies(step - 1, 1 - slot) + copies(step, slot):
            copy.wait()


def feed_forward(core, third, cot, gain, shift, down_bias, up_bias, packed, shard):
    rows, width = third.shape
    parts = packed.shape[0]
    hidden = up_bias.shape[1]
    tile = min(hidden, width)
    per = width // tile
    tall = hidden // parts
    spread = tile // tall
    steps = hidden // tile
    whole = lambda shape: pl.BlockSpec(shape, lambda j, c: (0,) * len(shape))
    return pl.pallas_call(
        block_kernel,
        grid_spec=pltpu.PrefetchScalarGridSpec(
            num_scalar_prefetch=1,
            grid=(steps,),
            in_specs=[
                whole((rows, width)),
                whole((rows, width)),
                whole((1, width)),
                whole((1, width)),
                whole((1, width)),
                pl.BlockSpec((1, tile), lambda j, c: (0, j)),
                pl.BlockSpec((parts, shard, tile), lambda j, c: (0, j // per, j % per)),
                pl.BlockSpec((spread, tall, width), lambda j, c: (j, 1, 0)),
            ],
            out_specs=[
                whole((rows, width)),
                whole((rows, width)),
                pl.BlockSpec(memory_space=pl.ANY),
                pl.BlockSpec(memory_space=pl.ANY),
                whole((8, width)),
                pl.BlockSpec((1, tile), lambda j, c: (0, j)),
            ],
            scratch_shapes=[
                pltpu.VMEM((rows, width), f32),
                pltpu.VMEM((rows, width), bf16),
                pltpu.VMEM((width, rows), bf16),
                pltpu.VMEM((rows, width), f32),
                pltpu.VMEM((rows, width), f32),
                pltpu.VMEM((rows, 1), f32),
                pltpu.VMEM((2, 2, parts // 2, shard, tile), bf16),
                pltpu.VMEM((2, 2, spread // 2, tall, width), bf16),
                pltpu.SemaphoreType.DMA((4, 2)),
            ],
        ),
        out_shape=[
            jax.ShapeDtypeStruct((rows, width), bf16),
            jax.ShapeDtypeStruct((rows, width), f32),
            jax.ShapeDtypeStruct((parts // 2, 2 * tall, width), bf16),
            jax.ShapeDtypeStruct((parts // 2, 2 * tall, width), bf16),
            jax.ShapeDtypeStruct((8, width), f32),
            jax.ShapeDtypeStruct((1, hidden), f32),
        ],
        compiler_params=params(),
        name="feed_forward",
        cost_estimate=pl.CostEstimate(flops=1, bytes_accessed=1, transcendentals=0),
    )(core, third, cot, gain, shift, down_bias, up_bias, packed, packed)


def grads_kernel(jobs, core_ref, *refs):
    ins, (keep_ref, send_ref) = refs[:-2], refs[-2:]
    step = pl.program_id(0)
    half, room, width = keep_ref.shape

    def store(block, rows):
        block = block.astype(bf16).reshape(half, 2, rows, width)
        keep_ref[:, :rows] = block[:, 0]
        send_ref[:, :rows] = block[:, 1]

    def swapped(block, rows):
        block = block.astype(bf16).reshape(half, 2, rows, width)
        keep_ref[:, :rows] = block[:, 1]
        send_ref[:, :rows] = block[:, 0]

    for at, (left, right, column) in enumerate(jobs):

        @pl.when(step == at)
        def _():
            rows = ins[left].shape[1] // (2 * half)
            if rows < room:
                keep_ref[...] = jnp.zeros_like(keep_ref)
                send_ref[...] = jnp.zeros_like(send_ref)
            block = dot(ins[left][...], ins[right][:, column * width : (column + 1) * width], TN)

            @pl.when(core_ref[0] == 0)
            def _():
                store(block, rows)

            @pl.when(core_ref[0] == 1)
            def _():
                swapped(block, rows)


def weight_grads(core, arrays, jobs, parts, shard, width):
    count = len(jobs)
    whole = lambda array: pl.BlockSpec(array.shape, lambda j, c: (0, 0))
    out = pl.BlockSpec((parts // 2, shard, width), lambda j, c: (0, j, 0))
    flops = sum(2 * arrays[i].shape[0] * arrays[i].shape[1] * width for i, _, _ in jobs)
    return pl.pallas_call(
        partial(grads_kernel, jobs),
        grid_spec=pltpu.PrefetchScalarGridSpec(
            num_scalar_prefetch=1,
            grid=(count,),
            in_specs=[whole(array) for array in arrays],
            out_specs=[out, out],
        ),
        out_shape=[jax.ShapeDtypeStruct((parts // 2, count * shard, width), bf16)] * 2,
        compiler_params=params(),
        name="weight_grads",
        cost_estimate=pl.CostEstimate(flops=1, bytes_accessed=1, transcendentals=0),
    )(core, *arrays)


class Grid:
    def __init__(self, mesh):
        self.obj, self.seq = mesh.shape["obj"], mesh.shape["ring"] * 2
        self.all = self.obj * self.seq
        self.place = lax.axis_index("ring") * 2 + lax.axis_index("core")
        self.me = lax.axis_index("obj") * self.seq + self.place
        self.group = [m for m in (1 << k for k in range(20)) if m < self.seq // 2]
        self.far = self.seq // 2

    def swap(self, value, mask):
        return lax.ppermute(value, BOTH, [(i, i ^ mask) for i in range(self.all)])

    def bit(self, mask):
        return (self.me // mask) % 2

    def gather_group(self, value):
        found = {0: value}
        for mask in self.group[1:][::-1] + self.group[:1]:
            found.update({d ^ mask: self.swap(v, mask) for d, v in list(found.items())})
        return [found[d] for d in range(self.seq // 2)]

    def in_order(self, terms):
        spot = self.place % len(terms)
        stacked = jnp.stack(terms)
        return [
            lax.dynamic_index_in_dim(stacked, spot ^ j, 0, keepdims=False) for j in range(len(terms))
        ]

    def exchange(self, blocks):
        spot = self.place % blocks.shape[0]
        found = []
        for d in range(blocks.shape[0]):
            block = lax.dynamic_index_in_dim(blocks, spot ^ d, 0, keepdims=False)
            found.append(self.swap(block, d) if d else block)
        return found

    def gather_self(self, blocks):
        found = yield self.exchange(blocks)
        found = jnp.stack(self.in_order(found))
        for mask in [m for m in (1 << k for k in range(20)) if self.far <= m < self.all]:
            moved = yield self.swap(found, mask)
            found = jnp.where(
                self.bit(mask) == 0, jnp.concatenate([found, moved]), jnp.concatenate([moved, found])
            )
        yield found

    def scatter_self(self, grad):
        terms = [grad]
        for mask in [m for m in (1 << k for k in range(20)) if self.far <= m < self.all][::-1]:
            terms = [t.reshape(2, t.shape[0] // 2, *t.shape[1:]) for t in terms]
            pick = lambda t, which: lax.dynamic_index_in_dim(t, which, 0, keepdims=False)
            moved = yield self.swap(add([pick(t, 1 - self.bit(mask)) for t in terms]), mask)
            terms = [pick(t, self.bit(mask)) for t in terms] + [moved]
        found = yield self.exchange(add(terms))
        yield jnp.stack(self.in_order(found), 1)

    def scatter(self, keep, send, whole):
        moved = yield self.swap(send, 1)
        total = add([keep, moved]).reshape(self.obj, self.seq // 2, *keep.shape[1:])
        total = yield total
        total = yield lax.psum_scatter(total, "obj", scatter_dimension=0, tiled=False)
        if whole:
            moved = yield lax.all_to_all(total, "ring", 0, 0, tiled=True)
            yield jnp.sum(moved.astype(f32), 0)
            return
        terms = [total]
        for mask in self.group[1:] + [self.far]:
            terms = [t.reshape(t.shape[0] // 2, 2, *t.shape[1:]) for t in terms]
            pick = lambda t, which: lax.dynamic_index_in_dim(t, which, 1, keepdims=False)
            moved = self.swap(add([pick(t, 1 - self.bit(mask)) for t in terms]), mask)
            if 4 * mask >= self.seq:
                moved = yield moved
            terms = [pick(t, self.bit(mask)) for t in terms] + [moved]
        yield sum(t[0].astype(f32) for t in terms)

    def exchange_core(self, terms):
        return [self.swap(t, 1) for t in terms[1::2]]

    def exchange_line(self, terms, moved):
        pairs = [add([t, m]) for t, m in zip(terms[::2], moved)]
        step = len(pairs) // 2
        while step > 1:
            pairs = [add([pairs[k], self.swap(pairs[k + step], 2 * step)]) for k in range(step)]
            step //= 2
        return pairs[0], self.swap(pairs[1], 2)


together = lax.optimization_barrier


def add(terms):
    if len(terms) == 1:
        return terms[0]
    return sum(t.astype(f32) for t in terms).astype(bf16)


def split_pairs(matrix):
    rows, width = matrix.shape
    return matrix.reshape(rows, 2, width // (2 * PAIR), PAIR).transpose(0, 2, 1, 3).reshape(rows, width)


def join_pairs(matrix):
    rows, width = matrix.shape
    return matrix.reshape(rows, width // (2 * PAIR), 2, PAIR).transpose(0, 2, 1, 3).reshape(rows, width)


def stack_columns(matrix, width):
    rows = matrix.shape[0]
    return matrix.reshape(rows, -1, width).transpose(1, 0, 2).reshape(-1, width)


def unstack_columns(matrix, rows):
    width = matrix.shape[1]
    return matrix.reshape(-1, rows, width).transpose(1, 0, 2).reshape(rows, -1)


def pad_rows(matrix, rows):
    return jnp.pad(matrix, ((0, rows - matrix.shape[0]), (0, 0)))


def on_device(
    mesh,
    tokens,
    camera,
    patches,
    patch_count,
    patch_index,
    cotangent,
    camera_weight,
    self_weight,
    self_output,
    mid_gain,
    mid_bias,
    patch_weight,
    view_table,
    cross_query,
    cross_memory,
    cross_output,
    last_gain,
    last_bias,
    up_weight,
    up_bias,
    down_weight,
    down_bias,
):
    grid = Grid(mesh)
    parts = grid.all
    width = self_output.shape[1]
    low = lambda v: v.astype(bf16)
    factor = HEAD_DIM**-0.5
    core = grid.bit(1)
    half = grid.bit(grid.far)

    def compact(value):
        mine = lax.dynamic_index_in_dim(value, half, 0, keepdims=False)
        other = lax.dynamic_index_in_dim(value, 1 - half, 0, keepdims=False)
        return jnp.concatenate([mine, grid.swap(other, grid.far)], 0)

    def spread(mine, other):
        mine = mine[: other.shape[0]]
        return jnp.where(half == 0, jnp.stack([mine, other]), jnp.stack([other, mine]))

    def chunks(terms):
        return jnp.split(terms, grid.seq // 2, 0)

    shard = self_output.shape[0]
    self_mixed = jnp.concatenate(
        [low(self_weight[:, :width]), split_pairs(low(self_weight[:, width:]))], 1
    )
    small = jnp.concatenate(
        [
            low(camera_weight).reshape(-1),
            low(view_table).reshape(-1),
            low(mid_gain),
            low(mid_bias),
            low(last_gain),
            low(last_bias),
            low(down_bias),
            low(up_bias),
        ]
    )
    small_sizes = [
        camera_weight.size,
        view_table.size,
        shard,
        shard,
        shard,
        shard,
        shard,
        up_bias.size,
    ]
    patch_rows = patch_weight.shape[0]
    group = grid.seq // 2
    lot = 3 * width // group
    few = width // group
    small_count = -(-small.size // lot)
    small_rows = jnp.pad(small, (0, small_count * lot - small.size)).reshape(-1, lot)
    blocks = jnp.concatenate(
        [
            self_mixed[:, :width].reshape(shard, group, few),
            self_mixed[:, width:].reshape(shard, group, 2 * few),
        ],
        2,
    ).transpose(1, 0, 2)
    blocks = jnp.concatenate(
        [blocks, jnp.broadcast_to(pad_rows(small_rows, -(-small_count // 8) * 8), (group, -(-small_count // 8) * 8, lot))], 1
    )
    patch_room = -(-patch_rows // shard) * shard
    first = jnp.concatenate(
        [
            stack_columns(low(up_weight), width),
            low(down_weight),
            low(self_output),
            low(cross_query),
            low(cross_output),
            stack_columns(split_pairs(low(cross_memory)), width),
            pad_rows(low(patch_weight), patch_room),
        ],
        0,
    )
    own_gather = grid.gather_self(blocks)
    blocks = next(own_gather)
    tokens_all = jnp.concatenate(grid.gather_group(compact(tokens)), 0)
    first = lax.all_gather(first, BOTH, axis=0, tiled=False)
    while isinstance(blocks, list) or blocks.shape[0] < parts:
        blocks = own_gather.send(blocks)
        if isinstance(blocks, list) or blocks.shape[0] == parts // 2:
            break
    blocks, tokens_all, patches, patch_index = together((blocks, tokens_all, patches, patch_index))
    feats_all = jnp.concatenate(grid.gather_group(compact(patches)), 0)
    views_all = jnp.concatenate(grid.gather_group(compact(patch_index)), 0) // VIEW_PATCHES
    blocks = own_gather.send(blocks)
    self_own = blocks[:, :shard].reshape(parts * shard, lot)
    tiny = blocks[:, shard : shard + small_count].reshape(parts, -1)
    pieces = []
    at = 0
    for size in small_sizes:
        pieces.append(tiny[:, at : at + size].astype(f32))
        at += size
    full_camera = pieces[0].reshape(parts, 16, -1).transpose(1, 0, 2).reshape(16, -1)
    full_view = pieces[1].reshape(parts, VIEWS, -1).transpose(1, 0, 2).reshape(VIEWS, -1)
    g_mid, b_mid, g_last, b_last, b_down, b_up = (p.reshape(1, -1) for p in pieces[2:])

    own = tokens_all.shape[0] // (grid.seq // 2)
    slots_own = feats_all.shape[0] // (grid.seq // 2)
    x_all = tokens_all.astype(f32)
    x = x_all[:own]
    camera_mine = lax.dynamic_index_in_dim(camera, half, 0, keepdims=False)
    live = lax.dynamic_index_in_dim(patch_count, half, 0, keepdims=False)
    modulation = jnp.sum(camera_mine[:, None] * full_camera, 0)
    scale1, shift1 = 1.0 + modulation[None, :width], modulation[None, width:]
    hidden_all = low(norm_parts(x_all)[0] * scale1 + shift1)
    triple = low(dot(hidden_all, self_own))
    query = low(triple[:, :few].astype(f32) * factor)
    kv = triple[:, few:]
    query, kv, feats_all, views_all, cotangent = together((query, kv, feats_all, views_all, cotangent))
    attended_own, lse1 = attend(query, kv, None)
    attended_own, first = together((attended_own, first))
    attended = grid.exchange(jnp.stack(grid.in_order(chunks(attended_own))))

    packed = first

    def square(start, rows=shard):
        start += 2 * down_weight.shape[0]
        return first[:, start : start + rows].reshape(parts * rows, width)

    full_out = square(0)
    full_cq = square(shard)
    full_co = square(2 * shard)
    full_mem = jnp.concatenate([square(3 * shard), square(4 * shard)], 1)
    full_patch = square(5 * shard, patch_rows)
    hot_all = (views_all[:, None] == jnp.arange(VIEWS)[None, :]).astype(f32)
    view_part = sum(hot_all[:, v : v + 1] * full_view[v : v + 1] for v in range(VIEWS))
    embedded_all = low(dot(feats_all, full_patch) + view_part)
    mem = low(dot(embedded_all, full_mem))
    attended, mem = together((attended, mem))
    attended = jnp.concatenate(grid.in_order(attended), 1)
    place = grid.place
    chunk = patches.shape[1]
    lane = jnp.arange(chunk)
    slots = jnp.concatenate(
        [
            chunk * (place ^ d ^ far) + lane
            for d in range(grid.seq // 2)
            for far in (0, grid.far)
        ]
    )
    bias = jnp.where(slots < live, 0.0, -1e30).astype(f32).reshape(1, -1)

    second = x + dot(attended, full_out)
    unit2, rstd2 = norm_parts(second)
    normed = low(unit2 * g_mid + b_mid)
    asked = low(low(dot(normed, full_cq)).astype(f32) * factor)
    asked, cotangent = together((asked, cotangent))
    cot = compact(cotangent)
    crossed, lse2 = attend(asked, mem, bias)
    third = second + dot(crossed, full_co)
    third, cot = together((third, cot))
    core_now = core.reshape(1).astype(jnp.int32)
    result, third_grad, ffn_keep, ffn_send, last_vectors, up_bias_grad = feed_forward(
        core_now, third, cot, g_last, b_last, b_down, b_up, packed, shard
    )
    tall = down_weight.shape[0]

    ffn = grid.scatter(ffn_keep, ffn_send, True)
    ffn_moved = next(ffn)
    half_rows = result.shape[0] // 2
    third_low = low(third_grad)
    crossed_grad = low(dot(third_low, full_co, NT))
    ffn_moved, crossed_grad = together((ffn_moved, crossed_grad))
    ffn_moved = ffn.send(ffn_moved)
    ffn_moved, crossed_grad = together((ffn_moved, crossed_grad))

    ffn_moved = ffn.send(ffn_moved)
    result_moved = grid.swap(result[half_rows:], grid.far)
    asked_grad, mem_terms = attend_back(asked, mem, crossed, crossed_grad, lse2, bias)
    asked_grad, mem_terms, result_moved = together((asked_grad, mem_terms, result_moved))
    normed_grad = dot(asked_grad, full_cq, NT)
    second_grad = third_grad + norm_back(unit2, rstd2, normed_grad * g_mid)
    second_low = low(second_grad)
    attended_grad = low(dot(second_low, full_out, NT))
    embedded_grad = low(dot(mem_terms, full_mem, NT))
    arrays = [
        crossed,
        third_low,
        normed,
        asked_grad,
        attended,
        second_low,
        embedded_all,
        mem_terms,
        feats_all,
        embedded_grad,
    ]
    jobs = ((0, 1, 0), (2, 3, 0), (4, 5, 0), (6, 7, 0), (6, 7, 1), (8, 9, 0))
    attended_grad, arrays = together((attended_grad, arrays))
    grad_moved = []
    for d in range(group):
        at = ((grid.place % group) ^ d) * few
        part = lax.dynamic_slice_in_dim(attended_grad, at, few, 1)
        grad_moved.append(grid.swap(part, d) if d else part)
    keep, send = weight_grads(core_now, arrays, jobs, parts, shard, width)
    grad_moved, keep, send = together((grad_moved, keep, send))
    rest = grid.scatter(keep, send, False)
    moved = next(rest)
    patch_terms = chunks(low(dot(embedded_grad, full_patch, NT)))
    grad_own = jnp.concatenate(grad_moved, 0)
    grad_own, patch_terms, moved = together((grad_own, patch_terms, moved))
    moved = rest.send(moved)
    patch_moved = grid.exchange_core(patch_terms)
    grad_own, patch_moved, moved, ffn_moved = together((grad_own, patch_moved, moved, ffn_moved))

    moved = rest.send(moved)
    ffn_moved = ffn.send(ffn_moved)
    patch_mine, patch_moved = grid.exchange_line(patch_terms, patch_moved)
    query_grad, pair_grad = attend_back(query, kv, attended_own, grad_own, lse1, None)
    patch_moved, query_grad, pair_grad = together((patch_moved, query_grad, pair_grad))

    triple_grad = jnp.concatenate([query_grad, pair_grad], 1)
    hidden_terms = chunks(low(dot(triple_grad, self_own, NT)))
    hidden_terms, triple_grad = together((hidden_terms, triple_grad))
    hidden_moved = grid.exchange_core(hidden_terms)
    self_grad = low(dot(hidden_all, triple_grad, TN))
    self_grad, hidden_moved = together((self_grad, hidden_moved))

    own_scatter = grid.scatter_self(self_grad.reshape(parts, shard, lot))
    own_moved = next(own_scatter)
    hidden_mine, hidden_moved = grid.exchange_line(hidden_terms, hidden_moved)
    patch_low = low(patch_mine.astype(f32) + patch_moved.astype(f32))
    patch_half = patch_low.shape[0] // 2
    patch_moved = grid.swap(patch_low[patch_half:], grid.far)
    result = spread(result, result_moved)
    view_grad = jnp.stack(
        [jnp.sum(hot_all[:, v : v + 1] * embedded_grad.astype(f32), 0) for v in range(VIEWS)]
    )
    mid_vectors = jnp.stack([jnp.sum(normed_grad * unit2, 0), jnp.sum(normed_grad, 0)])
    own_moved, hidden_moved, patch_moved, result, view_grad, mid_vectors, last_vectors, up_bias_grad = together(
        (own_moved, hidden_moved, patch_moved, result, view_grad, mid_vectors, last_vectors, up_bias_grad)
    )

    unit1, rstd1 = norm_parts(together(tokens_all[:own]).astype(f32))
    hidden_grad = hidden_mine.astype(f32) + hidden_moved.astype(f32)
    token_grad = low(second_grad + norm_back(unit1, rstd1, hidden_grad * scale1))
    token_grad, hidden_grad, own_moved, moved, ffn_moved = together(
        (token_grad, hidden_grad, own_moved, moved, ffn_moved)
    )
    token_moved = grid.swap(token_grad[half_rows:], grid.far)
    moved = rest.send(moved)
    own_moved = own_scatter.send(own_moved)
    modulation_grad = jnp.concatenate(
        [jnp.sum(hidden_grad * unit1, 0), jnp.sum(hidden_grad, 0)]
    )
    camera_grad = camera_mine[:, None] * modulation_grad[None]
    vectors = jnp.concatenate(
        [
            view_grad,
            mid_vectors,
            last_vectors[0:3],
        ],
        0,
    )
    small_grad = jnp.concatenate(
        [
            low(camera_grad).reshape(16, parts, -1).transpose(1, 0, 2).reshape(parts, -1),
            low(vectors).reshape(VIEWS + 5, parts, -1).transpose(1, 0, 2).reshape(parts, -1),
            low(up_bias_grad).reshape(parts, -1),
        ],
        1,
    )
    small_grad = jnp.pad(small_grad, ((0, 0), (0, small_count * lot - small_grad.shape[1])))
    small_grad, own_moved, token_moved, moved = together((small_grad, own_moved, token_moved, moved))
    while not isinstance(own_moved, list):
        own_moved = own_scatter.send(own_moved)
        if own_moved.shape[0] == group:
            break
    moved = rest.send(moved)
    small_grad = lax.all_to_all(small_grad.reshape(parts, small_count, lot), BOTH, 0, 0, tiled=True)
    token_grad = spread(token_grad, token_moved)
    ffn_grad = ffn.send(ffn_moved)
    ffn_up, ffn_down = unstack_columns(ffn_grad[:tall], shard), ffn_grad[tall:]
    patch_grad = spread(patch_low, patch_moved)
    own_moved = own_scatter.send(own_moved)
    own_moved, moved, token_grad, small_grad, patch_grad, ffn_up, ffn_down = together(
        (own_moved, moved, token_grad, small_grad, patch_grad, ffn_up, ffn_down)
    )
    tiny = jnp.sum(small_grad.astype(f32), 0).reshape(-1)
    rest_sum = rest.send(moved)
    self_sum = own_scatter.send(own_moved).astype(f32)
    pieces = []
    at = 0
    for size in small_sizes:
        pieces.append(tiny[at : at + size])
        at += size
    self_sum = jnp.concatenate(
        [
            self_sum[:, :, :few].reshape(shard, width),
            join_pairs(self_sum[:, :, few:].reshape(shard, 2 * width)),
        ],
        1,
    )
    return (
        result,
        token_grad,
        patch_grad,
        pieces[0].reshape(camera_weight.shape),
        self_sum,
        rest_sum[2 * shard : 3 * shard],
        pieces[2],
        pieces[3],
        rest_sum[5 * shard : 5 * shard + patch_rows],
        pieces[1].reshape(view_table.shape),
        rest_sum[shard : 2 * shard],
        join_pairs(unstack_columns(rest_sum[3 * shard : 5 * shard], shard)),
        rest_sum[:shard],
        pieces[4],
        pieces[5],
        ffn_up,
        pieces[7],
        ffn_down,
        pieces[6],
    )


def solution(mesh):
    line = mesh.shape["seq"] // 2
    mesh = jax.sharding.Mesh(
        mesh.devices.reshape(mesh.shape["obj"], line, 2), ("obj", "ring", "core")
    )
    rows, flat, lanes = P(BOTH, None), P(BOTH), P(None, BOTH)
    sequence = P("obj", SEQ, None)
    in_specs = (
        sequence,
        P("obj", None),
        sequence,
        P("obj"),
        P("obj", SEQ),
        sequence,
        lanes,
        rows,
        rows,
        flat,
        flat,
        rows,
        lanes,
        rows,
        rows,
        rows,
        flat,
        flat,
        rows,
        flat,
        rows,
        flat,
    )
    out_specs = (
        sequence,
        sequence,
        sequence,
        lanes,
        rows,
        rows,
        flat,
        flat,
        rows,
        lanes,
        rows,
        rows,
        rows,
        flat,
        flat,
        rows,
        flat,
        rows,
        flat,
    )
    return jax.shard_map(
        partial(on_device, mesh),
        mesh=mesh,
        in_specs=in_specs,
        out_specs=out_specs,
        check_vma=False,
    )
```
